32 devices in a mesh: seq: 4 (over y, core), fsdp: 8 (over z, x).
Axes of the slice: x: 2, y: 2, z: 4, core: 2. Of those that a mesh axis runs over, the one named last changes fastest.
Arguments:
- inputs: bfloat16 [8, 2048, 768], P('fsdp', 'seq'), may hold values from -6 to 6
- norm_one: bfloat16 [768], P('fsdp'), may hold values from 0.5 to 1.5
- qkv_weight: bfloat16 [768, 2304], P('fsdp'), may hold values from -0.21875 to 0.21875
- attn_out_weight: bfloat16 [768, 768], P('fsdp'), may hold values from -6 to 6
- norm_two: bfloat16 [768], P('fsdp'), may hold values from 0.5 to 1.5
- mlp_in_weight: bfloat16 [768, 2304], P('fsdp'), may hold values from -0.21875 to 0.21875
- mlp_out_weight: bfloat16 [1152, 768], P('fsdp'), may hold values from -0.1875 to 0.1875
- cotangent: bfloat16 [8, 2048, 768], P('fsdp', 'seq'), may hold values from -6 to 6
Outputs:
- output: bfloat16 [8, 2048, 768], P('fsdp', 'seq')
- input_grad: bfloat16 [8, 2048, 768], P('fsdp', 'seq')
- norm_one_grad: float32 [768], P('fsdp')
- qkv_grad: float32 [768, 2304], P('fsdp')
- attn_out_grad: float32 [768, 768], P('fsdp')
- norm_two_grad: float32 [768], P('fsdp')
- mlp_in_grad: float32 [768, 2304], P('fsdp')
- mlp_out_grad: float32 [1152, 768], P('fsdp')
The draws below stay inside these ranges and needn't reach their ends.
All inputs are finite; a program needn't handle non-finite values.
Results may differ from the reference program's by a relative error of at most 0.018.
Values may be sent and summed in bfloat16 or wider, within the bound.
No kernel may reach another device: no remote copies, remote signals or barrier semaphores. Data moves between devices by JAX's collectives and lax.ppermute only.
A program may use at most 128 MiB of HBM per device.

```python
import jax
import jax.numpy as jnp
from jax import lax

D = 768
HEADS = 12
HEAD = 64
FF = 1152
LEN = 2048
SEQUENCES = 8


def level_of(own_key, dims, cuts, least, largest):
    def one(axis_at, blocks):
        heights = jax.random.uniform(jax.random.fold_in(jax.random.fold_in(own_key, 6), axis_at), (blocks,), jnp.float32, least / len(cuts), largest / len(cuts))
        return jnp.repeat(jnp.exp(heights), dims[axis_at] // blocks).reshape((-1,) + (1,) * (len(dims) - axis_at - 1))

    loudness = one(*cuts[0])
    for cut in cuts[1:]:
        loudness = loudness * one(*cut)
    return loudness


def noise(own_key, shape, spread, bound, cuts=(), kind=jnp.bfloat16):
    loudness = level_of(own_key, shape, cuts, -0.22, 0.18) if cuts else 1.0
    array = jax.random.normal(own_key, shape, jnp.float32) * spread * loudness
    return jnp.minimum(jnp.maximum(array, -bound), bound).astype(kind)


def setup_inputs(seed: int = 0) -> dict:
    seeds = jax.random.split(jax.random.key(seed), 9)
    inputs = noise(seeds[0], (SEQUENCES, LEN, D), 1.0, 6.0, ((0, 8), (1, 4)))
    norm_one = jnp.clip(1.0 + 0.1 * jax.random.normal(seeds[1], (D,), jnp.float32), 0.5, 1.5).astype(jnp.bfloat16)
    qkv_weight = noise(seeds[2], (D, 3 * D), D ** -0.5, 0.21875, ((0, 8),))
    attn_out_weight = noise(seeds[3], (D, D), (max(1, 3 * D // LEN)) ** -0.5, 6.0, ((0, 8),))
    norm_two = jnp.clip(1.0 + 0.1 * jax.random.normal(seeds[4], (D,), jnp.float32), 0.5, 1.5).astype(jnp.bfloat16)
    mlp_in_weight = noise(seeds[5], (D, 2 * FF), D ** -0.5, 0.21875, ((0, 8),))
    mlp_out_weight = noise(seeds[6], (FF, D), FF ** -0.5, 0.1875, ((0, 8),))
    cotangent = noise(seeds[7], (SEQUENCES, LEN, D), 1.0, 6.0, ((0, 8), (1, 4)))
    return dict(inputs=inputs, norm_one=norm_one, qkv_weight=qkv_weight, attn_out_weight=attn_out_weight, norm_two=norm_two, mlp_in_weight=mlp_in_weight, mlp_out_weight=mlp_out_weight, cotangent=cotangent)


@jax.custom_vjp
def low(v):
    return lax.optimization_barrier(v.astype(jnp.bfloat16)).astype(jnp.float32)

@jax.custom_vjp
def low_back(v):
    return v

def low_keep(v):
    return (low(v), None)

def low_pass(kept, grad):
    return (grad,)

def back_keep(v):
    return (v, None)

def back_low(kept, grad):
    return (low(grad),)
low.defvjp(low_keep, low_pass)
low_back.defvjp(back_keep, back_low)
EPSILON = 1e-05
ROPE_BASE = 160000.0

def both_ways(value):
    return low_back(low(value))

def matmul(left, right):
    return jnp.dot(left, right, precision=lax.Precision.HIGHEST, preferred_element_type=jnp.float32)

def layer_norm(values, gain):
    centred = values - lax.optimization_barrier(jnp.mean(values, axis=1, keepdims=True))
    variance = lax.optimization_barrier(jnp.mean(centred * centred, axis=1, keepdims=True))
    return centred * lax.rsqrt(variance + EPSILON) * gain

def rope_tables(count, head_size):
    half_size = head_size // 2
    places = jnp.arange(count, dtype=jnp.float32)
    inverse = ROPE_BASE ** (-(jnp.arange(half_size, dtype=jnp.float32) * 2.0 / head_size))
    angles = places[:, None] * inverse[None, :]
    angles = jnp.concatenate([angles, angles], axis=1)
    return (jnp.cos(angles), jnp.sin(angles))

def rotate(values, cosine, sine):
    half_size = HEAD // 2
    shaped = values.reshape(values.shape[0], HEADS, HEAD)
    turned = jnp.concatenate([-shaped[..., half_size:], shaped[..., :half_size]], axis=-1)
    return shaped * cosine[:, None, :] + turned * sine[:, None, :]

def attend_head(triple):
    queries, keys, values = triple
    scores = low_back(matmul(queries, keys.T) * HEAD ** (-0.5))
    probs = jax.nn.softmax(scores, axis=-1)
    return matmul(low(probs), values)

def forward(inputs, norm_one, qkv_weight, attn_out_weight, norm_two, mlp_in_weight, mlp_out_weight):
    length = inputs.shape[0]
    cosine, sine = rope_tables(length, HEAD)
    normed_one = low(layer_norm(inputs, norm_one))
    qkv = low_back(matmul(normed_one, qkv_weight))
    queries = both_ways(rotate(qkv[:, :D], cosine, sine))
    keys = both_ways(rotate(qkv[:, D:2 * D], cosine, sine))
    values = both_ways(qkv[:, 2 * D:].reshape(length, HEADS, HEAD))
    heads_out = lax.map(jax.checkpoint(attend_head), (queries.transpose(1, 0, 2), keys.transpose(1, 0, 2), values.transpose(1, 0, 2)))
    context = both_ways(heads_out.transpose(1, 0, 2).reshape(length, D))
    attended = inputs + low_back(matmul(context, attn_out_weight))
    normed_two = low(layer_norm(attended, norm_two))
    gate_up = low_back(matmul(normed_two, mlp_in_weight))
    hidden = low(jax.nn.gelu(gate_up[:, :FF], approximate=False) * gate_up[:, FF:])
    return attended + matmul(hidden, mlp_out_weight)

def reference(inputs, norm_one, qkv_weight, attn_out_weight, norm_two, mlp_in_weight, mlp_out_weight, cotangent):
    weights = tuple((weight.astype(jnp.float32) for weight in (norm_one, qkv_weight, attn_out_weight, norm_two, mlp_in_weight, mlp_out_weight)))

    def one_sequence(carry, pair):
        seq_input, seq_cotangent = pair
        result, backward = jax.vjp(forward, seq_input.astype(jnp.float32), *weights)
        grads = backward(seq_cotangent.astype(jnp.float32))
        carry = tuple((total + grad for total, grad in zip(carry, grads[1:])))
        return (carry, (result.astype(jnp.bfloat16), grads[0].astype(jnp.bfloat16)))
    zeros = tuple((jnp.zeros_like(weight) for weight in weights))
    sums, (results, input_grads) = lax.scan(one_sequence, zeros, (inputs, cotangent))
    return (results, input_grads, sums[0], sums[1], sums[2], sums[3], sums[4], sums[5])
```

```python
import functools
import jax, jax.numpy as jnp
from jax import lax
from jax.experimental import pallas as pl
from jax.experimental.pallas import tpu as pltpu

from jax.sharding import PartitionSpec as P

HEADS = 12
HEAD = 64
PAD = 128
VMEM = 56 * 1024 * 1024

def _dot(a, b, ca, cb):
    return lax.dot_general(a, b, (((ca,), (cb,)), ((), ())), preferred_element_type=jnp.float32)

def _half_turn(v):
    lane = lax.broadcasted_iota(jnp.int32, v.shape, 1)
    ahead = pltpu.roll(v, v.shape[1] - HEAD // 2, 1)
    behind = pltpu.roll(v, HEAD // 2, 1)
    return jnp.where(lane % HEAD < HEAD // 2, ahead, behind)

def project_kernel(heads, x_ref, gain_ref, w_ref, cos_ref, sin_ref, normed_ref, q_ref, k_ref, v_ref):
    x = x_ref[...].astype(jnp.float32)
    centred = x - jnp.mean(x, axis=1, keepdims=True)
    variance = jnp.mean(centred * centred, axis=1, keepdims=True)
    normed = (centred * lax.rsqrt(variance + 1e-5) * gain_ref[...]).astype(jnp.bfloat16)
    normed_ref[...] = normed
    qkv = _dot(normed, w_ref[...], 1, 0)
    span = heads * HEAD
    qk = qkv[:, : 2 * span]
    cos = jnp.concatenate([cos_ref[...]] * heads, axis=1)
    sin = jnp.concatenate([sin_ref[...]] * heads, axis=1)
    qk = qk * cos + _half_turn(qk) * sin
    rows = x.shape[0]
    zeros = jnp.zeros((rows, PAD - HEAD), jnp.bfloat16)
    ones = jnp.where(lax.broadcasted_iota(jnp.int32, (rows, PAD - HEAD), 1) < 3, 1.0, 0.0).astype(jnp.bfloat16)
    for h in range(heads):
        at = slice(h * PAD, (h + 1) * PAD)
        lo = h * HEAD
        q_ref[:, at] = jnp.concatenate([(qk[:, lo : lo + HEAD] * HEAD ** -0.5).astype(jnp.bfloat16), zeros], axis=1)
        k_ref[:, at] = jnp.concatenate([qk[:, span + lo : span + lo + HEAD].astype(jnp.bfloat16), ones], axis=1)
        v_ref[:, at] = jnp.concatenate([qkv[:, 2 * span + lo : 2 * span + lo + HEAD].astype(jnp.bfloat16), ones], axis=1)

def project(x, gain, w, cos, sin, heads, block=512):
    length, width = x.shape
    row = lambda n: pl.BlockSpec((block, n), lambda i: (i, 0))
    whole = lambda a: pl.BlockSpec(a.shape, lambda i: (0, 0))
    outs = [jax.ShapeDtypeStruct((length, width), jnp.bfloat16)] + [jax.ShapeDtypeStruct((length, heads * PAD), jnp.bfloat16)] * 3
    return pl.pallas_call(
        functools.partial(project_kernel, heads),
        grid=(length // block,),
        in_specs=[row(width), whole(gain), whole(w), row(cos.shape[1]), row(sin.shape[1])],
        out_specs=[row(width)] + [row(heads * PAD)] * 3,
        out_shape=outs,
        compiler_params=pltpu.CompilerParams(vmem_limit_bytes=VMEM),
        name="project",
    )(x, gain, w, cos, sin)

def _parts(v):
    high = v.astype(jnp.bfloat16)
    rest = v - high.astype(jnp.float32)
    mid = rest.astype(jnp.bfloat16)
    low = (rest - mid.astype(jnp.float32)).astype(jnp.bfloat16)
    return high, mid, low

def _with_parts(base, v):
    rows = base.shape[0]
    high, mid, low = _parts(v)
    lane = lax.broadcasted_iota(jnp.int32, (rows, PAD - HEAD), 1)
    f = lambda p: p.astype(jnp.float32)
    tail = jnp.where(lane == 0, f(high), jnp.where(lane == 1, f(mid), jnp.where(lane == 2, f(low), 0.0)))
    return jnp.concatenate([base[:, :HEAD], tail.astype(jnp.bfloat16)], axis=1)

def forward_kernel(heads, q_ref, k_ref, v_ref, ctx_ref, out_ref, qx_ref):
    outs = []
    for h in range(heads):
        at = slice(h * PAD, (h + 1) * PAD)
        q = q_ref[:, at]
        scores = _dot(q, k_ref[:, at], 1, 1)
        top = jnp.max(scores, axis=1, keepdims=True)
        weights = jnp.exp(scores - top).astype(jnp.bfloat16)
        sums = _dot(weights, v_ref[:, at], 1, 0)
        total = sums[:, HEAD : HEAD + 1]
        outs.append(sums[:, :HEAD] / total)
        qx_ref[:, at] = _with_parts(q, -(top + jnp.log(total)))
    out = jnp.concatenate(outs, axis=1)
    out_ref[...] = out
    ctx_ref[...] = out.astype(jnp.bfloat16)

def attend_forward(q, k, v, heads, block=512):
    length = q.shape[0]
    row = lambda n: pl.BlockSpec((block, n), lambda i: (i, 0))
    whole = lambda a: pl.BlockSpec(a.shape, lambda i: (0, 0))
    return pl.pallas_call(
        functools.partial(forward_kernel, heads),
        grid=(length // block,),
        in_specs=[row(heads * PAD), whole(k), whole(v)],
        out_specs=[row(heads * HEAD), row(heads * HEAD), row(heads * PAD)],
        out_shape=[jax.ShapeDtypeStruct((length, heads * HEAD), jnp.bfloat16), jax.ShapeDtypeStruct((length, heads * HEAD), jnp.float32), jax.ShapeDtypeStruct((length, heads * PAD), jnp.bfloat16)],
        compiler_params=pltpu.CompilerParams(vmem_limit_bytes=VMEM),
        name="attend_forward",
    )(q, k, v)

def backward_kernel(heads, q_ref, k_ref, v_ref, do_ref, out_ref, dq_ref, dk_ref, dv_ref, dk_acc, dv_acc):
    step = pl.program_id(0)

    @pl.when(step == 0)
    def _():
        dk_acc[...] = jnp.zeros_like(dk_acc)
        dv_acc[...] = jnp.zeros_like(dv_acc)

    do_all = do_ref[...]
    prod = do_all.astype(jnp.float32) * out_ref[...]
    dqs = []
    for h in range(heads):
        at = slice(h * PAD, (h + 1) * PAD)
        lo = h * HEAD
        q, k, v = q_ref[:, at], k_ref[:, at], v_ref[:, at]
        delta = jnp.sum(prod[:, lo : lo + HEAD], axis=1, keepdims=True)
        do = _with_parts(do_all[:, lo : lo + HEAD], -delta)
        probs = jnp.exp(_dot(k, q, 1, 1))
        back = _dot(v, do, 1, 1)
        score_back = (probs * back).astype(jnp.bfloat16)
        dv_acc[:, at] += _dot(probs.astype(jnp.bfloat16), do, 1, 0)
        dk_acc[:, at] += _dot(score_back, q, 1, 0)
        dqs.append(_dot(score_back, k, 0, 0)[:, :HEAD])
    dq_ref[...] = (jnp.concatenate(dqs, axis=1) * HEAD ** -0.5).astype(jnp.bfloat16)

    @pl.when(step == pl.num_programs(0) - 1)
    def _():
        pick = lambda acc: jnp.concatenate([acc[:, h * PAD : h * PAD + HEAD] for h in range(heads)], axis=1).astype(jnp.bfloat16)
        dk_ref[...] = pick(dk_acc)
        dv_ref[...] = pick(dv_acc)

def attend_backward(q, k, v, do, out, heads, block=512):
    length = q.shape[0]
    row = lambda n: pl.BlockSpec((block, n), lambda i: (i, 0))
    whole = lambda n: pl.BlockSpec((length, n), lambda i: (0, 0))
    span = heads * HEAD
    return pl.pallas_call(
        functools.partial(backward_kernel, heads),
        grid=(length // block,),
        in_specs=[row(heads * PAD), whole(heads * PAD), whole(heads * PAD), row(span), row(span)],
        out_specs=[row(span), whole(span), whole(span)],
        out_shape=[jax.ShapeDtypeStruct((length, span), jnp.bfloat16)] * 3,
        scratch_shapes=[pltpu.VMEM((length, heads * PAD), jnp.float32)] * 2,
        compiler_params=pltpu.CompilerParams(vmem_limit_bytes=VMEM),
        name="attend_backward",
    )(q, k, v, do, out)

def weights_kernel(heads, dq_ref, dk_ref, dv_ref, cos_ref, sin_ref, normed_ref, w_ref, back_ref, grad_ref, acc):
    step = pl.program_id(0)

    @pl.when(step == 0)
    def _():
        acc[...] = jnp.zeros_like(acc)

    cos = jnp.concatenate([cos_ref[...]] * heads, axis=1)
    sin = jnp.concatenate([sin_ref[...]] * heads, axis=1)
    qk = jnp.concatenate([dq_ref[...], dk_ref[...]], axis=1).astype(jnp.float32)
    qk = (qk * cos - _half_turn(qk) * sin).astype(jnp.bfloat16)
    grads = jnp.concatenate([qk, dv_ref[...]], axis=1)
    back_ref[...] = _dot(grads, w_ref[...], 1, 1).astype(jnp.bfloat16)
    acc[...] += _dot(normed_ref[...], grads, 0, 0)

    @pl.when(step == pl.num_programs(0) - 1)
    def _():
        grad_ref[...] = acc[...].astype(jnp.bfloat16)

def project_back(dq, dk, dv, cos, sin, normed, w, heads, block=512):
    length, width = normed.shape
    row = lambda n: pl.BlockSpec((block, n), lambda i: (i, 0))
    whole = lambda a: pl.BlockSpec(a.shape, lambda i: (0, 0))
    span = heads * HEAD
    return pl.pallas_call(
        functools.partial(weights_kernel, heads),
        grid=(length // block,),
        in_specs=[row(span)] * 3 + [row(cos.shape[1]), row(sin.shape[1]), row(width), whole(w)],
        out_specs=[row(width), whole(w)],
        out_shape=[jax.ShapeDtypeStruct((length, width), jnp.bfloat16), jax.ShapeDtypeStruct(w.shape, jnp.bfloat16)],
        scratch_shapes=[pltpu.VMEM(w.shape, jnp.float32)],
        compiler_params=pltpu.CompilerParams(vmem_limit_bytes=VMEM),
        name="project_back",
    )(dq, dk, dv, cos, sin, normed, w)


def exchange(value, axis, distance):
    size = lax.axis_size(axis)
    return lax.ppermute(value, axis, [(i, i ^ distance) for i in range(size)])


def gather_rows(piece, axis):
    size = lax.axis_size(axis)
    here = lax.axis_index(axis)
    pieces, order = piece[None], [0]
    distance = size // 2
    while distance:
        pieces = jnp.concatenate([pieces, exchange(pieces, axis, distance)], axis=0)
        order = order + [place ^ distance for place in order]
        distance //= 2
    where = jnp.asarray([order.index(place) for place in range(size)], jnp.int32)
    spots = where[here ^ jnp.arange(size)]
    return jnp.stack([lax.dynamic_index_in_dim(pieces, spots[place], 0, keepdims=False) for place in range(size)])


def halve(value, axis, bit, dim):
    own = (lax.axis_index(axis) >> bit) & 1
    kept = lax.dynamic_index_in_dim(value, own, dim, keepdims=False)
    sent = lax.dynamic_index_in_dim(value, 1 - own, dim, keepdims=False)
    arrived = exchange(sent, axis, 1 << bit)
    return (kept.astype(jnp.float32) + arrived.astype(jnp.float32)).astype(jnp.bfloat16)


def scatter_rows(value, axis):
    bits = lax.axis_size(axis).bit_length() - 1
    rest = value.shape[1:]
    value = value.reshape((2,) * bits + rest)
    for bit in range(bits):
        value = halve(value, axis, bit, bits - 1 - bit)
    return value


EPSILON = 1e-05
ROPE_BASE = 160000.0


def matmul(left, right):
    return jnp.dot(left, right, preferred_element_type=jnp.float32)


def left_contract(left, right):
    return _dot(left, right, 0, 0)


def right_contract(left, right):
    return _dot(left, right, 1, 1)


def normalize(values):
    centred = values - jnp.mean(values, axis=1, keepdims=True)
    variance = jnp.mean(centred * centred, axis=1, keepdims=True)
    scale_inv = lax.rsqrt(variance + EPSILON)
    return (centred * scale_inv, scale_inv)


def norm_back(grad_hat, normed, scale_inv):
    return scale_inv * (
        grad_hat
        - jnp.mean(grad_hat, axis=1, keepdims=True)
        - normed * jnp.mean(grad_hat * normed, axis=1, keepdims=True)
    )


def rope_tables(places):
    half = HEAD // 2
    inverse = ROPE_BASE ** (-(jnp.arange(half, dtype=jnp.float32) * 2.0 / HEAD))
    angles = places[:, None] * inverse[None, :]
    cosine, sine = lax.optimization_barrier((jnp.cos(angles), jnp.sin(angles)))
    return (
        jnp.concatenate([cosine] * 4, axis=1),
        jnp.concatenate([-sine, sine] * 2, axis=1),
    )


def from_slices(block):
    far = exchange(block, "seq", 2)
    return [block, exchange(block, "seq", 1), far, exchange(far, "seq", 1)]


def in_order(blocks, here):
    stacked = jnp.stack(blocks)
    return [lax.dynamic_index_in_dim(stacked, here ^ i, 0, keepdims=False) for i in range(len(blocks))]


def body(
    inputs,
    norm_one,
    qkv_weight,
    attn_out_weight,
    norm_two,
    mlp_in_weight,
    mlp_out_weight,
    cotangent,
):
    here = lax.axis_index("seq")
    slices = lax.axis_size("seq")
    owners = lax.axis_size("fsdp")
    heads = HEADS // slices
    span = heads * HEAD
    rows, width = inputs.shape[1:]
    share = qkv_weight.shape[0]
    hidden_share = mlp_out_weight.shape[0]
    hidden_size = hidden_share * owners

    x = inputs[0]
    own_columns = lax.dynamic_index_in_dim(
        qkv_weight.reshape(share, 3, slices, span), here, 2, keepdims=False
    ).reshape(share, 3 * span)
    gains = jnp.concatenate([norm_one, norm_two, jnp.zeros((3 * span - 2 * share,), jnp.bfloat16)])
    packed = gather_rows(jnp.concatenate([own_columns, gains[None]], axis=0), "fsdp")
    w_qkv = packed[:, :share].reshape(width, 3 * span)
    gain_one = packed[:, share, :share].reshape(1, width).astype(jnp.float32)
    gain_two = packed[:, share, share : 2 * share].reshape(1, width).astype(jnp.float32)
    x_all = jnp.concatenate(from_slices(x), axis=0)

    def whole(weight):
        part = weight.shape[0] // slices
        if part * slices != weight.shape[0]:
            return lax.all_gather(weight, "fsdp", axis=0, tiled=True)
        mine = lax.dynamic_slice_in_dim(weight, here * part, part, 0)
        return lax.all_gather(mine, ("fsdp", "seq"), axis=0, tiled=True)

    w_attn = whole(attn_out_weight)
    w_in = whole(mlp_in_weight)
    w_out = whole(mlp_out_weight)

    order = here ^ jnp.arange(slices)
    places = (order[:, None] * rows + jnp.arange(rows)[None, :]).reshape(-1).astype(jnp.float32)
    cosine, sine = rope_tables(places)

    normed_all, query, key, value = project(x_all, gain_one, w_qkv, cosine, sine, heads)
    context_all, out_all, query = attend_forward(query, key, value, heads)
    context_blocks = context_all.reshape(slices, rows, span)
    context = [context_blocks[0]] + [exchange(context_blocks[j], "seq", j) for j in range(1, slices)]
    context_low = jnp.concatenate(in_order(context, here), axis=1)

    attended = x.astype(jnp.float32) + matmul(context_low, w_attn)
    normed_hat2, scale_two = normalize(attended)
    normed_low2 = (normed_hat2 * gain_two).astype(jnp.bfloat16)
    gate_up = matmul(normed_low2, w_in)
    first_half = gate_up[:, :hidden_size]
    second_half = gate_up[:, hidden_size:]
    gelu_first, gelu_back = jax.vjp(lambda entry: jax.nn.gelu(entry, approximate=False), first_half)
    hidden_low = (gelu_first * second_half).astype(jnp.bfloat16)
    result = (attended + matmul(hidden_low, w_out)).astype(jnp.bfloat16)
    grad_low = cotangent[0]
    grad_w_out = left_contract(hidden_low, grad_low)
    hidden_grad = right_contract(grad_low, w_out)
    first_grad = gelu_back(hidden_grad * second_half)[0]
    second_grad = hidden_grad * gelu_first
    gate_up_grad = jnp.concatenate([first_grad, second_grad], axis=1).astype(jnp.bfloat16)
    grad_w_in = left_contract(normed_low2, gate_up_grad)
    normed_grad2 = right_contract(gate_up_grad, w_in)
    attended_grad = grad_low.astype(jnp.float32) + norm_back(
        normed_grad2 * gain_two, normed_hat2, scale_two
    )
    branch_low = attended_grad.astype(jnp.bfloat16)
    grad_w_attn = left_contract(context_low, branch_low)
    context_grad = right_contract(branch_low, w_attn).astype(jnp.bfloat16)

    grad_blocks = context_grad.reshape(rows, slices, span)
    grad_blocks = [lax.dynamic_index_in_dim(grad_blocks, here ^ j, 1, keepdims=False) for j in range(slices)]
    context_grad_all = jnp.concatenate(
        [grad_blocks[0]] + [exchange(grad_blocks[j], "seq", j) for j in range(1, slices)], axis=0
    )

    mlp_grads = jnp.concatenate(
        [grad_w_attn.reshape(owners, share, width)]
        + [grad_w_in[:, at : at + width].reshape(owners, share, width) for at in range(0, 2 * hidden_size, width)]
        + [grad_w_out.reshape(owners, hidden_share, width)],
        axis=1,
    ).astype(jnp.bfloat16)
    total_rows = mlp_grads.shape[1]
    half = total_rows // 2
    mlp_grads = halve(mlp_grads.reshape(owners, 2, half, width), "seq", 0, 1)
    cut = (half // 2 + 7) // 8 * 8
    one = mlp_grads[:, :cut].reshape(owners, cut, 2, width // 2)
    two = mlp_grads[:, cut:].reshape(owners, half - cut, 2, width // 2)
    one = scatter_rows(halve(one, "seq", 1, 2), "fsdp")
    two = halve(scatter_rows(two, "fsdp"), "seq", 1, 1)
    mlp_part = jnp.concatenate([one, two], axis=0)

    query_grad, key_grad, value_grad = attend_backward(query, key, value, context_grad_all, out_all, heads)
    back_all, grad_w_qkv = project_back(query_grad, key_grad, value_grad, cosine, sine, normed_all, w_qkv, heads)

    back_blocks = back_all.reshape(slices, rows, width)
    back_near = exchange(back_blocks[1::2], "seq", 1)
    back_pair = back_blocks[::2].astype(jnp.float32) + back_near.astype(jnp.float32)
    back_far = exchange(back_pair[1].astype(jnp.bfloat16), "seq", 2)
    normed_grad1 = back_pair[0] + back_far.astype(jnp.float32)

    qkv_part = scatter_rows(grad_w_qkv.reshape(owners, share, 3 * span), "fsdp")

    float_input = x.astype(jnp.float32)
    normed_hat1, scale_one = normalize(float_input)
    input_grad = attended_grad + norm_back(normed_grad1 * gain_one, normed_hat1, scale_one)

    qkv_blocks = in_order(from_slices(qkv_part), here)
    qkv_grad = jnp.stack([b.reshape(share, 3, span) for b in qkv_blocks], axis=2)
    qkv_grad = qkv_grad.reshape(share, 3 * width).astype(jnp.float32)

    mlp_blocks = in_order(from_slices(mlp_part), here)
    mlp_total = jnp.concatenate(
        [jnp.concatenate([mlp_blocks[core], mlp_blocks[2 + core]], axis=1) for core in range(2)], axis=0
    ).astype(jnp.float32)
    attn_grad = mlp_total[:share]
    count = 2 * hidden_size // width
    in_grad = jnp.concatenate([mlp_total[share * (1 + c) : share * (2 + c)] for c in range(count)], axis=1)
    out_grad = mlp_total[share * (1 + count) :]

    gain_grad1 = jnp.sum(qkv_weight.astype(jnp.float32) * qkv_grad, axis=1) / norm_one.astype(jnp.float32)
    gain_grad2 = jnp.sum(mlp_in_weight.astype(jnp.float32) * in_grad, axis=1) / norm_two.astype(jnp.float32)
    return (
        result[None],
        input_grad.astype(jnp.bfloat16)[None],
        gain_grad1,
        qkv_grad,
        attn_grad,
        gain_grad2,
        in_grad,
        out_grad,
    )


def solution(mesh):
    tokens = P("fsdp", "seq", None)
    vector = P("fsdp")
    matrix = P("fsdp", None)
    return jax.shard_map(
        body,
        mesh=mesh,
        in_specs=(tokens, vector, matrix, matrix, vector, matrix, matrix, tokens),
        out_specs=(tokens, tokens, vector, matrix, matrix, vector, matrix, matrix),
        check_vma=False,
    )
```

```python
import functools
import jax, jax.numpy as jnp
from jax import lax
from jax.experimental import pallas as pl
from jax.experimental.pallas import tpu as pltpu

from jax.sharding import PartitionSpec as P

HEADS = 12
HEAD = 64
PAD = 128
EPSILON = 1e-05
VMEM = 56 * 1024 * 1024
F32 = jnp.float32
BF16 = jnp.bfloat16


def _dot(a, b, ca, cb):
    return lax.dot_general(a, b, (((ca,), (cb,)), ((), ())), preferred_element_type=F32)


def _normalize(values):
    centred = values - jnp.mean(values, axis=1, keepdims=True)
    variance = jnp.mean(centred * centred, axis=1, keepdims=True)
    scale_inv = lax.rsqrt(variance + EPSILON)
    return centred * scale_inv, scale_inv


def _norm_back(grad_hat, normed, scale_inv):
    return scale_inv * (
        grad_hat
        - jnp.mean(grad_hat, axis=1, keepdims=True)
        - normed * jnp.mean(grad_hat * normed, axis=1, keepdims=True)
    )


def _half_turn(v):
    lane = lax.broadcasted_iota(jnp.int32, v.shape, 1)
    ahead = pltpu.roll(v, v.shape[1] - HEAD // 2, 1)
    behind = pltpu.roll(v, HEAD // 2, 1)
    return jnp.where(lane % HEAD < HEAD // 2, ahead, behind)


def _parts(v):
    high = v.astype(BF16)
    rest = v - high.astype(F32)
    mid = rest.astype(BF16)
    low = (rest - mid.astype(F32)).astype(BF16)
    return high, mid, low


def _with_parts(base, v):
    rows = base.shape[0]
    high, mid, low = _parts(v)
    lane = lax.broadcasted_iota(jnp.int32, (rows, PAD - HEAD), 1)
    f = lambda p: p.astype(F32)
    tail = jnp.where(lane == 0, f(high), jnp.where(lane == 1, f(mid), jnp.where(lane == 2, f(low), 0.0)))
    return jnp.concatenate([base[:, :HEAD], tail.astype(BF16)], axis=1)


def _params():
    return pltpu.CompilerParams(vmem_limit_bytes=VMEM)


def _row(block, n, first=0):
    return pl.BlockSpec((block, n), lambda i, *_: (i + first, 0))


def _whole(a):
    rank = len(a.shape)
    return pl.BlockSpec(a.shape, lambda i, *_: (0,) * rank)


def _shape(shape, dtype=BF16):
    return jax.ShapeDtypeStruct(shape, dtype)


def _cost(flops, size, transcendentals=0):
    return pl.CostEstimate(flops=int(flops), bytes_accessed=int(size), transcendentals=int(transcendentals))


def project_kernel(heads, spots, x0, x1, x2, x3, even_ref, odd_ref, cos_ref, sin_ref, w_ref, normed_ref, q_ref, k_ref, v_ref, x_scr):
    step = pl.program_id(0)
    owners = w_ref.shape[0] // even_ref.shape[1]
    share = even_ref.shape[1]

    @pl.when(step == 0)
    def _():
        for i in range(owners):
            at = slice(i * share, (i + 1) * share)
            spot = spots[i]
            if owners == 1:
                w_ref[at] = even_ref[0]
            else:
                half = owners // 2

                @pl.when(spot < half)
                def _():
                    w_ref[at] = even_ref[spot]

                @pl.when(spot >= half)
                def _():
                    w_ref[at] = odd_ref[spot - half]

    for j, ref in enumerate((x0, x1, x2, x3)):

        @pl.when(step == j)
        def _(ref=ref):
            x_scr[...] = ref[...]

    normed = _normalize(x_scr[...].astype(F32))[0].astype(BF16)
    normed_ref[...] = normed
    qkv = _dot(normed, w_ref[...], 1, 0)
    span = heads * HEAD
    qk = qkv[:, : 2 * span]
    cos = jnp.concatenate([cos_ref[...]] * heads, axis=1)
    sin = jnp.concatenate([sin_ref[...]] * heads, axis=1)
    qk = qk * cos + _half_turn(qk) * sin
    rows = x0.shape[0]
    zeros = jnp.zeros((rows, PAD - HEAD), BF16)
    ones = jnp.where(lax.broadcasted_iota(jnp.int32, (rows, PAD - HEAD), 1) < 3, 1.0, 0.0).astype(BF16)
    for h in range(heads):
        at = slice(h * PAD, (h + 1) * PAD)
        lo = h * HEAD
        q_ref[:, at] = jnp.concatenate([(qk[:, lo : lo + HEAD] * HEAD ** -0.5).astype(BF16), zeros], axis=1)
        k_ref[:, at] = jnp.concatenate([qk[:, span + lo : span + lo + HEAD].astype(BF16), ones], axis=1)
        v_ref[:, at] = jnp.concatenate([qkv[:, 2 * span + lo : 2 * span + lo + HEAD].astype(BF16), ones], axis=1)


def project(spots, xs, even, odd, cos, sin, heads):
    rows, width = xs[0].shape
    length = rows * len(xs)
    columns = even.shape[2]
    w_shape = _shape((width, columns))
    return pl.pallas_call(
        functools.partial(project_kernel, heads),
        grid_spec=pltpu.PrefetchScalarGridSpec(
            num_scalar_prefetch=1,
            grid=(len(xs),),
            in_specs=[_whole(x) for x in xs] + [_whole(even), _whole(odd), _row(rows, cos.shape[1]), _row(rows, sin.shape[1])],
            out_specs=[_whole(w_shape), _row(rows, width)] + [_row(rows, heads * PAD)] * 3,
            scratch_shapes=[pltpu.VMEM((rows, width), BF16)],
        ),
        out_shape=[w_shape, _shape((length, width))] + [_shape((length, heads * PAD))] * 3,
        compiler_params=_params(),
        cost_estimate=_cost(2 * length * width * columns, 12 << 20),
        name="project",
    )(spots, *xs, even, odd, cos, sin)


def forward_kernel(heads, q_ref, k_ref, v_ref, ctx_ref, out_ref, qx_ref):
    outs = []
    for h in range(heads):
        at = slice(h * PAD, (h + 1) * PAD)
        q = q_ref[:, at]
        scores = _dot(q, k_ref[:, at], 1, 1)
        top = jnp.max(scores, axis=1, keepdims=True)
        weights = jnp.exp(scores - top).astype(BF16)
        sums = _dot(weights, v_ref[:, at], 1, 0)
        total = sums[:, HEAD : HEAD + 1]
        outs.append(sums[:, :HEAD] / total)
        qx_ref[:, at] = _with_parts(q, -(top + jnp.log(total)))
    out = jnp.concatenate(outs, axis=1)
    out_ref[...] = out
    ctx_ref[0] = out.astype(BF16)


def attend_forward(q, k, v, heads, block, first, count):
    length = k.shape[0]
    span = heads * HEAD
    return pl.pallas_call(
        functools.partial(forward_kernel, heads),
        grid=(count,),
        in_specs=[_row(block, heads * PAD, first), _whole(k), _whole(v)],
        out_specs=[pl.BlockSpec((1, block, span), lambda i: (i, 0, 0)), _row(block, span), _row(block, heads * PAD)],
        out_shape=[_shape((count, block, span)), _shape((count * block, span), F32), _shape((count * block, heads * PAD))],
        compiler_params=_params(),
        cost_estimate=_cost(16 * heads * count * block * length * HEAD, 6 << 20, heads * count * block * length),
        name="attend_forward",
    )(q, k, v)


def backward_kernel(heads, q_ref, k_ref, v_ref, do0_ref, do1_ref, out_ref, dq_ref, dk_ref, dv_ref, dk_acc, dv_acc):
    step = pl.program_id(0)

    @pl.when(step == 0)
    def _():
        dk_acc[...] = jnp.zeros_like(dk_acc)
        dv_acc[...] = jnp.zeros_like(dv_acc)

    do_all = jnp.where(step == 0, do0_ref[...], do1_ref[...])
    prod = do_all.astype(F32) * out_ref[...]
    dqs = []
    for h in range(heads):
        at = slice(h * PAD, (h + 1) * PAD)
        lo = h * HEAD
        q, k, v = q_ref[:, at], k_ref[:, at], v_ref[:, at]
        delta = jnp.sum(prod[:, lo : lo + HEAD], axis=1, keepdims=True)
        do = _with_parts(do_all[:, lo : lo + HEAD], -delta)
        probs = jnp.exp(_dot(k, q, 1, 1))
        back = _dot(v, do, 1, 1)
        score_back = (probs * back).astype(BF16)
        dv_acc[:, at] += _dot(probs.astype(BF16), do, 1, 0)
        dk_acc[:, at] += _dot(score_back, q, 1, 0)
        dqs.append(_dot(score_back, k, 0, 0)[:, :HEAD])
    dq_ref[...] = (jnp.concatenate(dqs, axis=1) * HEAD ** -0.5).astype(BF16)

    @pl.when(step == pl.num_programs(0) - 1)
    def _():
        pick = lambda acc: jnp.concatenate([acc[:, h * PAD : h * PAD + HEAD] for h in range(heads)], axis=1).astype(BF16)
        dk_ref[...] = pick(dk_acc)
        dv_ref[...] = pick(dv_acc)


def attend_backward(q, k, v, do0, do1, out, heads):
    length = k.shape[0]
    block, span = do0.shape
    whole = _shape((length, span))
    return pl.pallas_call(
        functools.partial(backward_kernel, heads),
        grid=(2,),
        in_specs=[_row(block, heads * PAD), _whole(k), _whole(v), _whole(do0), _whole(do1), _row(block, span)],
        out_specs=[_row(block, span), _whole(whole), _whole(whole)],
        out_shape=[_shape((2 * block, span)), whole, whole],
        scratch_shapes=[pltpu.VMEM((length, heads * PAD), F32)] * 2,
        compiler_params=_params(),
        cost_estimate=_cost(40 * heads * 2 * block * length * HEAD, 8 << 20, heads * 2 * block * length),
        name="attend_backward",
    )(q, k, v, do0, do1, out)


def _gelu(first):
    cumulative = 0.5 * (1.0 + lax.erf(first * 0.5 ** 0.5))
    density = jnp.exp(-0.5 * first * first) * 0.3989422804014327
    return first * cumulative, cumulative + first * density


def feed_kernel(share, group, here, x_ref, cot_ref, own_ref, near_ref, far_ref, diag_ref, w_ref, result_ref, back_ref, grad0, grad1, grad2, ctx_ref, n2_ref, hidden_ref, gates_ref, branch_ref, attn_scr, in_scr, out_scr):
    width = x_ref.shape[1]
    hidden_size = out_scr.shape[0]
    owners = w_ref.shape[0]
    span = width // group
    blocks = in_scr.shape[0]

    @pl.when(pl.program_id(0) == 0)
    def _():
        pick = lambda lo, hi: w_ref[:, lo:hi].reshape(owners * (hi - lo), width)
        attn = pick(0, share)
        for g in range(group):
            spot = here[0] ^ g
            attn_scr[pl.ds(pl.multiple_of(spot * span, span), span)] = attn[g * span : (g + 1) * span]
        for c in range(blocks):
            in_scr[c] = pick(share * (1 + c), share * (2 + c))
        out_scr[...] = pick(share * (1 + blocks), share * (1 + blocks) + hidden_size // owners)

    ctx = jnp.concatenate([own_ref[0], near_ref[0], far_ref[0], diag_ref[0]], axis=1)
    ctx_ref[...] = ctx
    attended = x_ref[...].astype(F32) + _dot(ctx, attn_scr[...], 1, 0)
    hat, scale = _normalize(attended)
    n2 = hat.astype(BF16)
    n2_ref[...] = n2
    gate_up = jnp.concatenate([_dot(n2, in_scr[c], 1, 0) for c in range(blocks)], axis=1)
    first, second = gate_up[:, :hidden_size], gate_up[:, hidden_size:]
    gelu, slope = _gelu(first)
    hidden = (gelu * second).astype(BF16)
    hidden_ref[...] = hidden
    result_ref[0] = (attended + _dot(hidden, out_scr[...], 1, 0)).astype(BF16)
    cot = cot_ref[...]
    hidden_back = _dot(cot, out_scr[...], 1, 1)
    gates = jnp.concatenate([hidden_back * second * slope, hidden_back * gelu], axis=1).astype(BF16)
    gates_ref[...] = gates
    back = sum(_dot(gates[:, c * width : (c + 1) * width], in_scr[c], 1, 1) for c in range(blocks))
    back = cot.astype(F32) + _norm_back(back, hat, scale)
    back_ref[...] = back
    branch = back.astype(BF16)
    branch_ref[...] = branch
    grads = _dot(branch, attn_scr[...], 1, 1).astype(BF16)
    grad0[...] = grads[:, :span]
    grad1[...] = grads[:, span : 2 * span]
    grad2[0] = grads[:, 2 * span : 3 * span]
    grad2[1] = grads[:, 3 * span :]


def feed(here, x, cot, own, near, far, diag, packed, share, hidden_size, block=256):
    rows, width = x.shape
    span = own.shape[2]
    group = width // span
    blocks = 2 * hidden_size // width
    lead = lambda: pl.BlockSpec((1, block, span), lambda i, *_: (0, i, 0))
    widths = (width, width, hidden_size, 2 * hidden_size, width)
    return pl.pallas_call(
        functools.partial(feed_kernel, share, group),
        grid_spec=pltpu.PrefetchScalarGridSpec(
            num_scalar_prefetch=1,
            grid=(rows // block,),
            in_specs=[_row(block, width), _row(block, width), lead(), lead(), lead(), lead(), _whole(packed)],
            out_specs=[pl.BlockSpec((1, block, width), lambda i, *_: (0, i, 0)), _row(block, width), _row(block, span), _row(block, span), pl.BlockSpec((2, block, span), lambda i, *_: (0, i, 0))]
            + [_row(block, n) for n in widths],
            scratch_shapes=[pltpu.VMEM((width, width), BF16), pltpu.VMEM((blocks, width, width), BF16), pltpu.VMEM((hidden_size, width), BF16)],
        ),
        out_shape=[_shape((1, rows, width)), _shape((rows, width), F32), _shape((rows, span)), _shape((rows, span)), _shape((2, rows, span))]
        + [_shape((rows, n)) for n in widths],
        compiler_params=_params(),
        cost_estimate=_cost(4 * rows * width * (width + 3 * hidden_size), 20 << 20, 2 * rows * hidden_size),
        name="feed",
    )(here, x, cot, own, near, far, diag, packed)


def feed_grads_kernel(owners, share, hidden_share, group, here, ctx_ref, branch_ref, n2_ref, gates_ref, hidden_ref, cot_ref, kept_ref, sent_ref, attn_scr):
    width = branch_ref.shape[1]
    span = width // group
    half = kept_ref.shape[1]
    core = here[0] & 1

    def place(value, start, size):
        value = value.reshape(owners, size, width).astype(BF16)
        for side in range(2):
            lo, hi = max(start, side * half), min(start + size, (side + 1) * half)
            if lo < hi:
                part = value[:, lo - start : hi - start]
                at = slice(lo - side * half, hi - side * half)

                @pl.when(core == side)
                def _(part=part, at=at):
                    kept_ref[:, at] = part

                @pl.when(core != side)
                def _(part=part, at=at):
                    sent_ref[:, at] = part

    total = share * (1 + gates_ref.shape[1] // width) + hidden_share
    attn = _dot(ctx_ref[...], branch_ref[...], 0, 0)
    for g in range(group):
        spot = here[0] ^ g
        attn_scr[pl.ds(pl.multiple_of(spot * span, span), span)] = attn[g * span : (g + 1) * span]
    place(attn_scr[...], 0, share)
    n2 = n2_ref[...]
    for c in range(gates_ref.shape[1] // width):
        place(_dot(n2, gates_ref[:, c * width : (c + 1) * width], 0, 0), share * (1 + c), share)
    place(_dot(hidden_ref[...], cot_ref[...], 0, 0), total - hidden_share, hidden_share)
    if total < 2 * half:
        place(jnp.zeros((owners * (2 * half - total), width), F32), total, 2 * half - total)


def feed_grads(here, ctx, branch, n2, gates, hidden, cot, owners, half):
    width = branch.shape[1]
    arrays = (ctx, branch, n2, gates, hidden, cot)
    return pl.pallas_call(
        functools.partial(feed_grads_kernel, owners, width // owners, hidden.shape[1] // owners, 4),
        grid_spec=pltpu.PrefetchScalarGridSpec(
            num_scalar_prefetch=1,
            grid=(1,),
            in_specs=[_whole(a) for a in arrays],
            out_specs=[_whole(_shape((owners, half, width)))] * 2,
            scratch_shapes=[pltpu.VMEM((width, width), F32)],
        ),
        out_shape=[_shape((owners, half, width))] * 2,
        compiler_params=_params(),
        cost_estimate=_cost(2 * branch.shape[0] * width * (width + 3 * hidden.shape[1]), 12 << 20),
        name="feed_grads",
    )(here, *arrays)


def qkv_grads_kernel(heads, dq0, dq1, dk0, dk1, dv0, dv1, cos_ref, sin_ref, normed_ref, grads_ref, grad_ref, acc):
    step = pl.program_id(0)

    @pl.when(step == 0)
    def _():
        acc[...] = jnp.zeros_like(acc)

    cos = jnp.concatenate([cos_ref[...]] * heads, axis=1)
    sin = jnp.concatenate([sin_ref[...]] * heads, axis=1)
    dq = jnp.where(step < pl.num_programs(0) // 2, dq0[...].astype(F32), dq1[...].astype(F32))
    dk = dk0[...].astype(F32) + dk1[...].astype(F32)
    qk = jnp.concatenate([dq, dk], axis=1)
    qk = (qk * cos - _half_turn(qk) * sin).astype(BF16)
    dv = (dv0[...].astype(F32) + dv1[...].astype(F32)).astype(BF16)
    grads = jnp.concatenate([qk, dv], axis=1)
    grads_ref[...] = grads
    acc[...] += _dot(normed_ref[...], grads, 0, 0)

    @pl.when(step == pl.num_programs(0) - 1)
    def _():
        grad_ref[...] = acc[...].astype(BF16)


def qkv_grads(dqs, dks, dvs, cos, sin, normed, heads, block):
    length, width = normed.shape
    span = heads * HEAD
    grad = _shape((width, 3 * span))
    halves = length // block // 2
    return pl.pallas_call(
        functools.partial(qkv_grads_kernel, heads),
        grid=(2 * halves,),
        in_specs=[
            pl.BlockSpec((block, span), lambda i: (jnp.minimum(i, halves - 1), 0)),
            pl.BlockSpec((block, span), lambda i: (jnp.maximum(i - halves, 0), 0)),
        ]
        + [_row(block, span)] * 4
        + [_row(block, cos.shape[1])] * 2
        + [_row(block, width)],
        out_specs=[_row(block, 3 * span), _whole(grad)],
        out_shape=[_shape((length, 3 * span)), grad],
        scratch_shapes=[pltpu.VMEM(grad.shape, F32)],
        compiler_params=_params(),
        cost_estimate=_cost(2 * length * width * 3 * span, 8 << 20),
        name="qkv_grads",
    )(*dqs, *dks, *dvs, cos, sin, normed)


def input_back_kernel(grads_ref, w_ref, kept_ref, sent_ref):
    back = _dot(grads_ref[...], w_ref[...], 1, 1).astype(BF16)

    @pl.when(pl.program_id(0) % 2 == 0)
    def _():
        kept_ref[0] = back

    @pl.when(pl.program_id(0) % 2 == 1)
    def _():
        sent_ref[0] = back


def input_back(grads, w, block):
    length, columns = grads.shape
    width = w.shape[0]
    spec = pl.BlockSpec((1, block, width), lambda i: (i // 2, 0, 0))
    return pl.pallas_call(
        input_back_kernel,
        grid=(length // block,),
        in_specs=[_row(block, columns), _whole(w)],
        out_specs=[spec, spec],
        out_shape=[_shape((length // block // 2, block, width))] * 2,
        compiler_params=_params(),
        cost_estimate=_cost(2 * length * width * columns, 6 << 20),
        name="input_back",
    )(grads, w)


def exchange(value, axis, distance):
    size = lax.axis_size(axis)
    return lax.ppermute(value, axis, [(i, i ^ distance) for i in range(size)])


def gather_halves(piece, axis):
    size = lax.axis_size(axis)
    pieces, order = piece[None], [0]
    distance = size // 2
    while distance > 1:
        pieces = jnp.concatenate([pieces, exchange(pieces, axis, distance)], axis=0)
        order = order + [place ^ distance for place in order]
        distance //= 2
    other = exchange(pieces, axis, 1)
    order = order + [place ^ 1 for place in order]
    where = jnp.asarray([order.index(place) for place in range(size)], jnp.int32)
    return pieces, other, where[lax.axis_index(axis) ^ jnp.arange(size)]


def halve(addends, axis, bit, take):
    own = (lax.axis_index(axis) >> bit) & 1
    sent = sum(take(a, 1 - own).astype(F32) for a in addends).astype(BF16)
    return [take(a, own) for a in addends] + [exchange(sent, axis, 1 << bit)]


def scatter_rows(addends, axis):
    bits = lax.axis_size(axis).bit_length() - 1
    addends = [a.reshape((2,) * bits + a.shape[1:]) for a in addends]
    for bit in range(bits):
        dim = bits - 1 - bit
        addends = halve(addends, axis, bit, lambda a, at: lax.dynamic_index_in_dim(a, at, dim, keepdims=False))
    return addends


def total(addends):
    return sum(a.astype(F32) for a in addends)


ROPE_BASE = 160000.0


def rope_tables(places):
    half = HEAD // 2
    inverse = ROPE_BASE ** (-(jnp.arange(half, dtype=F32) * 2.0 / HEAD))
    angles = places[:, None] * inverse[None, :]
    cosine, sine = lax.optimization_barrier((jnp.cos(angles), jnp.sin(angles)))
    return (
        jnp.concatenate([cosine] * 4, axis=1),
        jnp.concatenate([-sine, sine] * 2, axis=1),
    )


def from_slices(block):
    far = exchange(block, "seq", 2)
    return [block, exchange(block, "seq", 1), far, exchange(far, "seq", 1)]


def in_order(blocks, here):
    stacked = jnp.stack(blocks)
    return [lax.dynamic_index_in_dim(stacked, here ^ i, 0, keepdims=False) for i in range(len(blocks))]


def up16(n):
    return -(-n // 16) * 16


def body(
    inputs,
    norm_one,
    qkv_weight,
    attn_out_weight,
    norm_two,
    mlp_in_weight,
    mlp_out_weight,
    cotangent,
):
    here = lax.axis_index("seq")
    slices = lax.axis_size("seq")
    owners = lax.axis_size("fsdp")
    heads = HEADS // slices
    span = heads * HEAD
    rows, width = inputs.shape[1:]
    share = qkv_weight.shape[0]
    hidden_share = mlp_out_weight.shape[0]
    hidden_size = hidden_share * owners
    blocks = 2 * hidden_size // width
    aligned = share % 16 == 0 and hidden_share % 16 == 0
    spot = jnp.reshape(here, (1,)).astype(jnp.int32)

    x = inputs[0]
    scaled_qkv = (qkv_weight.astype(F32) * norm_one.astype(F32)[:, None]).astype(BF16)
    scaled_in = (mlp_in_weight.astype(F32) * norm_two.astype(F32)[:, None]).astype(BF16)
    x_far = exchange(x, "seq", 2)
    own_columns = jnp.concatenate(
        [lax.dynamic_slice_in_dim(scaled_qkv, c * width + here * span, span, 1) for c in range(3)], axis=1
    )
    even, odd, spots = gather_halves(own_columns, "fsdp")
    xs = [x, exchange(x, "seq", 1), x_far, exchange(x_far, "seq", 1)]
    if not aligned:
        pieces = jnp.concatenate([even, odd], axis=0)
        even = jnp.take(pieces, spots, axis=0).reshape(1, width, 3 * span)
        odd, spots = even, jnp.zeros((1,), jnp.int32)

    shard = [attn_out_weight] + [scaled_in[:, c * width : (c + 1) * width] for c in range(blocks)] + [mlp_out_weight]
    shard_rows = share * (1 + blocks) + hidden_share
    part = up16(-(-shard_rows // slices))
    shard = jnp.concatenate(shard + [jnp.zeros((part * slices - shard_rows, width), BF16)], axis=0)
    packed = lax.all_gather(lax.dynamic_slice_in_dim(shard, here * part, part, 0), ("fsdp", "seq"), axis=0, tiled=True)
    packed = packed.reshape(owners, part * slices, width)
    packed_share = share
    if not aligned:
        cuts = [share * c for c in range(2 + blocks)] + [shard_rows]
        packed = jnp.concatenate([packed[:, a:b].reshape(-1, width) for a, b in zip(cuts, cuts[1:])], axis=0)[None]
        packed_share = width

    order = here ^ jnp.arange(slices)
    places = (order[:, None] * rows + jnp.arange(rows)[None, :]).reshape(-1).astype(F32)
    cosine, sine = rope_tables(places)

    w_qkv, normed_all, query, key, value = project(spots, xs, even, odd, cosine, sine, heads)
    context_far, out_far, query_far = attend_forward(query, key, value, heads, rows, 2, 2)
    context_far = exchange(context_far, "seq", 2)
    context_near, out_near, query_near = attend_forward(query, key, value, heads, rows, 0, 2)
    context_1 = exchange(context_near[1:], "seq", 1)
    context_3 = exchange(context_far[1:], "seq", 1)

    cot = cotangent[0]
    result, attended_grad, grad0, grad1, grad23, context_low, normed_two, hidden, gates, branch = feed(
        spot, x, cot, context_near, context_1, context_far, context_3, packed, packed_share, hidden_size
    )
    grad23 = exchange(grad23, "seq", 2)
    grad1 = exchange(grad1, "seq", 1)
    grad3 = exchange(grad23[1], "seq", 1)

    grad_rows = up16(-(-shard_rows // 2))
    packed_owners = owners if aligned else 1
    if aligned:
        kept, sent = feed_grads(spot, context_low, branch, normed_two, gates, hidden, cot, owners, grad_rows)
    else:
        whole_rows = width * (1 + blocks) + hidden_size
        kept, sent = feed_grads(spot, context_low, branch, normed_two, gates, hidden, cot, 1, whole_rows // 2)
        core = here & 1
        both = jnp.where(core == 0, jnp.concatenate([kept, sent], axis=1), jnp.concatenate([sent, kept], axis=1))[0]
        cuts = [width * c for c in range(2 + blocks)] + [whole_rows]
        both = jnp.concatenate([both[a:b].reshape(owners, -1, width) for a, b in zip(cuts, cuts[1:])], axis=1)
        both = jnp.pad(both, ((0, 0), (0, 2 * grad_rows - shard_rows), (0, 0)))
        kept = lax.dynamic_slice_in_dim(both, core * grad_rows, grad_rows, 1)
        sent = lax.dynamic_slice_in_dim(both, (1 - core) * grad_rows, grad_rows, 1)
    mlp_grads = [kept, exchange(sent, "seq", 1)]
    cut = up16(grad_rows // 2)
    columns = lambda a, at: lax.dynamic_slice_in_dim(a, at * (width // 2), width // 2, a.ndim - 1)
    one = scatter_rows(halve([a[:, :cut] for a in mlp_grads], "seq", 1, columns), "fsdp")
    two = halve(scatter_rows([a[:, cut:] for a in mlp_grads], "fsdp"), "seq", 1, columns)
    mlp_part = jnp.concatenate([total(one), total(two)], axis=0).astype(BF16)

    dq_near, dk_near, dv_near = attend_backward(query_near, key, value, grad0, grad1, out_near, heads)
    dq_far, dk_far, dv_far = attend_backward(query_far, key, value, grad23[0], grad3, out_far, heads)
    qkv_back, qkv_grad = qkv_grads(
        (dq_near, dq_far), (dk_near, dk_far), (dv_near, dv_far), cosine, sine, normed_all, heads, rows
    )
    qkv_part = total(scatter_rows([qkv_grad.reshape(owners, share, 3 * span)], "fsdp")).astype(BF16)

    back_kept, back_sent = input_back(qkv_back, w_qkv, rows)
    back_near = exchange(back_sent, "seq", 1)
    back_far = exchange((back_kept[1].astype(F32) + back_near[1].astype(F32)).astype(BF16), "seq", 2)
    normed_hat, scale_inv = _normalize(x.astype(F32))
    input_grad = attended_grad + _norm_back(total([back_kept[0], back_near[0], back_far]), normed_hat, scale_inv)

    qkv_blocks = in_order(from_slices(qkv_part), here)
    qkv_sum = jnp.concatenate(
        [b[:, c * span : (c + 1) * span] for c in range(3) for b in qkv_blocks], axis=1
    ).astype(F32)

    mlp_blocks = in_order(from_slices(mlp_part), here)
    mlp_sum = jnp.concatenate(
        [jnp.concatenate([mlp_blocks[core], mlp_blocks[2 + core]], axis=1) for core in range(2)], axis=0
    ).astype(F32)
    in_sum = jnp.concatenate([mlp_sum[share * (1 + c) : share * (2 + c)] for c in range(blocks)], axis=1)
    first_out = share * (1 + blocks)
    return (
        result,
        input_grad.astype(BF16)[None],
        jnp.sum(qkv_weight.astype(F32) * qkv_sum, axis=1),
        qkv_sum * norm_one.astype(F32)[:, None],
        mlp_sum[:share],
        jnp.sum(mlp_in_weight.astype(F32) * in_sum, axis=1),
        in_sum * norm_two.astype(F32)[:, None],
        mlp_sum[first_out : first_out + hidden_share],
    )


def solution(mesh):
    tokens = P("fsdp", "seq", None)
    vector = P("fsdp")
    matrix = P("fsdp", None)
    return jax.shard_map(
        body,
        mesh=mesh,
        in_specs=(tokens, vector, matrix, matrix, vector, matrix, matrix, tokens),
        out_specs=(tokens, tokens, vector, matrix, matrix, vector, matrix, matrix),
        check_vma=False,
    )
```

```python
import functools
import jax, jax.numpy as jnp
from jax import lax
from jax.experimental import pallas as pl
from jax.experimental.pallas import tpu as pltpu

from jax.sharding import PartitionSpec as P

HEADS = 12
HEAD = 64
PAD = 128
EPSILON = 1e-05
VMEM = 56 * 1024 * 1024
F32 = jnp.float32
BF16 = jnp.bfloat16


def _dot(a, b, ca, cb):
    return lax.dot_general(a, b, (((ca,), (cb,)), ((), ())), preferred_element_type=F32)


def _normalize(values):
    centred = values - jnp.mean(values, axis=1, keepdims=True)
    variance = jnp.mean(centred * centred, axis=1, keepdims=True)
    scale_inv = lax.rsqrt(variance + EPSILON)
    return centred * scale_inv, scale_inv


def _norm_back(grad_hat, normed, scale_inv):
    return scale_inv * (
        grad_hat
        - jnp.mean(grad_hat, axis=1, keepdims=True)
        - normed * jnp.mean(grad_hat * normed, axis=1, keepdims=True)
    )


def _half_turn(v):
    lane = lax.broadcasted_iota(jnp.int32, v.shape, 1)
    ahead = pltpu.roll(v, v.shape[1] - HEAD // 2, 1)
    behind = pltpu.roll(v, HEAD // 2, 1)
    return jnp.where(lane % HEAD < HEAD // 2, ahead, behind)


def _parts(v):
    high = v.astype(BF16)
    rest = v - high.astype(F32)
    mid = rest.astype(BF16)
    low = (rest - mid.astype(F32)).astype(BF16)
    return high, mid, low


def _with_parts(base, v):
    rows = base.shape[0]
    high, mid, low = _parts(v)
    lane = lax.broadcasted_iota(jnp.int32, (rows, PAD - HEAD), 1)
    f = lambda p: p.astype(F32)
    tail = jnp.where(lane == 0, f(high), jnp.where(lane == 1, f(mid), jnp.where(lane == 2, f(low), 0.0)))
    return jnp.concatenate([base[:, :HEAD], tail.astype(BF16)], axis=1)


def _params():
    return pltpu.CompilerParams(vmem_limit_bytes=VMEM)


def _row(block, n, first=0):
    return pl.BlockSpec((block, n), lambda i, *_: (i + first, 0))


def _whole(a):
    rank = len(a.shape)
    return pl.BlockSpec(a.shape, lambda i, *_: (0,) * rank)


def _unread(tokens):
    return [pl.BlockSpec(memory_space=pl.ANY) for _ in tokens]


def _shape(shape, dtype=BF16):
    return jax.ShapeDtypeStruct(shape, dtype)


def _cost(flops, size, transcendentals=0):
    return pl.CostEstimate(flops=int(flops), bytes_accessed=int(size), transcendentals=int(transcendentals))


def project_kernel(heads, spots, x0, x1, x2, x3, even_ref, odd_ref, cos_ref, sin_ref, w_ref, normed_ref, q_ref, k_ref, v_ref, x_scr):
    step = pl.program_id(0)
    owners = w_ref.shape[0] // even_ref.shape[1]
    share = even_ref.shape[1]

    @pl.when(step == 0)
    def _():
        for i in range(owners):
            at = slice(i * share, (i + 1) * share)
            spot = spots[i]
            if owners == 1:
                w_ref[at] = even_ref[0]
            else:
                half = owners // 2

                @pl.when(spot < half)
                def _():
                    w_ref[at] = even_ref[spot]

                @pl.when(spot >= half)
                def _():
                    w_ref[at] = odd_ref[spot - half]

    for j, ref in enumerate((x0, x1, x2, x3)):

        @pl.when(step == j)
        def _(ref=ref):
            x_scr[...] = ref[...]

    normed = _normalize(x_scr[...].astype(F32))[0].astype(BF16)
    normed_ref[...] = normed
    qkv = _dot(normed, w_ref[...], 1, 0)
    span = heads * HEAD
    qk = qkv[:, : 2 * span]
    cos = jnp.concatenate([cos_ref[...]] * heads, axis=1)
    sin = jnp.concatenate([sin_ref[...]] * heads, axis=1)
    qk = qk * cos + _half_turn(qk) * sin
    rows = x0.shape[0]
    zeros = jnp.zeros((rows, PAD - HEAD), BF16)
    ones = jnp.where(lax.broadcasted_iota(jnp.int32, (rows, PAD - HEAD), 1) < 3, 1.0, 0.0).astype(BF16)
    for h in range(heads):
        at = slice(h * PAD, (h + 1) * PAD)
        lo = h * HEAD
        q_ref[:, at] = jnp.concatenate([(qk[:, lo : lo + HEAD] * HEAD ** -0.5).astype(BF16), zeros], axis=1)
        k_ref[:, at] = jnp.concatenate([qk[:, span + lo : span + lo + HEAD].astype(BF16), ones], axis=1)
        v_ref[:, at] = jnp.concatenate([qkv[:, 2 * span + lo : 2 * span + lo + HEAD].astype(BF16), ones], axis=1)


def project(spots, xs, even, odd, cos, sin, heads):
    rows, width = xs[0].shape
    length = rows * len(xs)
    columns = even.shape[2]
    w_shape = _shape((width, columns))
    return pl.pallas_call(
        functools.partial(project_kernel, heads),
        grid_spec=pltpu.PrefetchScalarGridSpec(
            num_scalar_prefetch=1,
            grid=(len(xs),),
            in_specs=[_whole(x) for x in xs] + [_whole(even), _whole(odd), _row(rows, cos.shape[1]), _row(rows, sin.shape[1])],
            out_specs=[_whole(w_shape), _row(rows, width)] + [_row(rows, heads * PAD)] * 3,
            scratch_shapes=[pltpu.VMEM((rows, width), BF16)],
        ),
        out_shape=[w_shape, _shape((length, width))] + [_shape((length, heads * PAD))] * 3,
        compiler_params=_params(),
        cost_estimate=_cost(2 * length * width * columns, 12 << 20),
        name="project",
    )(spots, *xs, even, odd, cos, sin)


def forward_kernel(heads, q_ref, k_ref, v_ref, ctx_ref, out_ref, qx_ref):
    outs = []
    for h in range(heads):
        at = slice(h * PAD, (h + 1) * PAD)
        q = q_ref[:, at]
        scores = _dot(q, k_ref[:, at], 1, 1)
        top = jnp.max(scores, axis=1, keepdims=True)
        weights = jnp.exp(scores - top).astype(BF16)
        sums = _dot(weights, v_ref[:, at], 1, 0)
        total = sums[:, HEAD : HEAD + 1]
        outs.append(sums[:, :HEAD] / total)
        qx_ref[:, at] = _with_parts(q, -(top + jnp.log(total)))
    out = jnp.concatenate(outs, axis=1)
    out_ref[...] = out
    ctx_ref[0] = out.astype(BF16)


def attend_forward(q, k, v, heads, block, first, count):
    length = k.shape[0]
    span = heads * HEAD
    return pl.pallas_call(
        functools.partial(forward_kernel, heads),
        grid=(count,),
        in_specs=[_row(block, heads * PAD, first), _whole(k), _whole(v)],
        out_specs=[pl.BlockSpec((1, block, span), lambda i: (i, 0, 0)), _row(block, span), _row(block, heads * PAD)],
        out_shape=[_shape((count, block, span)), _shape((count * block, span), F32), _shape((count * block, heads * PAD))],
        compiler_params=_params(),
        cost_estimate=_cost(16 * heads * count * block * length * HEAD, 6 << 20, heads * count * block * length),
        name="attend_forward",
    )(q, k, v)


def backward_kernel(heads, tokens, q_ref, k_ref, v_ref, do0_ref, do1_ref, out_ref, *refs):
    dq_ref, dk_ref, dv_ref, dk_acc, dv_acc = refs[tokens:]
    step = pl.program_id(0)

    @pl.when(step == 0)
    def _():
        dk_acc[...] = jnp.zeros_like(dk_acc)
        dv_acc[...] = jnp.zeros_like(dv_acc)

    do_all = jnp.where(step == 0, do0_ref[...], do1_ref[...])
    prod = do_all.astype(F32) * out_ref[...]
    dqs = []
    for h in range(heads):
        at = slice(h * PAD, (h + 1) * PAD)
        lo = h * HEAD
        q, k, v = q_ref[:, at], k_ref[:, at], v_ref[:, at]
        delta = jnp.sum(prod[:, lo : lo + HEAD], axis=1, keepdims=True)
        do = _with_parts(do_all[:, lo : lo + HEAD], -delta)
        probs = jnp.exp(_dot(k, q, 1, 1))
        back = _dot(v, do, 1, 1)
        score_back = (probs * back).astype(BF16)
        dv_acc[:, at] += _dot(probs.astype(BF16), do, 1, 0)
        dk_acc[:, at] += _dot(score_back, q, 1, 0)
        dqs.append(_dot(score_back, k, 0, 0)[:, :HEAD])
    dq_ref[...] = (jnp.concatenate(dqs, axis=1) * HEAD ** -0.5).astype(BF16)

    @pl.when(step == pl.num_programs(0) - 1)
    def _():
        pick = lambda acc: jnp.concatenate([acc[:, h * PAD : h * PAD + HEAD] for h in range(heads)], axis=1).astype(BF16)
        dk_ref[...] = pick(dk_acc)
        dv_ref[...] = pick(dv_acc)


def attend_backward(q, k, v, do0, do1, out, heads, tokens=()):
    length = k.shape[0]
    block, span = do0.shape
    whole = _shape((length, span))
    return pl.pallas_call(
        functools.partial(backward_kernel, heads, len(tokens)),
        grid=(2,),
        in_specs=[_row(block, heads * PAD), _whole(k), _whole(v), _whole(do0), _whole(do1), _row(block, span)] + _unread(tokens),
        out_specs=[_row(block, span), _whole(whole), _whole(whole)],
        out_shape=[_shape((2 * block, span)), whole, whole],
        scratch_shapes=[pltpu.VMEM((length, heads * PAD), F32)] * 2,
        compiler_params=_params(),
        cost_estimate=_cost(40 * heads * 2 * block * length * HEAD, 8 << 20, heads * 2 * block * length),
        name="attend_backward",
    )(q, k, v, do0, do1, out, *tokens)


def _gelu(first):
    cumulative = 0.5 * (1.0 + lax.erf(first * 0.5 ** 0.5))
    density = jnp.exp(-0.5 * first * first) * 0.3989422804014327
    return first * cumulative, cumulative + first * density


def feed_kernel(share, group, here, x_ref, cot_ref, own_ref, near_ref, far_ref, diag_ref, w_ref, result_ref, back_ref, grad0, grad1, grad2, ctx_ref, n2_ref, hidden_ref, gates_ref, branch_ref, attn_scr, in_scr, out_scr):
    width = x_ref.shape[1]
    hidden_size = out_scr.shape[0]
    owners = w_ref.shape[0]
    span = width // group
    blocks = in_scr.shape[0]

    @pl.when(pl.program_id(0) == 0)
    def _():
        pick = lambda lo, hi: w_ref[:, lo:hi].reshape(owners * (hi - lo), width)
        attn = pick(0, share)
        for g in range(group):
            spot = here[0] ^ g
            attn_scr[pl.ds(pl.multiple_of(spot * span, span), span)] = attn[g * span : (g + 1) * span]
        for c in range(blocks):
            in_scr[c] = pick(share * (1 + c), share * (2 + c))
        out_scr[...] = pick(share * (1 + blocks), share * (1 + blocks) + hidden_size // owners)

    ctx = jnp.concatenate([own_ref[0], near_ref[0], far_ref[0], diag_ref[0]], axis=1)
    ctx_ref[...] = ctx
    attended = x_ref[...].astype(F32) + _dot(ctx, attn_scr[...], 1, 0)
    hat, scale = _normalize(attended)
    n2 = hat.astype(BF16)
    n2_ref[...] = n2
    gate_up = jnp.concatenate([_dot(n2, in_scr[c], 1, 0) for c in range(blocks)], axis=1)
    first, second = gate_up[:, :hidden_size], gate_up[:, hidden_size:]
    gelu, slope = _gelu(first)
    hidden = (gelu * second).astype(BF16)
    hidden_ref[...] = hidden
    result_ref[0] = (attended + _dot(hidden, out_scr[...], 1, 0)).astype(BF16)
    cot = cot_ref[...]
    hidden_back = _dot(cot, out_scr[...], 1, 1)
    gates = jnp.concatenate([hidden_back * second * slope, hidden_back * gelu], axis=1).astype(BF16)
    gates_ref[...] = gates
    back = sum(_dot(gates[:, c * width : (c + 1) * width], in_scr[c], 1, 1) for c in range(blocks))
    back = cot.astype(F32) + _norm_back(back, hat, scale)
    back_ref[...] = back
    branch = back.astype(BF16)
    branch_ref[...] = branch
    grads = _dot(branch, attn_scr[...], 1, 1).astype(BF16)
    grad0[...] = grads[:, :span]
    grad1[...] = grads[:, span : 2 * span]
    grad2[0] = grads[:, 2 * span : 3 * span]
    grad2[1] = grads[:, 3 * span :]


def feed(here, x, cot, own, near, far, diag, packed, share, hidden_size, block=256):
    rows, width = x.shape
    span = own.shape[2]
    group = width // span
    blocks = 2 * hidden_size // width
    lead = lambda: pl.BlockSpec((1, block, span), lambda i, *_: (0, i, 0))
    widths = (width, width, hidden_size, 2 * hidden_size, width)
    return pl.pallas_call(
        functools.partial(feed_kernel, share, group),
        grid_spec=pltpu.PrefetchScalarGridSpec(
            num_scalar_prefetch=1,
            grid=(rows // block,),
            in_specs=[_row(block, width), _row(block, width), lead(), lead(), lead(), lead(), _whole(packed)],
            out_specs=[pl.BlockSpec((1, block, width), lambda i, *_: (0, i, 0)), _row(block, width), _row(block, span), _row(block, span), pl.BlockSpec((2, block, span), lambda i, *_: (0, i, 0))]
            + [_row(block, n) for n in widths],
            scratch_shapes=[pltpu.VMEM((width, width), BF16), pltpu.VMEM((blocks, width, width), BF16), pltpu.VMEM((hidden_size, width), BF16)],
        ),
        out_shape=[_shape((1, rows, width)), _shape((rows, width), F32), _shape((rows, span)), _shape((rows, span)), _shape((2, rows, span))]
        + [_shape((rows, n)) for n in widths],
        compiler_params=_params(),
        cost_estimate=_cost(4 * rows * width * (width + 3 * hidden_size), 20 << 20, 2 * rows * hidden_size),
        name="feed",
    )(here, x, cot, own, near, far, diag, packed)


def feed_grads_kernel(owners, share, hidden_share, group, here, ctx_ref, branch_ref, n2_ref, gates_ref, hidden_ref, cot_ref, kept_ref, sent_ref, attn_scr):
    width = branch_ref.shape[1]
    span = width // group
    half = kept_ref.shape[1]
    core = here[0] & 1

    def place(value, start, size):
        value = value.reshape(owners, size, width).astype(BF16)
        for side in range(2):
            lo, hi = max(start, side * half), min(start + size, (side + 1) * half)
            if lo < hi:
                part = value[:, lo - start : hi - start]
                at = slice(lo - side * half, hi - side * half)

                @pl.when(core == side)
                def _(part=part, at=at):
                    kept_ref[:, at] = part

                @pl.when(core != side)
                def _(part=part, at=at):
                    sent_ref[:, at] = part

    total = share * (1 + gates_ref.shape[1] // width) + hidden_share
    attn = _dot(ctx_ref[...], branch_ref[...], 0, 0)
    for g in range(group):
        spot = here[0] ^ g
        attn_scr[pl.ds(pl.multiple_of(spot * span, span), span)] = attn[g * span : (g + 1) * span]
    place(attn_scr[...], 0, share)
    n2 = n2_ref[...]
    for c in range(gates_ref.shape[1] // width):
        place(_dot(n2, gates_ref[:, c * width : (c + 1) * width], 0, 0), share * (1 + c), share)
    place(_dot(hidden_ref[...], cot_ref[...], 0, 0), total - hidden_share, hidden_share)
    if total < 2 * half:
        place(jnp.zeros((owners * (2 * half - total), width), F32), total, 2 * half - total)


def feed_grads(here, ctx, branch, n2, gates, hidden, cot, owners, half):
    width = branch.shape[1]
    arrays = (ctx, branch, n2, gates, hidden, cot)
    return pl.pallas_call(
        functools.partial(feed_grads_kernel, owners, width // owners, hidden.shape[1] // owners, 4),
        grid_spec=pltpu.PrefetchScalarGridSpec(
            num_scalar_prefetch=1,
            grid=(1,),
            in_specs=[_whole(a) for a in arrays],
            out_specs=[_whole(_shape((owners, half, width)))] * 2,
            scratch_shapes=[pltpu.VMEM((width, width), F32)],
        ),
        out_shape=[_shape((owners, half, width))] * 2,
        compiler_params=_params(),
        cost_estimate=_cost(2 * branch.shape[0] * width * (width + 3 * hidden.shape[1]), 12 << 20),
        name="feed_grads",
    )(here, *arrays)


def qkv_grads_kernel(heads, tokens, dq0, dq1, dk0, dk1, dv0, dv1, cos_ref, sin_ref, normed_ref, *refs):
    grads_ref, grad_ref, acc = refs[tokens:]
    step = pl.program_id(0)

    @pl.when(step == 0)
    def _():
        acc[...] = jnp.zeros_like(acc)

    cos = jnp.concatenate([cos_ref[...]] * heads, axis=1)
    sin = jnp.concatenate([sin_ref[...]] * heads, axis=1)
    dq = jnp.where(step < pl.num_programs(0) // 2, dq0[...].astype(F32), dq1[...].astype(F32))
    dk = dk0[...].astype(F32) + dk1[...].astype(F32)
    qk = jnp.concatenate([dq, dk], axis=1)
    qk = (qk * cos - _half_turn(qk) * sin).astype(BF16)
    dv = (dv0[...].astype(F32) + dv1[...].astype(F32)).astype(BF16)
    grads = jnp.concatenate([qk, dv], axis=1)
    grads_ref[...] = grads
    acc[...] += _dot(normed_ref[...], grads, 0, 0)

    @pl.when(step == pl.num_programs(0) - 1)
    def _():
        grad_ref[...] = acc[...].astype(BF16)


def qkv_grads(dqs, dks, dvs, cos, sin, normed, heads, block, tokens=()):
    length, width = normed.shape
    span = heads * HEAD
    grad = _shape((width, 3 * span))
    halves = length // block // 2
    return pl.pallas_call(
        functools.partial(qkv_grads_kernel, heads, len(tokens)),
        grid=(2 * halves,),
        in_specs=[
            pl.BlockSpec((block, span), lambda i: (jnp.minimum(i, halves - 1), 0)),
            pl.BlockSpec((block, span), lambda i: (jnp.maximum(i - halves, 0), 0)),
        ]
        + [_row(block, span)] * 4
        + [_row(block, cos.shape[1])] * 2
        + [_row(block, width)]
        + _unread(tokens),
        out_specs=[_row(block, 3 * span), _whole(grad)],
        out_shape=[_shape((length, 3 * span)), grad],
        scratch_shapes=[pltpu.VMEM(grad.shape, F32)],
        compiler_params=_params(),
        cost_estimate=_cost(2 * length * width * 3 * span, 8 << 20),
        name="qkv_grads",
    )(*dqs, *dks, *dvs, cos, sin, normed, *tokens)


def input_back_kernel(grads_ref, w_ref, *refs):
    kept_ref, sent_ref = refs[-2:]
    back = _dot(grads_ref[...], w_ref[...], 1, 1).astype(BF16)

    @pl.when(pl.program_id(0) % 2 == 0)
    def _():
        kept_ref[0] = back

    @pl.when(pl.program_id(0) % 2 == 1)
    def _():
        sent_ref[0] = back


def input_back(grads, w, block, tokens=()):
    length, columns = grads.shape
    width = w.shape[0]
    spec = pl.BlockSpec((1, block, width), lambda i: (i // 2, 0, 0))
    return pl.pallas_call(
        input_back_kernel,
        grid=(length // block,),
        in_specs=[_row(block, columns), _whole(w)] + _unread(tokens),
        out_specs=[spec, spec],
        out_shape=[_shape((length // block // 2, block, width))] * 2,
        compiler_params=_params(),
        cost_estimate=_cost(2 * length * width * columns, 6 << 20),
        name="input_back",
    )(grads, w, *tokens)


def exchange(value, axis, distance):
    size = lax.axis_size(axis)
    return lax.ppermute(value, axis, [(i, i ^ distance) for i in range(size)])


def gather_halves(piece, axis):
    size = lax.axis_size(axis)
    pieces, order = piece[None], [0]
    distance = size // 2
    while distance > 1:
        pieces = jnp.concatenate([pieces, exchange(pieces, axis, distance)], axis=0)
        order = order + [place ^ distance for place in order]
        distance //= 2
    other = exchange(pieces, axis, 1)
    order = order + [place ^ 1 for place in order]
    where = jnp.asarray([order.index(place) for place in range(size)], jnp.int32)
    return pieces, other, where[lax.axis_index(axis) ^ jnp.arange(size)]


def halve(addends, axis, bit, take):
    own = (lax.axis_index(axis) >> bit) & 1
    sent = sum(take(a, 1 - own).astype(F32) for a in addends).astype(BF16)
    return [take(a, own) for a in addends] + [exchange(sent, axis, 1 << bit)]


def split_owners(addends, axis):
    bits = lax.axis_size(axis).bit_length() - 1
    return [a.reshape((2,) * bits + a.shape[1:]) for a in addends]


def halve_owners(addends, axis, bit):
    dim = lax.axis_size(axis).bit_length() - 2 - bit
    return halve(addends, axis, bit, lambda a, at: lax.dynamic_index_in_dim(a, at, dim, keepdims=False))


def scatter_rows(addends, axis, first=0):
    for bit in range(first, lax.axis_size(axis).bit_length() - 1):
        addends = halve_owners(addends, axis, bit)
    return addends


def total(addends):
    return sum(a.astype(F32) for a in addends)


ROPE_BASE = 160000.0


def rope_tables(places):
    half = HEAD // 2
    inverse = ROPE_BASE ** (-(jnp.arange(half, dtype=F32) * 2.0 / HEAD))
    angles = places[:, None] * inverse[None, :]
    cosine, sine = lax.optimization_barrier((jnp.cos(angles), jnp.sin(angles)))
    return (
        jnp.concatenate([cosine] * 4, axis=1),
        jnp.concatenate([-sine, sine] * 2, axis=1),
    )


def from_slices(block):
    far = exchange(block, "seq", 2)
    return [block, exchange(block, "seq", 1), far, exchange(far, "seq", 1)]


def in_order(blocks, here):
    stacked = jnp.stack(blocks)
    return [lax.dynamic_index_in_dim(stacked, here ^ i, 0, keepdims=False) for i in range(len(blocks))]


def up16(n):
    return -(-n // 16) * 16


def body(
    inputs,
    norm_one,
    qkv_weight,
    attn_out_weight,
    norm_two,
    mlp_in_weight,
    mlp_out_weight,
    cotangent,
):
    here = lax.axis_index("seq")
    slices = lax.axis_size("seq")
    owners = lax.axis_size("fsdp")
    heads = HEADS // slices
    span = heads * HEAD
    rows, width = inputs.shape[1:]
    share = qkv_weight.shape[0]
    hidden_share = mlp_out_weight.shape[0]
    hidden_size = hidden_share * owners
    blocks = 2 * hidden_size // width
    aligned = share % 16 == 0 and hidden_share % 16 == 0
    spot = jnp.reshape(here, (1,)).astype(jnp.int32)

    x = inputs[0]
    scaled_qkv = (qkv_weight.astype(F32) * norm_one.astype(F32)[:, None]).astype(BF16)
    scaled_in = (mlp_in_weight.astype(F32) * norm_two.astype(F32)[:, None]).astype(BF16)
    x_far = exchange(x, "seq", 2)
    own_columns = jnp.concatenate(
        [lax.dynamic_slice_in_dim(scaled_qkv, c * width + here * span, span, 1) for c in range(3)], axis=1
    )
    even, odd, spots = gather_halves(own_columns, "fsdp")
    xs = [x, exchange(x, "seq", 1), x_far, exchange(x_far, "seq", 1)]
    if not aligned:
        pieces = jnp.concatenate([even, odd], axis=0)
        even = jnp.take(pieces, spots, axis=0).reshape(1, width, 3 * span)
        odd, spots = even, jnp.zeros((1,), jnp.int32)

    shard = [attn_out_weight] + [scaled_in[:, c * width : (c + 1) * width] for c in range(blocks)] + [mlp_out_weight]
    shard_rows = share * (1 + blocks) + hidden_share
    part = up16(-(-shard_rows // slices))
    shard = jnp.concatenate(shard + [jnp.zeros((part * slices - shard_rows, width), BF16)], axis=0)
    packed = lax.all_gather(lax.dynamic_slice_in_dim(shard, here * part, part, 0), ("fsdp", "seq"), axis=0, tiled=True)
    packed = packed.reshape(owners, part * slices, width)
    packed_share = share
    if not aligned:
        cuts = [share * c for c in range(2 + blocks)] + [shard_rows]
        packed = jnp.concatenate([packed[:, a:b].reshape(-1, width) for a, b in zip(cuts, cuts[1:])], axis=0)[None]
        packed_share = width

    order = here ^ jnp.arange(slices)
    places = (order[:, None] * rows + jnp.arange(rows)[None, :]).reshape(-1).astype(F32)
    cosine, sine = rope_tables(places)

    w_qkv, normed_all, query, key, value = project(spots, xs, even, odd, cosine, sine, heads)
    context_far, out_far, query_far = attend_forward(query, key, value, heads, rows, 2, 2)
    context_far = exchange(context_far, "seq", 2)
    context_near, out_near, query_near = attend_forward(query, key, value, heads, rows, 0, 2)
    context_1 = exchange(context_near[1:], "seq", 1)
    context_3 = exchange(context_far[1:], "seq", 1)

    cot = cotangent[0]
    result, attended_grad, grad0, grad1, grad23, context_low, normed_two, hidden, gates, branch = feed(
        spot, x, cot, context_near, context_1, context_far, context_3, packed, packed_share, hidden_size
    )
    grad23 = exchange(grad23, "seq", 2)
    grad1 = exchange(grad1, "seq", 1)
    grad3 = exchange(grad23[1], "seq", 1)

    grad_rows = up16(-(-shard_rows // 2))
    packed_owners = owners if aligned else 1
    if aligned:
        kept, sent = feed_grads(spot, context_low, branch, normed_two, gates, hidden, cot, owners, grad_rows)
    else:
        whole_rows = width * (1 + blocks) + hidden_size
        kept, sent = feed_grads(spot, context_low, branch, normed_two, gates, hidden, cot, 1, whole_rows // 2)
        core = here & 1
        both = jnp.where(core == 0, jnp.concatenate([kept, sent], axis=1), jnp.concatenate([sent, kept], axis=1))[0]
        cuts = [width * c for c in range(2 + blocks)] + [whole_rows]
        both = jnp.concatenate([both[a:b].reshape(owners, -1, width) for a, b in zip(cuts, cuts[1:])], axis=1)
        both = jnp.pad(both, ((0, 0), (0, 2 * grad_rows - shard_rows), (0, 0)))
        kept = lax.dynamic_slice_in_dim(both, core * grad_rows, grad_rows, 1)
        sent = lax.dynamic_slice_in_dim(both, (1 - core) * grad_rows, grad_rows, 1)
    mlp_grads = [kept, exchange(sent, "seq", 1)]
    cut = up16(grad_rows // 2)
    columns = lambda a, at: lax.dynamic_slice_in_dim(a, at * (width // 2), width // 2, a.ndim - 1)
    one, two = [a[:, :cut] for a in mlp_grads], split_owners([a[:, cut:] for a in mlp_grads], "fsdp")

    dq_near, dk_near, dv_near = attend_backward(query_near, key, value, grad0, grad1, out_near, heads)
    one = split_owners(halve(one, "seq", 1, columns), "fsdp")
    two = halve_owners(two, "fsdp", 0)
    dq_far, dk_far, dv_far = attend_backward(
        query_far, key, value, grad23[0], grad3, out_far, heads, tokens=(mlp_grads[-1],)
    )
    tokens = (one[-1], two[-1])
    one = halve_owners(one, "fsdp", 0)
    two = halve_owners(two, "fsdp", 1)
    qkv_back, qkv_grad = qkv_grads(
        (dq_near, dq_far), (dk_near, dk_far), (dv_near, dv_far), cosine, sine, normed_all, heads, rows, tokens=tokens
    )
    tokens = (one[-1], two[-1])
    qkv_part = split_owners([qkv_grad.reshape(owners, share, 3 * span)], "fsdp")
    qkv_part = total(scatter_rows(qkv_part, "fsdp")).astype(BF16)
    one = scatter_rows(one, "fsdp", 1)
    two = halve(scatter_rows(two, "fsdp", 2), "seq", 1, columns)
    mlp_part = jnp.concatenate([total(one), total(two)], axis=0).astype(BF16)

    back_kept, back_sent = input_back(qkv_back, w_qkv, rows, tokens=tokens)
    back_near = exchange(back_sent, "seq", 1)
    back_far = exchange((back_kept[1].astype(F32) + back_near[1].astype(F32)).astype(BF16), "seq", 2)
    normed_hat, scale_inv = _normalize(x.astype(F32))
    input_grad = attended_grad + _norm_back(total([back_kept[0], back_near[0], back_far]), normed_hat, scale_inv)

    qkv_blocks = in_order(from_slices(qkv_part), here)
    qkv_sum = jnp.concatenate(
        [b[:, c * span : (c + 1) * span] for c in range(3) for b in qkv_blocks], axis=1
    ).astype(F32)

    mlp_blocks = in_order(from_slices(mlp_part), here)
    mlp_sum = jnp.concatenate(
        [jnp.concatenate([mlp_blocks[core], mlp_blocks[2 + core]], axis=1) for core in range(2)], axis=0
    ).astype(F32)
    in_sum = jnp.concatenate([mlp_sum[share * (1 + c) : share * (2 + c)] for c in range(blocks)], axis=1)
    first_out = share * (1 + blocks)
    return (
        result,
        input_grad.astype(BF16)[None],
        jnp.sum(qkv_weight.astype(F32) * qkv_sum, axis=1),
        qkv_sum * norm_one.astype(F32)[:, None],
        mlp_sum[:share],
        jnp.sum(mlp_in_weight.astype(F32) * in_sum, axis=1),
        in_sum * norm_two.astype(F32)[:, None],
        mlp_sum[first_out : first_out + hidden_share],
    )


def solution(mesh):
    tokens = P("fsdp", "seq", None)
    vector = P("fsdp")
    matrix = P("fsdp", None)
    return jax.shard_map(
        body,
        mesh=mesh,
        in_specs=(tokens, vector, matrix, matrix, vector, matrix, matrix, tokens),
        out_specs=(tokens, tokens, vector, matrix, matrix, vector, matrix, matrix),
        check_vma=False,
    )
```

```python
import functools
import jax, jax.numpy as jnp
from jax import lax
from jax.experimental import pallas as pl
from jax.experimental.pallas import tpu as pltpu

from jax.sharding import PartitionSpec as P

HEADS = 12
HEAD = 64
PAD = 128
EPSILON = 1e-05
MIB = 1 << 20
LOG2E = 1.4426950408889634
F32 = jnp.float32
BF16 = jnp.bfloat16


def _dot(a, b, ca, cb):
    return lax.dot_general(a, b, (((ca,), (cb,)), ((), ())), preferred_element_type=F32)


def _normalize(values):
    centred = values - jnp.mean(values, axis=1, keepdims=True)
    variance = jnp.mean(centred * centred, axis=1, keepdims=True)
    scale_inv = lax.rsqrt(variance + EPSILON)
    return centred * scale_inv, scale_inv


def _norm_back(grad_hat, normed, scale_inv):
    return scale_inv * (
        grad_hat
        - jnp.mean(grad_hat, axis=1, keepdims=True)
        - normed * jnp.mean(grad_hat * normed, axis=1, keepdims=True)
    )


def _half_turn(v):
    lane = lax.broadcasted_iota(jnp.int32, v.shape, 1)
    ahead = pltpu.roll(v, v.shape[1] - HEAD // 2, 1)
    behind = pltpu.roll(v, HEAD // 2, 1)
    return jnp.where(lane % HEAD < HEAD // 2, ahead, behind)


def _parts(v):
    high = v.astype(BF16)
    rest = v - high.astype(F32)
    mid = rest.astype(BF16)
    low = (rest - mid.astype(F32)).astype(BF16)
    return high, mid, low


def _with_parts(base, v):
    rows = base.shape[0]
    high, mid, low = _parts(v)
    lane = lax.broadcasted_iota(jnp.int32, (rows, PAD - HEAD), 1)
    f = lambda p: p.astype(F32)
    tail = jnp.where(lane == 0, f(high), jnp.where(lane == 1, f(mid), jnp.where(lane == 2, f(low), 0.0)))
    return jnp.concatenate([base[:, :HEAD], tail.astype(BF16)], axis=1)


def _params(mib):
    return pltpu.CompilerParams(vmem_limit_bytes=mib * MIB)


def _row(block, n, first=0):
    return pl.BlockSpec((block, n), lambda i, *_: (i + first, 0))


def _whole(a):
    rank = len(a.shape)
    return pl.BlockSpec(a.shape, lambda i, *_: (0,) * rank)


def _unread(tokens):
    return [pl.BlockSpec(memory_space=pl.ANY) for _ in tokens]


def _shape(shape, dtype=BF16):
    return jax.ShapeDtypeStruct(shape, dtype)


def _cost(flops, size, transcendentals=0):
    return pl.CostEstimate(flops=int(flops), bytes_accessed=int(size), transcendentals=int(transcendentals))


def project_kernel(heads, spots, x0, x1, x2, x3, even_ref, odd_ref, cos_ref, sin_ref, w_ref, normed_ref, q_ref, k_ref, v_ref, x_scr):
    step = pl.program_id(0)
    owners = w_ref.shape[0] // even_ref.shape[1]
    share = even_ref.shape[1]

    @pl.when(step == 0)
    def _():
        for i in range(owners):
            at = slice(i * share, (i + 1) * share)
            spot = spots[i]
            if owners == 1:
                w_ref[at] = even_ref[0]
            else:
                half = owners // 2

                @pl.when(spot < half)
                def _():
                    w_ref[at] = even_ref[spot]

                @pl.when(spot >= half)
                def _():
                    w_ref[at] = odd_ref[spot - half]

    for j, ref in enumerate((x0, x1, x2, x3)):

        @pl.when(step == j)
        def _(ref=ref):
            x_scr[...] = ref[...]

    normed = _normalize(x_scr[...].astype(F32))[0].astype(BF16)
    normed_ref[...] = normed
    qkv = _dot(normed, w_ref[...], 1, 0)
    span = heads * HEAD
    qk = qkv[:, : 2 * span]
    cos = jnp.concatenate([cos_ref[...]] * heads, axis=1)
    sin = jnp.concatenate([sin_ref[...]] * heads, axis=1)
    qk = qk * cos + _half_turn(qk) * sin
    rows = x0.shape[0]
    zeros = jnp.zeros((rows, PAD - HEAD), BF16)
    ones = jnp.where(lax.broadcasted_iota(jnp.int32, (rows, PAD - HEAD), 1) < 3, 1.0, 0.0).astype(BF16)
    for h in range(heads):
        at = slice(h * PAD, (h + 1) * PAD)
        lo = h * HEAD
        q_ref[:, at] = jnp.concatenate([(qk[:, lo : lo + HEAD] * (LOG2E * HEAD ** -0.5)).astype(BF16), zeros], axis=1)
        k_ref[:, at] = jnp.concatenate([qk[:, span + lo : span + lo + HEAD].astype(BF16), ones], axis=1)
        v_ref[:, at] = jnp.concatenate([qkv[:, 2 * span + lo : 2 * span + lo + HEAD].astype(BF16), ones], axis=1)


def project(spots, xs, even, odd, cos, sin, heads):
    rows, width = xs[0].shape
    length = rows * len(xs)
    columns = even.shape[2]
    w_shape = _shape((width, columns))
    return pl.pallas_call(
        functools.partial(project_kernel, heads),
        grid_spec=pltpu.PrefetchScalarGridSpec(
            num_scalar_prefetch=1,
            grid=(len(xs),),
            in_specs=[_whole(x) for x in xs] + [_whole(even), _whole(odd), _row(rows, cos.shape[1]), _row(rows, sin.shape[1])],
            out_specs=[_whole(w_shape), _row(rows, width)] + [_row(rows, heads * PAD)] * 3,
            scratch_shapes=[pltpu.VMEM((rows, width), BF16)],
        ),
        out_shape=[w_shape, _shape((length, width))] + [_shape((length, heads * PAD))] * 3,
        compiler_params=_params(28),
        cost_estimate=_cost(2 * length * width * columns, 12 << 20),
        name="project",
    )(spots, *xs, even, odd, cos, sin)


def forward_kernel(heads, sub, q_ref, k_ref, v_ref, ctx0_ref, ctx1_ref, out_ref, qx_ref):
    step = pl.program_id(0)
    for r in range(q_ref.shape[0] // sub):
        part = slice(r * sub, (r + 1) * sub)
        outs = []
        for h in range(heads):
            at = slice(h * PAD, (h + 1) * PAD)
            q = q_ref[part, at]
            scores = _dot(q, k_ref[:, at], 1, 1)
            top = jnp.max(scores, axis=1, keepdims=True)
            weights = jnp.exp2(scores - top).astype(BF16)
            sums = _dot(weights, v_ref[:, at], 1, 0)
            total = sums[:, HEAD : HEAD + 1]
            outs.append(sums[:, :HEAD] / total)
            qx_ref[part, at] = _with_parts(q, -(top + jnp.log2(total)))
        out = jnp.concatenate(outs, axis=1)
        out_ref[part] = out

        @pl.when(step == 0)
        def _(part=part, out=out):
            ctx0_ref[part] = out.astype(BF16)

        @pl.when(step == 1)
        def _(part=part, out=out):
            ctx1_ref[part] = out.astype(BF16)


def attend_forward(q, k, v, heads, block, first):
    length = k.shape[0]
    span = heads * HEAD
    ctx = _shape((block, span))
    return pl.pallas_call(
        functools.partial(forward_kernel, heads, min(256, block)),
        grid=(2,),
        in_specs=[_row(block, heads * PAD, first), _whole(k), _whole(v)],
        out_specs=[_whole(ctx), _whole(ctx), _row(block, span), _row(block, heads * PAD)],
        out_shape=[ctx, ctx, _shape((2 * block, span), F32), _shape((2 * block, heads * PAD))],
        compiler_params=_params(28),
        cost_estimate=_cost(16 * heads * 2 * block * length * HEAD, 6 << 20, heads * 2 * block * length),
        name="attend_forward",
    )(q, k, v)


def backward_kernel(heads, sub, count, k_ref, v_ref, *refs):
    items = [refs[3 * i : 3 * i + 3] for i in range(count)]
    dq_refs, (dk_ref, dv_ref, dk_acc, dv_acc) = refs[-4 - count : -4], refs[-4:]
    fresh = True
    for (q_ref, do_ref, out_ref), dq_ref in zip(items, dq_refs):
        do_all = do_ref[...]
        prod = do_all.astype(F32) * out_ref[...]
        for r in range(q_ref.shape[0] // sub):
            part = slice(r * sub, (r + 1) * sub)
            dqs = []
            for h in range(heads):
                at = slice(h * PAD, (h + 1) * PAD)
                lo = h * HEAD
                q, k, v = q_ref[part, at], k_ref[:, at], v_ref[:, at]
                delta = jnp.sum(prod[part, lo : lo + HEAD], axis=1, keepdims=True)
                do = _with_parts(do_all[part, lo : lo + HEAD], -delta)
                probs = jnp.exp2(_dot(q, k, 1, 1))
                back = _dot(do, v, 1, 1)
                score_back = (probs * back).astype(BF16)
                dv = _dot(do, probs.astype(BF16), 0, 0)
                dk = _dot(q, score_back, 0, 0)
                dv_acc[at] = dv if fresh else dv_acc[at] + dv
                dk_acc[at] = dk if fresh else dk_acc[at] + dk
                dqs.append(_dot(score_back, k, 1, 0)[:, :HEAD])
            dq_ref[part] = (jnp.concatenate(dqs, axis=1) * HEAD ** -0.5).astype(BF16)
            fresh = False
    pick = lambda acc, scale: jnp.concatenate(
        [(acc[h * PAD : h * PAD + HEAD] * scale).T for h in range(heads)], axis=1
    ).astype(BF16)
    dk_ref[...] = pick(dk_acc, 1 / LOG2E)
    dv_ref[...] = pick(dv_acc, 1.0)


def attend_backward(k, v, items, heads, tokens=()):
    length = k.shape[0]
    block, span = items[0][3].shape
    whole, rows = _shape((length, span)), _shape((block, span))
    specs, operands = [], []
    for q, out, first, do in items:
        specs += [_row(block, heads * PAD, first), _whole(do), _row(block, span, first)]
        operands += [q, do, out]
    count = len(items)
    return pl.pallas_call(
        functools.partial(backward_kernel, heads, min(256, block), count),
        grid=(1,),
        in_specs=[_whole(k), _whole(v)] + specs + _unread(tokens),
        out_specs=[_whole(rows)] * count + [_whole(whole)] * 2,
        out_shape=[rows] * count + [whole] * 2,
        scratch_shapes=[pltpu.VMEM((heads * PAD, length), F32)] * 2,
        compiler_params=_params(40),
        cost_estimate=_cost(40 * heads * count * block * length * HEAD, 8 << 20, heads * count * block * length),
        name="attend_backward",
    )(k, v, *operands, *tokens)


def _gelu(first):
    cumulative = 0.5 * (1.0 + lax.erf(first * 0.5 ** 0.5))
    density = jnp.exp(-0.5 * first * first) * 0.3989422804014327
    return first * cumulative, cumulative + first * density


def feed_kernel(share, group, here, x_ref, cot_ref, own_ref, near_ref, far_ref, diag_ref, w_ref, result_ref, back_ref, grad0, grad1, grad2, ctx_ref, n2_ref, hidden_ref, gates_ref, branch_ref, attn_scr, in_scr, out_scr):
    width = x_ref.shape[1]
    hidden_size = out_scr.shape[0]
    owners = w_ref.shape[0]
    span = width // group
    blocks = in_scr.shape[0]

    @pl.when(pl.program_id(0) == 0)
    def _():
        pick = lambda lo, hi: w_ref[:, lo:hi].reshape(owners * (hi - lo), width)
        attn = pick(0, share)
        for g in range(group):
            spot = here[0] ^ g
            attn_scr[pl.ds(pl.multiple_of(spot * span, span), span)] = attn[g * span : (g + 1) * span]
        for c in range(blocks):
            in_scr[c] = pick(share * (1 + c), share * (2 + c))
        out_scr[...] = pick(share * (1 + blocks), share * (1 + blocks) + hidden_size // owners)

    ctx = jnp.concatenate([own_ref[...], near_ref[...], far_ref[0], diag_ref[...]], axis=1)
    ctx_ref[...] = ctx
    attended = x_ref[...].astype(F32) + _dot(ctx, attn_scr[...], 1, 0)
    hat, scale = _normalize(attended)
    n2 = hat.astype(BF16)
    n2_ref[...] = n2
    gate_up = jnp.concatenate([_dot(n2, in_scr[c], 1, 0) for c in range(blocks)], axis=1)
    first, second = gate_up[:, :hidden_size], gate_up[:, hidden_size:]
    gelu, slope = _gelu(first)
    hidden = (gelu * second).astype(BF16)
    hidden_ref[...] = hidden
    result_ref[0] = (attended + _dot(hidden, out_scr[...], 1, 0)).astype(BF16)
    cot = cot_ref[...]
    hidden_back = _dot(cot, out_scr[...], 1, 1)
    gates = jnp.concatenate([hidden_back * second * slope, hidden_back * gelu], axis=1).astype(BF16)
    gates_ref[...] = gates
    back = sum(_dot(gates[:, c * width : (c + 1) * width], in_scr[c], 1, 1) for c in range(blocks))
    back = cot.astype(F32) + _norm_back(back, hat, scale)
    back_ref[...] = back
    branch = back.astype(BF16)
    branch_ref[...] = branch
    grads = _dot(branch, attn_scr[...], 1, 1).astype(BF16)
    grad0[...] = grads[:, :span]
    grad1[...] = grads[:, span : 2 * span]
    grad2[0] = grads[:, 2 * span : 3 * span]
    grad2[1] = grads[:, 3 * span :]


def feed(here, x, cot, own, near, far, diag, packed, share, hidden_size, block=256):
    rows, width = x.shape
    span = own.shape[1]
    group = width // span
    blocks = 2 * hidden_size // width
    lead = lambda: pl.BlockSpec((1, block, span), lambda i, *_: (0, i, 0))
    widths = (width, width, hidden_size, 2 * hidden_size, width)
    return pl.pallas_call(
        functools.partial(feed_kernel, share, group),
        grid_spec=pltpu.PrefetchScalarGridSpec(
            num_scalar_prefetch=1,
            grid=(rows // block,),
            in_specs=[_row(block, width), _row(block, width), _row(block, span), _row(block, span), lead(), _row(block, span), _whole(packed)],
            out_specs=[pl.BlockSpec((1, block, width), lambda i, *_: (0, i, 0)), _row(block, width), _row(block, span), _row(block, span), pl.BlockSpec((2, block, span), lambda i, *_: (0, i, 0))]
            + [_row(block, n) for n in widths],
            scratch_shapes=[pltpu.VMEM((width, width), BF16), pltpu.VMEM((blocks, width, width), BF16), pltpu.VMEM((hidden_size, width), BF16)],
        ),
        out_shape=[_shape((1, rows, width)), _shape((rows, width), F32), _shape((rows, span)), _shape((rows, span)), _shape((2, rows, span))]
        + [_shape((rows, n)) for n in widths],
        compiler_params=_params(50),
        cost_estimate=_cost(4 * rows * width * (width + 3 * hidden_size), 20 << 20, 2 * rows * hidden_size),
        name="feed",
    )(here, x, cot, own, near, far, diag, packed)


def feed_grads_kernel(owners, share, hidden_share, group, here, ctx_ref, branch_ref, n2_ref, gates_ref, hidden_ref, cot_ref, *refs):
    kept, sent, attn_scr = refs[:2], refs[2:4], refs[4]
    width = branch_ref.shape[1]
    span = width // group
    cut = kept[0].shape[1]
    half = cut + kept[1].shape[1]
    core = here[0] & 1

    def place(value, start, size):
        value = value.reshape(owners, size, width).astype(BF16)
        for side in range(2):
            for g, (first, last) in enumerate(((0, cut), (cut, half))):
                first, last = side * half + first, side * half + last
                lo, hi = max(start, first), min(start + size, last)
                if lo < hi:
                    part = value[:, lo - start : hi - start]
                    at = slice(lo - first, hi - first)

                    @pl.when(core == side)
                    def _(part=part, at=at, g=g):
                        kept[g][:, at] = part

                    @pl.when(core != side)
                    def _(part=part, at=at, g=g):
                        sent[g][:, at] = part

    total = share * (1 + gates_ref.shape[1] // width) + hidden_share
    attn = _dot(ctx_ref[...], branch_ref[...], 0, 0)
    for g in range(group):
        spot = here[0] ^ g
        attn_scr[pl.ds(pl.multiple_of(spot * span, span), span)] = attn[g * span : (g + 1) * span]
    place(attn_scr[...], 0, share)
    n2 = n2_ref[...]
    for c in range(gates_ref.shape[1] // width):
        place(_dot(n2, gates_ref[:, c * width : (c + 1) * width], 0, 0), share * (1 + c), share)
    place(_dot(hidden_ref[...], cot_ref[...], 0, 0), total - hidden_share, hidden_share)
    if total < 2 * half:
        place(jnp.zeros((owners * (2 * half - total), width), F32), total, 2 * half - total)


def feed_grads(here, ctx, branch, n2, gates, hidden, cot, owners, half, cut):
    width = branch.shape[1]
    arrays = (ctx, branch, n2, gates, hidden, cot)
    outs = [_shape((owners, cut, width)), _shape((owners, half - cut, width))] * 2
    return pl.pallas_call(
        functools.partial(feed_grads_kernel, owners, width // owners, hidden.shape[1] // owners, 4),
        grid_spec=pltpu.PrefetchScalarGridSpec(
            num_scalar_prefetch=1,
            grid=(1,),
            in_specs=[_whole(a) for a in arrays],
            out_specs=[_whole(o) for o in outs],
            scratch_shapes=[pltpu.VMEM((width, width), F32)],
        ),
        out_shape=outs,
        compiler_params=_params(44),
        cost_estimate=_cost(2 * branch.shape[0] * width * (width + 3 * hidden.shape[1]), 12 << 20),
        name="feed_grads",
    )(here, *arrays)


def qkv_grads_kernel(heads, tokens, owner, *refs):
    dqs, dks, dvs = refs[:4], refs[4:7], refs[7:10]
    cos_ref, sin_ref, normed_ref = refs[10:13]
    refs = refs[13:]
    grads_ref, kept_ref, sent_ref, acc = refs[tokens:]
    step = pl.program_id(0)

    @pl.when(step == 0)
    def _():
        acc[...] = jnp.zeros_like(acc)

    cos = jnp.concatenate([cos_ref[...]] * heads, axis=1)
    sin = jnp.concatenate([sin_ref[...]] * heads, axis=1)
    dq = dqs[0][...].astype(F32)
    for j in range(1, 4):
        dq = jnp.where(step == j, dqs[j][...].astype(F32), dq)
    dk = sum(ref[...].astype(F32) for ref in dks)
    qk = jnp.concatenate([dq, dk], axis=1)
    qk = (qk * cos - _half_turn(qk) * sin).astype(BF16)
    dv = sum(ref[...].astype(F32) for ref in dvs).astype(BF16)
    grads = jnp.concatenate([qk, dv], axis=1)
    grads_ref[...] = grads
    acc[...] += _dot(normed_ref[...], grads, 0, 0)

    @pl.when(step == pl.num_programs(0) - 1)
    def _():
        pairs, share = kept_ref.shape[:2]
        for i in range(2 * pairs):
            part = acc[i * share : (i + 1) * share].astype(BF16)

            @pl.when((owner[0] & 1) == i % 2)
            def _(part=part, i=i):
                kept_ref[i // 2] = part

            @pl.when((owner[0] & 1) != i % 2)
            def _(part=part, i=i):
                sent_ref[i // 2] = part


def qkv_grads(owner, dqs, dks, dvs, cos, sin, normed, heads, block, owners, tokens=()):
    length, width = normed.shape
    span = heads * HEAD
    half = _shape((owners // 2, width // owners, 3 * span))
    return pl.pallas_call(
        functools.partial(qkv_grads_kernel, heads, len(tokens)),
        grid_spec=pltpu.PrefetchScalarGridSpec(
            num_scalar_prefetch=1,
            grid=(length // block,),
            in_specs=[_whole(dqs[0])] * 4
            + [_row(block, span)] * 6
            + [_row(block, cos.shape[1])] * 2
            + [_row(block, width)]
            + _unread(tokens),
            out_specs=[_row(block, 3 * span), _whole(half), _whole(half)],
            scratch_shapes=[pltpu.VMEM((width, 3 * span), F32)],
        ),
        out_shape=[_shape((length, 3 * span)), half, half],
        compiler_params=_params(28),
        cost_estimate=_cost(2 * length * width * 3 * span, 8 << 20),
        name="qkv_grads",
    )(owner, *dqs, *dks, *dvs, cos, sin, normed, *tokens)


def input_back_kernel(grads_ref, w_ref, *refs):
    kept_ref, sent_ref = refs[-2:]
    back = _dot(grads_ref[...], w_ref[...], 1, 1).astype(BF16)

    @pl.when(pl.program_id(0) % 2 == 0)
    def _():
        kept_ref[0] = back

    @pl.when(pl.program_id(0) % 2 == 1)
    def _():
        sent_ref[0] = back


def input_back(grads, w, block, tokens=()):
    length, columns = grads.shape
    width = w.shape[0]
    spec = pl.BlockSpec((1, block, width), lambda i: (i // 2, 0, 0))
    return pl.pallas_call(
        input_back_kernel,
        grid=(length // block,),
        in_specs=[_row(block, columns), _whole(w)] + _unread(tokens),
        out_specs=[spec, spec],
        out_shape=[_shape((length // block // 2, block, width))] * 2,
        compiler_params=_params(20),
        cost_estimate=_cost(2 * length * width * columns, 6 << 20),
        name="input_back",
    )(grads, w, *tokens)


def combine_kernel(count, *refs):
    refs[-1][...] = sum(ref[...].astype(F32) for ref in refs[:count]).astype(BF16)


def combine(addends, tokens=()):
    whole = pl.BlockSpec(memory_space=pltpu.VMEM)
    return pl.pallas_call(
        functools.partial(combine_kernel, len(addends)),
        in_specs=[whole] * len(addends) + _unread(tokens),
        out_specs=whole,
        out_shape=_shape(addends[0].shape),
        compiler_params=_params(16),
        name="combine",
    )(*addends, *tokens)


def _pick(here, blocks, group):
    value = blocks[0]
    for j in range(1, len(blocks)):
        value = jnp.where((here ^ group) == j, blocks[j], value)
    return value


def finish_qkv_kernel(here, b0, b1, b2, b3, weight_ref, gain_ref, grad_ref, gain_grad_ref):
    blocks = [b[...].astype(F32) for b in (b0, b1, b2, b3)]
    ordered = [_pick(here[0], blocks, g) for g in range(4)]
    span = b0.shape[1] // 3
    summed = jnp.concatenate([o[:, c * span : (c + 1) * span] for c in range(3) for o in ordered], axis=1)
    gain_grad_ref[...] = jnp.sum(weight_ref[...].astype(F32) * summed, axis=1, keepdims=True)
    grad_ref[...] = summed * gain_ref[...].astype(F32)


def finish_feed_kernel(here, b0, b1, b2, b3, weight_ref, gain_ref, attn_ref, in_ref, gain_grad_ref, out_ref):
    share, width = attn_ref.shape
    half = b0.shape[0]
    blocks = [b[...].astype(F32) for b in (b0, b1, b2, b3)]
    ordered = [_pick(here[0], blocks, g) for g in range(4)]
    rows = jnp.concatenate([jnp.concatenate([ordered[core], ordered[2 + core]], axis=1) for core in range(2)], axis=0)
    attn_ref[...] = rows[:share]
    count = in_ref.shape[1] // width
    summed = jnp.concatenate([rows[share * (1 + c) : share * (2 + c)] for c in range(count)], axis=1)
    gain_grad_ref[...] = jnp.sum(weight_ref[...].astype(F32) * summed, axis=1, keepdims=True)
    in_ref[...] = summed * gain_ref[...].astype(F32)
    first = share * (1 + count)
    out_ref[...] = rows[first : first + out_ref.shape[0]]


def finish(kernel, name, here, blocks, weight, gain, shapes):
    whole = pl.BlockSpec(memory_space=pltpu.VMEM)
    return pl.pallas_call(
        kernel,
        in_specs=[pl.BlockSpec(memory_space=pltpu.SMEM)] + [whole] * 6,
        out_specs=[whole] * len(shapes),
        out_shape=[_shape(s, F32) for s in shapes],
        compiler_params=_params(16),
        name=name,
    )(here, *blocks, weight, gain)


def input_grad_kernel(x_ref, direct_ref, kept_ref, near_ref, far_ref, out_ref):
    hat, scale = _normalize(x_ref[...].astype(F32))
    back = kept_ref[0].astype(F32) + near_ref[0].astype(F32) + far_ref[...].astype(F32)
    out_ref[0] = (direct_ref[...] + _norm_back(back, hat, scale)).astype(BF16)


def input_grad(x, direct, kept, near, far, block=256):
    rows, width = x.shape
    lead = pl.BlockSpec((1, block, width), lambda i: (0, i, 0))
    return pl.pallas_call(
        input_grad_kernel,
        grid=(rows // block,),
        in_specs=[_row(block, width), _row(block, width), lead, lead, _row(block, width)],
        out_specs=lead,
        out_shape=_shape((1, rows, width)),
        compiler_params=_params(16),
        name="input_grad",
    )(x, direct, kept, near, far)


def halve_pair_kernel(columns, own, a_ref, b_ref, *refs):
    kept_ref, sent_ref = refs[-2:]
    if columns:
        half = a_ref.shape[2] // 2
        for side in range(2):
            at = slice(side * half, (side + 1) * half)
            part = (a_ref[:, :, at].astype(F32) + b_ref[:, :, at].astype(F32)).astype(BF16)

            @pl.when(own[0] == side)
            def _(part=part):
                kept_ref[...] = part

            @pl.when(own[0] != side)
            def _(part=part):
                sent_ref[...] = part

    else:
        for i in range(kept_ref.shape[0]):
            for ref, side in ((kept_ref, own[0]), (sent_ref, 1 - own[0])):
                at = 2 * i + side
                ref[i] = (a_ref[at].astype(F32) + b_ref[at].astype(F32)).astype(BF16)


def halve_pair(own, a, b, columns=False, tokens=()):
    n, rows, width = a.shape
    half = _shape((n, rows, width // 2) if columns else (n // 2, rows, width))
    whole = pl.BlockSpec(memory_space=pltpu.VMEM)
    return pl.pallas_call(
        functools.partial(halve_pair_kernel, columns),
        in_specs=[pl.BlockSpec(memory_space=pltpu.SMEM), whole, whole] + _unread(tokens),
        out_specs=[whole, whole],
        out_shape=[half, half],
        compiler_params=_params(16),
        name="halve_pair",
    )(own, a, b, *tokens)


def exchange(value, axis, distance):
    size = lax.axis_size(axis)
    return lax.ppermute(value, axis, [(i, i ^ distance) for i in range(size)])


def gather_halves(piece, axis):
    size = lax.axis_size(axis)
    pieces, order = piece[None], [0]
    distance = size // 2
    while distance > 1:
        pieces = jnp.concatenate([pieces, exchange(pieces, axis, distance)], axis=0)
        order = order + [place ^ distance for place in order]
        distance //= 2
    other = exchange(pieces, axis, 1)
    order = order + [place ^ 1 for place in order]
    where = jnp.asarray([order.index(place) for place in range(size)], jnp.int32)
    return pieces, other, where[lax.axis_index(axis) ^ jnp.arange(size)]


def halve(addends, axis, bit, take):
    own = (lax.axis_index(axis) >> bit) & 1
    sent = sum(take(a, 1 - own).astype(F32) for a in addends).astype(BF16)
    return [take(a, own) for a in addends] + [exchange(sent, axis, 1 << bit)]


def split_owners(addends, axis):
    bits = lax.axis_size(axis).bit_length() - 1
    return [a.reshape((2,) * bits + a.shape[1:]) for a in addends]


def halve_owners(addends, axis, bit):
    dim = lax.axis_size(axis).bit_length() - 2 - bit
    return halve(addends, axis, bit, lambda a, at: lax.dynamic_index_in_dim(a, at, dim, keepdims=False))


def scatter_rows(addends, axis, first=0):
    for bit in range(first, lax.axis_size(axis).bit_length() - 1):
        addends = halve_owners(addends, axis, bit)
    return addends


def total(addends):
    return sum(a.astype(F32) for a in addends)


ROPE_BASE = 160000.0


def rope_tables(places):
    half = HEAD // 2
    inverse = ROPE_BASE ** (-(jnp.arange(half, dtype=F32) * 2.0 / HEAD))
    angles = places[:, None] * inverse[None, :]
    cosine, sine = lax.optimization_barrier((jnp.cos(angles), jnp.sin(angles)))
    return (
        jnp.concatenate([cosine] * 4, axis=1),
        jnp.concatenate([-sine, sine] * 2, axis=1),
    )


def from_slices(block):
    far = exchange(block, "seq", 2)
    return [block, exchange(block, "seq", 1), far, exchange(far, "seq", 1)]


def step(pair, axis, bit, columns=False, tokens=()):
    own = jnp.reshape((lax.axis_index(axis) >> bit) & 1, (1,)).astype(jnp.int32)
    kept, sent = halve_pair(own, *pair, columns, tokens)
    return [kept, exchange(sent, axis, 1 << bit)]


def in_order(blocks, here):
    stacked = jnp.stack(blocks)
    return [lax.dynamic_index_in_dim(stacked, here ^ i, 0, keepdims=False) for i in range(len(blocks))]


def up16(n):
    return -(-n // 16) * 16


def body(
    inputs,
    norm_one,
    qkv_weight,
    attn_out_weight,
    norm_two,
    mlp_in_weight,
    mlp_out_weight,
    cotangent,
):
    here = lax.axis_index("seq")
    slices = lax.axis_size("seq")
    owners = lax.axis_size("fsdp")
    heads = HEADS // slices
    span = heads * HEAD
    rows, width = inputs.shape[1:]
    share = qkv_weight.shape[0]
    hidden_share = mlp_out_weight.shape[0]
    hidden_size = hidden_share * owners
    blocks = 2 * hidden_size // width
    aligned = share % 16 == 0 and hidden_share % 16 == 0
    spot = jnp.reshape(here, (1,)).astype(jnp.int32)

    x = inputs[0]
    scaled_qkv = (qkv_weight.astype(F32) * norm_one.astype(F32)[:, None]).astype(BF16)
    scaled_in = (mlp_in_weight.astype(F32) * norm_two.astype(F32)[:, None]).astype(BF16)
    x_far = exchange(x, "seq", 2)
    own_columns = jnp.concatenate(
        [lax.dynamic_slice_in_dim(scaled_qkv, c * width + here * span, span, 1) for c in range(3)], axis=1
    )
    even, odd, spots = gather_halves(own_columns, "fsdp")
    xs = [x, exchange(x, "seq", 1), x_far, exchange(x_far, "seq", 1)]
    if not aligned:
        pieces = jnp.concatenate([even, odd], axis=0)
        even = jnp.take(pieces, spots, axis=0).reshape(1, width, 3 * span)
        odd, spots = even, jnp.zeros((1,), jnp.int32)

    shard = [attn_out_weight] + [scaled_in[:, c * width : (c + 1) * width] for c in range(blocks)] + [mlp_out_weight]
    shard_rows = share * (1 + blocks) + hidden_share
    part = -(-shard_rows // (8 * slices)) * 8
    shard = jnp.concatenate(shard + [jnp.zeros((part * slices - shard_rows, width), BF16)], axis=0)
    packed = lax.all_gather(lax.dynamic_slice_in_dim(shard, here * part, part, 0), ("fsdp", "seq"), axis=0, tiled=True)
    packed = packed.reshape(owners, part * slices, width)
    packed_share = share
    if not aligned:
        cuts = [share * c for c in range(2 + blocks)] + [shard_rows]
        packed = jnp.concatenate([packed[:, a:b].reshape(-1, width) for a, b in zip(cuts, cuts[1:])], axis=0)[None]
        packed_share = width

    order = here ^ jnp.arange(slices)
    places = (order[:, None] * rows + jnp.arange(rows)[None, :]).reshape(-1).astype(F32)
    cosine, sine = rope_tables(places)

    w_qkv, normed_all, query, key, value = project(spots, xs, even, odd, cosine, sine, heads)
    context_2, context_3, out_far, query_far = attend_forward(query, key, value, heads, rows, 2)
    context_far = exchange(jnp.stack([context_2, context_3]), "seq", 2)
    context_0, context_1, out_near, query_near = attend_forward(query, key, value, heads, rows, 0)
    context_1 = exchange(context_1, "seq", 1)
    context_3 = exchange(context_far[1], "seq", 1)

    cot = cotangent[0]
    result, attended_grad, grad0, grad1, grad23, context_low, normed_two, hidden, gates, branch = feed(
        spot, x, cot, context_0, context_1, context_far, context_3, packed, packed_share, hidden_size
    )
    grad23 = exchange(grad23, "seq", 2)
    grad1 = exchange(grad1, "seq", 1)
    grad3 = exchange(grad23[1], "seq", 1)

    grad_rows = up16(-(-shard_rows // 2))
    cut = up16(grad_rows // 2)
    if aligned:
        kept_one, kept_two, sent_one, sent_two = feed_grads(
            spot, context_low, branch, normed_two, gates, hidden, cot, owners, grad_rows, cut
        )
    else:
        whole_rows = width * (1 + blocks) + hidden_size
        grads = feed_grads(
            spot, context_low, branch, normed_two, gates, hidden, cot, 1, whole_rows // 2, whole_rows // 4
        )
        core = here & 1
        kept, sent = jnp.concatenate(grads[:2], axis=1), jnp.concatenate(grads[2:], axis=1)
        both = jnp.where(core == 0, jnp.concatenate([kept, sent], axis=1), jnp.concatenate([sent, kept], axis=1))[0]
        cuts = [width * c for c in range(2 + blocks)] + [whole_rows]
        both = jnp.concatenate([both[a:b].reshape(owners, -1, width) for a, b in zip(cuts, cuts[1:])], axis=1)
        both = jnp.pad(both, ((0, 0), (0, 2 * grad_rows - shard_rows), (0, 0)))
        kept = lax.dynamic_slice_in_dim(both, core * grad_rows, grad_rows, 1)
        sent = lax.dynamic_slice_in_dim(both, (1 - core) * grad_rows, grad_rows, 1)
        kept_one, kept_two, sent_one, sent_two = kept[:, :cut], kept[:, cut:], sent[:, :cut], sent[:, cut:]
    one = [kept_one, exchange(sent_one, "seq", 1)]
    two = [kept_two, exchange(sent_two, "seq", 1)]

    dq_0, *back_0 = attend_backward(key, value, [(query_near, out_near, 0, grad0)], heads)
    tokens = (one[1], two[1])
    one = step(one, "seq", 1, columns=True, tokens=(dq_0,))
    two = step(two, "fsdp", 0, tokens=(dq_0,))
    dq_1, dq_2, *back_12 = attend_backward(
        key, value, [(query_near, out_near, 1, grad1), (query_far, out_far, 0, grad23[0])], heads, tokens=tokens
    )
    tokens = (one[1], two[1])
    one = step(one, "fsdp", 0, tokens=(dq_1,))
    two = step(two, "fsdp", 1, tokens=(dq_1,))
    dq_3, *back_3 = attend_backward(key, value, [(query_far, out_far, 1, grad3)], heads, tokens=tokens)
    tokens = (one[1], two[1])
    one = step(one, "fsdp", 1, tokens=(dq_3,))
    two = step(two, "fsdp", 2, tokens=(dq_3,))
    owner = jnp.reshape(lax.axis_index("fsdp"), (1,)).astype(jnp.int32)
    qkv_back, qkv_kept, qkv_sent = qkv_grads(
        owner, (dq_0, dq_1, dq_2, dq_3), *zip(back_0, back_12, back_3), cosine, sine, normed_all, heads, rows,
        owners if aligned else 2, tokens=tokens
    )
    back_kept, back_sent = input_back(qkv_back, w_qkv, rows, tokens=(one[1], two[1]))
    bits = owners.bit_length() - 1
    if aligned:
        qkv = [qkv_kept, exchange(qkv_sent, "fsdp", 1)]
        for bit in range(1, bits):
            qkv = step(qkv, "fsdp", bit, tokens=(back_kept,) if bit == 1 else ())
        qkv = [a.reshape(share, 3 * span) for a in qkv]
    else:
        side = owner[0] & 1
        qkv = jnp.where(side == 0, jnp.concatenate([qkv_kept, qkv_sent]), jnp.concatenate([qkv_sent, qkv_kept]))
        qkv = scatter_rows(split_owners([qkv.reshape(owners, share, 3 * span)], "fsdp"), "fsdp")
    for bit in range(2, bits):
        one = step(one, "fsdp", bit)
    for bit in range(3, bits):
        two = step(two, "fsdp", bit)
    two = step(two, "seq", 1, columns=True)
    mlp_part = jnp.concatenate([total(one)[0], total(two)[0]], axis=0).astype(BF16)
    back_near = exchange(back_sent, "seq", 1)
    back_far = exchange((back_kept[1].astype(F32) + back_near[1].astype(F32)).astype(BF16), "seq", 2)
    input_gradient = input_grad(x, attended_grad, back_kept, back_near, back_far)
    qkv_blocks = from_slices(combine(qkv, tokens=(back_far,)))
    mlp_blocks = from_slices(mlp_part)
    gain_one, gain_two = norm_one[:, None], norm_two[:, None]
    if aligned:
        qkv_gradient, gain_grad1 = finish(
            finish_qkv_kernel, "finish_qkv", spot, qkv_blocks, qkv_weight, gain_one, ((share, 3 * width), (share, 1))
        )
        attn_gradient, in_gradient, gain_grad2, out_gradient = finish(
            finish_feed_kernel, "finish_feed", spot, mlp_blocks, mlp_in_weight, gain_two,
            ((share, width), (share, 2 * hidden_size), (share, 1), (hidden_share, width)),
        )
    else:
        ordered = in_order(qkv_blocks, here)
        summed = jnp.concatenate(
            [b[:, c * span : (c + 1) * span] for c in range(3) for b in ordered], axis=1
        ).astype(F32)
        gain_grad1 = jnp.sum(qkv_weight.astype(F32) * summed, axis=1, keepdims=True)
        qkv_gradient = summed * gain_one.astype(F32)
        ordered = in_order(mlp_blocks, here)
        summed = jnp.concatenate(
            [jnp.concatenate([ordered[core], ordered[2 + core]], axis=1) for core in range(2)], axis=0
        ).astype(F32)
        attn_gradient = summed[:share]
        first_out = share * (1 + blocks)
        out_gradient = summed[first_out : first_out + hidden_share]
        summed = jnp.concatenate([summed[share * (1 + c) : share * (2 + c)] for c in range(blocks)], axis=1)
        gain_grad2 = jnp.sum(mlp_in_weight.astype(F32) * summed, axis=1, keepdims=True)
        in_gradient = summed * gain_two.astype(F32)
    return (
        result,
        input_gradient,
        gain_grad1[:, 0],
        qkv_gradient,
        attn_gradient,
        gain_grad2[:, 0],
        in_gradient,
        out_gradient,
    )


def solution(mesh):
    tokens = P("fsdp", "seq", None)
    vector = P("fsdp")
    matrix = P("fsdp", None)
    return jax.shard_map(
        body,
        mesh=mesh,
        in_specs=(tokens, vector, matrix, matrix, vector, matrix, matrix, tokens),
        out_specs=(tokens, tokens, vector, matrix, matrix, vector, matrix, matrix),
        check_vma=False,
    )
```

```python
import functools
import jax, jax.numpy as jnp
from jax import lax
from jax.experimental import pallas as pl
from jax.experimental.pallas import tpu as pltpu

from jax.sharding import PartitionSpec as P

HEADS = 12
HEAD = 64
PAD = 128
EPSILON = 1e-05
MIB = 1 << 20
LOG2E = 1.4426950408889634
F32 = jnp.float32
BF16 = jnp.bfloat16


def _dot(a, b, ca, cb):
    return lax.dot_general(a, b, (((ca,), (cb,)), ((), ())), preferred_element_type=F32)


def _normalize(values):
    centred = values - jnp.mean(values, axis=1, keepdims=True)
    variance = jnp.mean(centred * centred, axis=1, keepdims=True)
    scale_inv = lax.rsqrt(variance + EPSILON)
    return centred * scale_inv, scale_inv


def _norm_back(grad_hat, normed, scale_inv):
    return scale_inv * (
        grad_hat
        - jnp.mean(grad_hat, axis=1, keepdims=True)
        - normed * jnp.mean(grad_hat * normed, axis=1, keepdims=True)
    )


def _tables(table_ref, heads):
    spread = lambda part: jnp.concatenate([part] * (2 * heads), axis=1)
    return spread(table_ref[:, :HEAD]), spread(table_ref[:, HEAD:])


def _half_turn(v):
    lane = lax.broadcasted_iota(jnp.int32, v.shape, 1)
    ahead = pltpu.roll(v, v.shape[1] - HEAD // 2, 1)
    behind = pltpu.roll(v, HEAD // 2, 1)
    return jnp.where(lane % HEAD < HEAD // 2, ahead, behind)


def _parts(v):
    high = v.astype(BF16)
    rest = v - high.astype(F32)
    mid = rest.astype(BF16)
    low = (rest - mid.astype(F32)).astype(BF16)
    return high, mid, low


def _with_parts(base, v):
    rows = base.shape[0]
    high, mid, low = _parts(v)
    lane = lax.broadcasted_iota(jnp.int32, (rows, PAD - HEAD), 1)
    f = lambda p: p.astype(F32)
    tail = jnp.where(lane == 0, f(high), jnp.where(lane == 1, f(mid), jnp.where(lane == 2, f(low), 0.0)))
    return jnp.concatenate([base[:, :HEAD], tail.astype(BF16)], axis=1)


def _params(mib):
    return pltpu.CompilerParams(vmem_limit_bytes=mib * MIB)


def _row(block, n, first=0):
    return pl.BlockSpec((block, n), lambda i, *_: (i + first, 0))


def _whole(a):
    rank = len(a.shape)
    return pl.BlockSpec(a.shape, lambda i, *_: (0,) * rank)


def _unread(tokens):
    return [pl.BlockSpec(memory_space=pl.ANY) for _ in tokens]


def _shape(shape, dtype=BF16):
    return jax.ShapeDtypeStruct(shape, dtype)


def _cost(flops, size, transcendentals=0):
    return pl.CostEstimate(flops=int(flops), bytes_accessed=int(size), transcendentals=int(transcendentals))


def project_kernel(heads, spots, x0, x1, x2, x3, even_ref, odd_ref, table_ref, w_ref, normed_ref, q_ref, k_ref, v_ref, x_scr):
    step = pl.program_id(0)
    owners = w_ref.shape[0] // even_ref.shape[1]
    share = even_ref.shape[1]

    @pl.when(step == 0)
    def _():
        for i in range(owners):
            at = slice(i * share, (i + 1) * share)
            spot = spots[i]
            if owners == 1:
                w_ref[at] = even_ref[0]
            else:
                half = owners // 2

                @pl.when(spot < half)
                def _():
                    w_ref[at] = even_ref[spot]

                @pl.when(spot >= half)
                def _():
                    w_ref[at] = odd_ref[spot - half]

    for j, ref in enumerate((x0, x1, x2, x3)):

        @pl.when(step == j)
        def _(ref=ref):
            x_scr[...] = ref[...]

    normed = _normalize(x_scr[...].astype(F32))[0].astype(BF16)
    normed_ref[...] = normed
    qkv = _dot(normed, w_ref[...], 1, 0)
    span = heads * HEAD
    qk = qkv[:, : 2 * span]
    cos, sin = _tables(table_ref, heads)
    qk = qk * cos + _half_turn(qk) * sin
    rows = x0.shape[0]
    zeros = jnp.zeros((rows, PAD - HEAD), BF16)
    ones = jnp.where(lax.broadcasted_iota(jnp.int32, (rows, PAD - HEAD), 1) < 3, 1.0, 0.0).astype(BF16)
    for h in range(heads):
        at = slice(h * PAD, (h + 1) * PAD)
        lo = h * HEAD
        q_ref[:, at] = jnp.concatenate([(qk[:, lo : lo + HEAD] * (LOG2E * HEAD ** -0.5)).astype(BF16), zeros], axis=1)
        k_ref[:, at] = jnp.concatenate([qk[:, span + lo : span + lo + HEAD].astype(BF16), ones], axis=1)
        v_ref[:, at] = jnp.concatenate([qkv[:, 2 * span + lo : 2 * span + lo + HEAD].astype(BF16), ones], axis=1)


def project(spots, xs, even, odd, table, heads):
    rows, width = xs[0].shape
    length = rows * len(xs)
    columns = even.shape[2]
    w_shape = _shape((width, columns))
    return pl.pallas_call(
        functools.partial(project_kernel, heads),
        grid_spec=pltpu.PrefetchScalarGridSpec(
            num_scalar_prefetch=1,
            grid=(len(xs),),
            in_specs=[_whole(x) for x in xs] + [_whole(even), _whole(odd), _row(rows, table.shape[1])],
            out_specs=[_whole(w_shape), _row(rows, width)] + [_row(rows, heads * PAD)] * 3,
            scratch_shapes=[pltpu.VMEM((rows, width), BF16)],
        ),
        out_shape=[w_shape, _shape((length, width))] + [_shape((length, heads * PAD))] * 3,
        compiler_params=_params(18),
        cost_estimate=_cost(2 * length * width * columns, 12 << 20),
        name="project",
    )(spots, *xs, even, odd, table)


def forward_kernel(heads, sub, q_ref, k_ref, v_ref, ctx0_ref, ctx1_ref, qx_ref):
    step = pl.program_id(0)
    for r in range(q_ref.shape[0] // sub):
        part = slice(r * sub, (r + 1) * sub)
        outs = []
        for h in range(heads):
            at = slice(h * PAD, (h + 1) * PAD)
            q = q_ref[part, at]
            scores = _dot(q, k_ref[:, at], 1, 1)
            top = jnp.max(scores, axis=1, keepdims=True)
            weights = jnp.exp2(scores - top).astype(BF16)
            sums = _dot(weights, v_ref[:, at], 1, 0)
            total = sums[:, HEAD : HEAD + 1]
            outs.append(sums[:, :HEAD] / total)
            qx_ref[part, at] = _with_parts(q, -(top + jnp.log2(total)))
        out = jnp.concatenate(outs, axis=1).astype(BF16)

        @pl.when(step == 0)
        def _(part=part, out=out):
            ctx0_ref[part] = out

        @pl.when(step == 1)
        def _(part=part, out=out):
            ctx1_ref[part] = out


def attend_forward(q, k, v, heads, block, first):
    length = k.shape[0]
    span = heads * HEAD
    ctx = _shape((block, span))
    return pl.pallas_call(
        functools.partial(forward_kernel, heads, min(256, block)),
        grid=(2,),
        in_specs=[_row(block, heads * PAD, first), _whole(k), _whole(v)],
        out_specs=[_whole(ctx), _whole(ctx), _row(block, heads * PAD)],
        out_shape=[ctx, ctx, _shape((2 * block, heads * PAD))],
        compiler_params=_params(16),
        cost_estimate=_cost(16 * heads * 2 * block * length * HEAD, 6 << 20, heads * 2 * block * length),
        name="attend_forward",
    )(q, k, v)


def backward_kernel(heads, sub, count, added, k_ref, v_ref, *refs):
    items = [refs[3 * i : 3 * i + 3] for i in range(count)]
    before = refs[3 * count : 3 * count + 2] if added else (None, None)
    dq_refs, (dk_ref, dv_ref, dk_acc, dv_acc) = refs[-4 - count : -4], refs[-4:]
    fresh = True
    for (q_ref, ctx_ref, do_ref), dq_ref in zip(items, dq_refs):
        do_all = do_ref[...]
        prod = do_all.astype(F32) * ctx_ref[...].astype(F32)
        for r in range(q_ref.shape[0] // sub):
            part = slice(r * sub, (r + 1) * sub)
            dqs = []
            for h in range(heads):
                at = slice(h * PAD, (h + 1) * PAD)
                lo = h * HEAD
                q, k, v = q_ref[part, at], k_ref[:, at], v_ref[:, at]
                delta = jnp.sum(prod[part, lo : lo + HEAD], axis=1, keepdims=True)
                do = _with_parts(do_all[part, lo : lo + HEAD], -delta)
                probs = jnp.exp2(_dot(q, k, 1, 1))
                back = _dot(do, v, 1, 1)
                score_back = (probs * back).astype(BF16)
                dv = _dot(do, probs.astype(BF16), 0, 0)
                dk = _dot(q, score_back, 0, 0)
                dv_acc[at] = dv if fresh else dv_acc[at] + dv
                dk_acc[at] = dk if fresh else dk_acc[at] + dk
                dqs.append(_dot(score_back, k, 1, 0)[:, :HEAD])
            dq_ref[part] = (jnp.concatenate(dqs, axis=1) * HEAD ** -0.5).astype(BF16)
            fresh = False

    def write(ref, acc, scale, before):
        value = jnp.concatenate([(acc[h * PAD : h * PAD + HEAD] * scale).T for h in range(heads)], axis=1)
        ref[...] = (value if before is None else value + before[...].astype(F32)).astype(BF16)

    write(dk_ref, dk_acc, 1 / LOG2E, before[0])
    write(dv_ref, dv_acc, 1.0, before[1])


def attend_backward(k, v, items, heads, before=(), tokens=()):
    length = k.shape[0]
    block, span = items[0][3].shape
    whole, rows = _shape((length, span)), _shape((block, span))
    specs, operands = [], []
    for q, first, context, do in items:
        specs += [_row(block, heads * PAD, first), _whole(context), _whole(do)]
        operands += [q, context, do]
    count = len(items)
    return pl.pallas_call(
        functools.partial(backward_kernel, heads, min(256, block), count, len(before) > 0),
        grid=(1,),
        in_specs=[_whole(k), _whole(v)] + specs + [_whole(a) for a in before] + _unread(tokens),
        out_specs=[_whole(rows)] * count + [_whole(whole)] * 2,
        out_shape=[rows] * count + [whole] * 2,
        scratch_shapes=[pltpu.VMEM((heads * PAD, length), F32)] * 2,
        compiler_params=_params(26),
        cost_estimate=_cost(40 * heads * count * block * length * HEAD, 8 << 20, heads * count * block * length),
        name="attend_backward",
    )(k, v, *operands, *before, *tokens)


def _gelu(first):
    cumulative = 0.5 * (1.0 + lax.erf(first * 0.5 ** 0.5))
    density = jnp.exp(-0.5 * first * first) * 0.3989422804014327
    return first * cumulative, cumulative + first * density


def feed_kernel(share, group, here, x_ref, cot_ref, own_ref, near_ref, far_ref, diag_ref, w_ref, result_ref, back_ref, grad0, grad1, grad2, *refs):
    kept, sent = refs[:2], refs[2:4]
    ctx_all, n2_all, hidden_all, gates_all, branch_all, attn_scr, in_scr, out_scr, attn_grad, sems = refs[4:]
    rows, width = x_ref.shape
    owners, hidden_share = out_scr.shape[:2]
    hidden_size = owners * hidden_share
    span = width // group
    blocks = in_scr.shape[0]
    step = pl.program_id(0)
    at = pl.ds(pl.multiple_of(step * rows, rows), rows)
    copies = []
    for g in range(group):
        if owners % group == 0:
            each = owners // group
            source, target = w_ref.at[pl.ds((here[0] ^ g) * each, each), :share], attn_scr.at[pl.ds(g * each, each)]
        else:
            source = w_ref.at[:, pl.ds(pl.multiple_of((here[0] ^ g) * span, span), span)]
            target = attn_scr.at[:, pl.ds(g * span, span)]
        copies.append(pltpu.make_async_copy(source, target, sems.at[g]))
    for c in range(blocks):
        copies.append(pltpu.make_async_copy(w_ref.at[:, share * (1 + c) : share * (2 + c)], in_scr.at[c], sems.at[group + c]))
    first_out = share * (1 + blocks)
    copies.append(pltpu.make_async_copy(w_ref.at[:, first_out : first_out + hidden_share], out_scr, sems.at[group + blocks]))

    @pl.when(step == 0)
    def _():
        for copy in copies:
            copy.start()
        for copy in copies[:group]:
            copy.wait()

    ctx = jnp.concatenate([own_ref[...], near_ref[...], far_ref[0], diag_ref[...]], axis=1)
    ctx_all[at] = ctx
    w_attn = attn_scr[...].reshape(width, width)
    attended = x_ref[...].astype(F32) + _dot(ctx, w_attn, 1, 0)
    hat, scale = _normalize(attended)
    n2 = hat.astype(BF16)
    n2_all[at] = n2

    @pl.when(step == 0)
    def _():
        for copy in copies[group:]:
            copy.wait()

    w_in = [in_scr[c].reshape(width, width) for c in range(blocks)]
    w_out = out_scr[...].reshape(hidden_size, width)
    gate_up = jnp.concatenate([_dot(n2, w, 1, 0) for w in w_in], axis=1)
    first, second = gate_up[:, :hidden_size], gate_up[:, hidden_size:]
    gelu, slope = _gelu(first)
    hidden = (gelu * second).astype(BF16)
    hidden_all[at] = hidden
    result_ref[0] = (attended + _dot(hidden, w_out, 1, 0)).astype(BF16)
    cot = cot_ref[at]
    hidden_back = _dot(cot, w_out, 1, 1)
    gates = jnp.concatenate([hidden_back * second * slope, hidden_back * gelu], axis=1).astype(BF16)
    gates_all[at] = gates
    back = sum(_dot(gates[:, c * width : (c + 1) * width], w, 1, 1) for c, w in enumerate(w_in))
    back = cot.astype(F32) + _norm_back(back, hat, scale)
    back_ref[...] = back
    branch = back.astype(BF16)
    branch_all[at] = branch
    grads = _dot(branch, w_attn, 1, 1).astype(BF16)
    grad0[...] = grads[:, :span]
    grad1[...] = grads[:, span : 2 * span]
    grad2[0] = grads[:, 2 * span : 3 * span]
    grad2[1] = grads[:, 3 * span :]

    cut = kept[0].shape[1]
    half = cut + kept[1].shape[1]
    core = here[0] & 1

    def place(value, start, size):
        value = value.reshape(owners, size, width).astype(BF16)
        for side in range(2):
            for g, (lower, upper) in enumerate(((0, cut), (cut, half))):
                lower, upper = side * half + lower, side * half + upper
                lo, hi = max(start, lower), min(start + size, upper)
                if lo < hi:
                    part = value[:, lo - start : hi - start]
                    rows_at = slice(lo - lower, hi - lower)

                    @pl.when(core == side)
                    def _(part=part, rows_at=rows_at, g=g):
                        kept[g][:, rows_at] = part

                    @pl.when(core != side)
                    def _(part=part, rows_at=rows_at, g=g):
                        sent[g][:, rows_at] = part

    @pl.when(step == pl.num_programs(0) - 1)
    def _():
        attn = _dot(ctx_all[...], branch_all[...], 0, 0)
        for g in range(group):
            spot = pl.multiple_of((here[0] ^ g) * span, span)
            attn_grad[pl.ds(spot, span)] = attn[g * span : (g + 1) * span]
        place(attn_grad[...], 0, share)
        n2_whole = n2_all[...]
        for c in range(blocks):
            place(_dot(n2_whole, gates_all[:, c * width : (c + 1) * width], 0, 0), share * (1 + c), share)
        place(_dot(hidden_all[...], cot_ref[...], 0, 0), first_out, hidden_share)
        last = first_out + hidden_share
        if last < 2 * half:
            place(jnp.zeros((owners * (2 * half - last), width), F32), last, 2 * half - last)


def feed(here, x, cot, own, near, far, diag, packed, share, hidden_size, half, cut, block=256):
    rows, width = x.shape
    span = own.shape[1]
    group = width // span
    blocks = 2 * hidden_size // width
    owners = packed.shape[0]
    lead = lambda n, lead_width: pl.BlockSpec((n, block, lead_width), lambda i, *_: (0, i, 0))
    parts = [_shape((owners, cut, width)), _shape((owners, half - cut, width))] * 2
    return pl.pallas_call(
        functools.partial(feed_kernel, share, group),
        grid_spec=pltpu.PrefetchScalarGridSpec(
            num_scalar_prefetch=1,
            grid=(rows // block,),
            in_specs=[_row(block, width), _whole(cot), _row(block, span), _row(block, span), lead(1, span), _row(block, span), pl.BlockSpec(memory_space=pl.ANY)],
            out_specs=[lead(1, width), _row(block, width), _row(block, span), _row(block, span), lead(2, span)] + [_whole(p) for p in parts],
            scratch_shapes=[pltpu.VMEM((rows, n), BF16) for n in (width, width, hidden_size, 2 * hidden_size, width)]
            + [
                pltpu.VMEM((owners, share, width), BF16),
                pltpu.VMEM((blocks, owners, share, width), BF16),
                pltpu.VMEM((owners, hidden_size // owners, width), BF16),
                pltpu.VMEM((width, width), F32),
                pltpu.SemaphoreType.DMA((group + blocks + 1,)),
            ],
        ),
        out_shape=[_shape((1, rows, width)), _shape((rows, width), F32), _shape((rows, span)), _shape((rows, span)), _shape((2, rows, span))] + parts,
        compiler_params=_params(44),
        cost_estimate=_cost(6 * rows * width * (width + 3 * hidden_size), 20 << 20, 2 * rows * hidden_size),
        name="feed",
    )(here, x, cot, own, near, far, diag, packed)


def qkv_grads_kernel(heads, tokens, owner, *refs):
    dqs, (dk_ref, dv_ref, table_ref, normed_ref), refs = refs[:4], refs[4:8], refs[8:]
    grads_ref, kept_ref, sent_ref, acc = refs[tokens:]
    step = pl.program_id(0)

    @pl.when(step == 0)
    def _():
        acc[...] = jnp.zeros_like(acc)

    cos, sin = _tables(table_ref, heads)
    dq = dqs[0][...].astype(F32)
    for j in range(1, 4):
        dq = jnp.where(step == j, dqs[j][...].astype(F32), dq)
    qk = jnp.concatenate([dq, dk_ref[...].astype(F32)], axis=1)
    qk = (qk * cos - _half_turn(qk) * sin).astype(BF16)
    grads = jnp.concatenate([qk, dv_ref[...]], axis=1)
    grads_ref[...] = grads
    acc[...] += _dot(normed_ref[...], grads, 0, 0)

    @pl.when(step == pl.num_programs(0) - 1)
    def _():
        pairs, share = kept_ref.shape[:2]
        for i in range(2 * pairs):
            part = acc[i * share : (i + 1) * share].astype(BF16)

            @pl.when((owner[0] & 1) == i % 2)
            def _(part=part, i=i):
                kept_ref[i // 2] = part

            @pl.when((owner[0] & 1) != i % 2)
            def _(part=part, i=i):
                sent_ref[i // 2] = part


def qkv_grads(owner, dqs, dk, dv, table, normed, heads, block, owners, tokens=()):
    length, width = normed.shape
    span = heads * HEAD
    half = _shape((owners // 2, width // owners, 3 * span))
    return pl.pallas_call(
        functools.partial(qkv_grads_kernel, heads, len(tokens)),
        grid_spec=pltpu.PrefetchScalarGridSpec(
            num_scalar_prefetch=1,
            grid=(length // block,),
            in_specs=[_whole(dqs[0])] * 4
            + [_row(block, span)] * 2
            + [_row(block, table.shape[1])]
            + [_row(block, width)]
            + _unread(tokens),
            out_specs=[_row(block, 3 * span), _whole(half), _whole(half)],
            scratch_shapes=[pltpu.VMEM((width, 3 * span), F32)],
        ),
        out_shape=[_shape((length, 3 * span)), half, half],
        compiler_params=_params(16),
        cost_estimate=_cost(2 * length * width * 3 * span, 8 << 20),
        name="qkv_grads",
    )(owner, *dqs, dk, dv, table, normed, *tokens)


def input_back_kernel(grads_ref, w_ref, *refs):
    kept_ref, sent_ref = refs[-2:]
    back = _dot(grads_ref[...], w_ref[...], 1, 1).astype(BF16)

    @pl.when(pl.program_id(0) % 2 == 0)
    def _():
        kept_ref[0] = back

    @pl.when(pl.program_id(0) % 2 == 1)
    def _():
        sent_ref[0] = back


def input_back(grads, w, block, tokens=()):
    length, columns = grads.shape
    width = w.shape[0]
    spec = pl.BlockSpec((1, block, width), lambda i: (i // 2, 0, 0))
    return pl.pallas_call(
        input_back_kernel,
        grid=(length // block,),
        in_specs=[_row(block, columns), _whole(w)] + _unread(tokens),
        out_specs=[spec, spec],
        out_shape=[_shape((length // block // 2, block, width))] * 2,
        compiler_params=_params(10),
        cost_estimate=_cost(2 * length * width * columns, 6 << 20),
        name="input_back",
    )(grads, w, *tokens)


def combine_kernel(count, *refs):
    refs[-1][...] = sum(ref[...].astype(F32) for ref in refs[:count]).astype(BF16)


def combine(addends, tokens=()):
    whole = pl.BlockSpec(memory_space=pltpu.VMEM)
    return pl.pallas_call(
        functools.partial(combine_kernel, len(addends)),
        in_specs=[whole] * len(addends) + _unread(tokens),
        out_specs=whole,
        out_shape=_shape(addends[0].shape),
        compiler_params=_params(10),
        name="combine",
    )(*addends, *tokens)


def _pick(here, blocks, group):
    value = blocks[0]
    for j in range(1, len(blocks)):
        value = jnp.where((here ^ group) == j, blocks[j], value)
    return value


def _row_sums(value):
    folded = sum(value[:, at : at + PAD] for at in range(0, value.shape[1], PAD))
    return jnp.sum(folded.T, axis=0, keepdims=True)


def finish_qkv_kernel(here, b0, b1, b2, b3, weight_ref, gain_ref, grad_ref, gain_grad_ref):
    blocks = [b[...].astype(F32) for b in (b0, b1, b2, b3)]
    ordered = [_pick(here[0], blocks, g) for g in range(4)]
    span = b0.shape[1] // 3
    summed = jnp.concatenate([o[:, c * span : (c + 1) * span] for c in range(3) for o in ordered], axis=1)
    gain_grad_ref[...] = _row_sums(weight_ref[...].astype(F32) * summed)
    grad_ref[...] = summed * gain_ref[...].astype(F32)


def finish_feed_kernel(here, b0, b1, b2, b3, weight_ref, gain_ref, attn_ref, in_ref, gain_grad_ref, out_ref):
    share, width = attn_ref.shape
    half = b0.shape[0]
    blocks = [b[...].astype(F32) for b in (b0, b1, b2, b3)]
    ordered = [_pick(here[0], blocks, g) for g in range(4)]
    rows = jnp.concatenate([jnp.concatenate([ordered[core], ordered[2 + core]], axis=1) for core in range(2)], axis=0)
    attn_ref[...] = rows[:share]
    count = in_ref.shape[1] // width
    summed = jnp.concatenate([rows[share * (1 + c) : share * (2 + c)] for c in range(count)], axis=1)
    gain_grad_ref[...] = _row_sums(weight_ref[...].astype(F32) * summed)
    in_ref[...] = summed * gain_ref[...].astype(F32)
    first = share * (1 + count)
    out_ref[...] = rows[first : first + out_ref.shape[0]]


def finish(kernel, name, here, blocks, weight, gain, shapes):
    whole = pl.BlockSpec(memory_space=pltpu.VMEM)
    return pl.pallas_call(
        kernel,
        in_specs=[pl.BlockSpec(memory_space=pltpu.SMEM)] + [whole] * 6,
        out_specs=[whole] * len(shapes),
        out_shape=[_shape(s, F32) for s in shapes],
        compiler_params=_params(10),
        name=name,
    )(here, *blocks, weight, gain)


def input_grad_kernel(x_ref, direct_ref, kept_ref, near_ref, far_ref, out_ref):
    hat, scale = _normalize(x_ref[...].astype(F32))
    back = kept_ref[0].astype(F32) + near_ref[0].astype(F32) + far_ref[...].astype(F32)
    out_ref[0] = (direct_ref[...] + _norm_back(back, hat, scale)).astype(BF16)


def input_grad(x, direct, kept, near, far, block=256):
    rows, width = x.shape
    lead = pl.BlockSpec((1, block, width), lambda i: (0, i, 0))
    return pl.pallas_call(
        input_grad_kernel,
        grid=(rows // block,),
        in_specs=[_row(block, width), _row(block, width), lead, lead, _row(block, width)],
        out_specs=lead,
        out_shape=_shape((1, rows, width)),
        compiler_params=_params(10),
        name="input_grad",
    )(x, direct, kept, near, far)


def halve_pair_kernel(columns, own, a_ref, b_ref, *refs):
    kept_ref, sent_ref = refs[-2:]
    if columns:
        half = a_ref.shape[2] // 2
        for side in range(2):
            at = slice(side * half, (side + 1) * half)
            part = (a_ref[:, :, at].astype(F32) + b_ref[:, :, at].astype(F32)).astype(BF16)

            @pl.when(own[0] == side)
            def _(part=part):
                kept_ref[...] = part

            @pl.when(own[0] != side)
            def _(part=part):
                sent_ref[...] = part

    else:
        for i in range(kept_ref.shape[0]):
            for ref, side in ((kept_ref, own[0]), (sent_ref, 1 - own[0])):
                at = 2 * i + side
                ref[i] = (a_ref[at].astype(F32) + b_ref[at].astype(F32)).astype(BF16)


def halve_pair(own, a, b, columns=False, tokens=()):
    n, rows, width = a.shape
    half = _shape((n, rows, width // 2) if columns else (n // 2, rows, width))
    whole = pl.BlockSpec(memory_space=pltpu.VMEM)
    return pl.pallas_call(
        functools.partial(halve_pair_kernel, columns),
        in_specs=[pl.BlockSpec(memory_space=pltpu.SMEM), whole, whole] + _unread(tokens),
        out_specs=[whole, whole],
        out_shape=[half, half],
        compiler_params=_params(10),
        name="halve_pair",
    )(own, a, b, *tokens)


def relay_kernel(*refs):
    pass


def relay(value, token):
    anywhere = pl.BlockSpec(memory_space=pl.ANY)
    return pl.pallas_call(
        relay_kernel,
        in_specs=[anywhere, anywhere],
        out_specs=anywhere,
        out_shape=_shape(value.shape, value.dtype),
        input_output_aliases={0: 0},
        name="relay",
    )(value, token)


def exchange(value, axis, distance):
    size = lax.axis_size(axis)
    return lax.ppermute(value, axis, [(i, i ^ distance) for i in range(size)])


def gather_halves(piece, axis, token):
    size = lax.axis_size(axis)
    pieces, order = piece[None], [0]
    distance = size // 2
    while distance > 1:
        pieces = jnp.concatenate([pieces, exchange(pieces, axis, distance)], axis=0)
        if distance == size // 2:
            pieces = relay(pieces, token)
        order = order + [place ^ distance for place in order]
        distance //= 2
    other = exchange(pieces, axis, 1)
    order = order + [place ^ 1 for place in order]
    where = jnp.asarray([order.index(place) for place in range(size)], jnp.int32)
    return pieces, other, where[lax.axis_index(axis) ^ jnp.arange(size)]


def halve(addends, axis, bit, take):
    own = (lax.axis_index(axis) >> bit) & 1
    sent = sum(take(a, 1 - own).astype(F32) for a in addends).astype(BF16)
    return [take(a, own) for a in addends] + [exchange(sent, axis, 1 << bit)]


def split_owners(addends, axis):
    bits = lax.axis_size(axis).bit_length() - 1
    return [a.reshape((2,) * bits + a.shape[1:]) for a in addends]


def halve_owners(addends, axis, bit):
    dim = lax.axis_size(axis).bit_length() - 2 - bit
    return halve(addends, axis, bit, lambda a, at: lax.dynamic_index_in_dim(a, at, dim, keepdims=False))


def scatter_rows(addends, axis, first=0):
    for bit in range(first, lax.axis_size(axis).bit_length() - 1):
        addends = halve_owners(addends, axis, bit)
    return addends


def total(addends):
    return sum(a.astype(F32) for a in addends)


ROPE_BASE = 160000.0


def rope_tables(places):
    half = HEAD // 2
    inverse = ROPE_BASE ** (-(jnp.arange(half, dtype=F32) * 2.0 / HEAD))
    angles = places[:, None] * inverse[None, :]
    cosine, sine = lax.optimization_barrier((jnp.cos(angles), jnp.sin(angles)))
    return jnp.concatenate([cosine, cosine, -sine, sine], axis=1), sine


def from_slices(block):
    far = exchange(block, "seq", 2)
    return [block, exchange(block, "seq", 1), far, exchange(far, "seq", 1)]


def step(pair, axis, bit, columns=False, tokens=()):
    own = jnp.reshape((lax.axis_index(axis) >> bit) & 1, (1,)).astype(jnp.int32)
    kept, sent = halve_pair(own, *pair, columns, tokens)
    return [kept, exchange(sent, axis, 1 << bit)]


def in_order(blocks, here):
    stacked = jnp.stack(blocks)
    return [lax.dynamic_index_in_dim(stacked, here ^ i, 0, keepdims=False) for i in range(len(blocks))]


def up16(n):
    return -(-n // 16) * 16


def body(
    inputs,
    norm_one,
    qkv_weight,
    attn_out_weight,
    norm_two,
    mlp_in_weight,
    mlp_out_weight,
    cotangent,
):
    here = lax.axis_index("seq")
    slices = lax.axis_size("seq")
    owners = lax.axis_size("fsdp")
    heads = HEADS // slices
    span = heads * HEAD
    rows, width = inputs.shape[1:]
    share = qkv_weight.shape[0]
    hidden_share = mlp_out_weight.shape[0]
    hidden_size = hidden_share * owners
    blocks = 2 * hidden_size // width
    aligned = share % 16 == 0 and hidden_share % 16 == 0
    spot = jnp.reshape(here, (1,)).astype(jnp.int32)

    x = inputs[0]
    scaled_qkv = (qkv_weight.astype(F32) * norm_one.astype(F32)[:, None]).astype(BF16)
    scaled_in = (mlp_in_weight.astype(F32) * norm_two.astype(F32)[:, None]).astype(BF16)
    x_far = exchange(x, "seq", 2)
    own_columns = jnp.concatenate(
        [lax.dynamic_slice_in_dim(scaled_qkv, c * width + here * span, span, 1) for c in range(3)], axis=1
    )
    order = here ^ jnp.arange(slices)
    places = (order[:, None] * rows + jnp.arange(rows)[None, :]).reshape(-1).astype(F32)
    table, sine = rope_tables(places)
    even, odd, spots = gather_halves(own_columns, "fsdp", sine)
    x_far = relay(x_far, even)
    xs = [x, exchange(x, "seq", 1), x_far, exchange(x_far, "seq", 1)]
    if not aligned:
        pieces = jnp.concatenate([even, odd], axis=0)
        even = jnp.take(pieces, spots, axis=0).reshape(1, width, 3 * span)
        odd, spots = even, jnp.zeros((1,), jnp.int32)

    shard = [attn_out_weight] + [scaled_in[:, c * width : (c + 1) * width] for c in range(blocks)] + [mlp_out_weight]
    shard_rows = share * (1 + blocks) + hidden_share
    part = -(-shard_rows // (8 * slices)) * 8
    shard = jnp.concatenate(shard + [jnp.zeros((part * slices - shard_rows, width), BF16)], axis=0)
    packed = lax.all_gather(lax.dynamic_slice_in_dim(shard, here * part, part, 0), ("fsdp", "seq"), axis=0, tiled=True)
    packed = packed.reshape(owners, part * slices, width)
    packed_share = share
    if not aligned:
        cuts = [share * c for c in range(2 + blocks)] + [shard_rows]
        packed = jnp.concatenate([packed[:, a:b].reshape(-1, width) for a, b in zip(cuts, cuts[1:])], axis=0)[None]
        packed_share = width

    w_qkv, normed_all, query, key, value = project(spots, xs, even, odd, table, heads)
    context_2, context_3, query_far = attend_forward(query, key, value, heads, rows, 2)
    context_far = exchange(jnp.stack([context_2, context_3]), "seq", 2)
    context_0, context_1, query_near = attend_forward(query, key, value, heads, rows, 0)
    from_1 = exchange(context_1, "seq", 1)
    from_3 = exchange(context_far[1], "seq", 1)

    cot = cotangent[0]
    grad_rows = up16(-(-shard_rows // 2))
    cut = up16(grad_rows // 2)
    packed_rows = packed_share * (1 + blocks) + hidden_size // packed.shape[0]
    cuts = (grad_rows, cut) if aligned else (packed_rows // 2, packed_rows // 4)
    result, attended_grad, grad0, grad1, grad23, *mlp_grads = feed(
        spot, x, cot, context_0, from_1, context_far, from_3, packed, packed_share, hidden_size, *cuts
    )
    grad23 = exchange(grad23, "seq", 2)
    grad1 = exchange(grad1, "seq", 1)
    grad3 = exchange(grad23[1], "seq", 1)

    kept_one, kept_two, sent_one, sent_two = mlp_grads
    if not aligned:
        core = here & 1
        kept, sent = jnp.concatenate(mlp_grads[:2], axis=1), jnp.concatenate(mlp_grads[2:], axis=1)
        both = jnp.where(core == 0, jnp.concatenate([kept, sent], axis=1), jnp.concatenate([sent, kept], axis=1))[0]
        edges = [width * c for c in range(2 + blocks)] + [packed_rows]
        both = jnp.concatenate([both[a:b].reshape(owners, -1, width) for a, b in zip(edges, edges[1:])], axis=1)
        both = jnp.pad(both, ((0, 0), (0, 2 * grad_rows - shard_rows), (0, 0)))
        kept = lax.dynamic_slice_in_dim(both, core * grad_rows, grad_rows, 1)
        sent = lax.dynamic_slice_in_dim(both, (1 - core) * grad_rows, grad_rows, 1)
        kept_one, kept_two, sent_one, sent_two = kept[:, :cut], kept[:, cut:], sent[:, :cut], sent[:, cut:]
    one = [kept_one, exchange(sent_one, "seq", 1)]
    two = [kept_two, exchange(sent_two, "seq", 1)]

    dq_0, *back = attend_backward(key, value, [(query_near, 0, context_0, grad0)], heads)
    tokens = (one[1], two[1])
    one = step(one, "seq", 1, columns=True, tokens=(dq_0,))
    two = step(two, "fsdp", 0, tokens=(dq_0,))
    dq_1, dq_2, *back = attend_backward(
        key, value, [(query_near, 1, context_1, grad1), (query_far, 0, context_2, grad23[0])], heads, back, tokens
    )
    tokens = (one[1], two[1])
    one = step(one, "fsdp", 0, tokens=(dq_1,))
    two = step(two, "fsdp", 1, tokens=(dq_1,))
    dq_3, *back = attend_backward(key, value, [(query_far, 1, context_3, grad3)], heads, back, tokens)
    tokens = (one[1], two[1])
    one = step(one, "fsdp", 1, tokens=(dq_3,))
    two = step(two, "fsdp", 2, tokens=(dq_3,))
    owner = jnp.reshape(lax.axis_index("fsdp"), (1,)).astype(jnp.int32)
    qkv_back, qkv_kept, qkv_sent = qkv_grads(
        owner, (dq_0, dq_1, dq_2, dq_3), *back, table, normed_all, heads, rows,
        owners if aligned else 2, tokens=tokens
    )
    back_kept, back_sent = input_back(qkv_back, w_qkv, rows, tokens=(one[1], two[1]))
    bits = owners.bit_length() - 1
    if aligned:
        qkv = [qkv_kept, exchange(qkv_sent, "fsdp", 1)]
        for bit in range(1, bits):
            qkv = step(qkv, "fsdp", bit, tokens=(back_kept,) if bit == 1 else ())
        qkv = [a.reshape(share, 3 * span) for a in qkv]
    else:
        side = owner[0] & 1
        qkv = jnp.where(side == 0, jnp.concatenate([qkv_kept, qkv_sent]), jnp.concatenate([qkv_sent, qkv_kept]))
        qkv = scatter_rows(split_owners([qkv.reshape(owners, share, 3 * span)], "fsdp"), "fsdp")
    for bit in range(2, bits):
        one = step(one, "fsdp", bit)
    for bit in range(3, bits):
        two = step(two, "fsdp", bit)
    two = step(two, "seq", 1, columns=True)
    mlp_part = jnp.concatenate([total(one)[0], total(two)[0]], axis=0).astype(BF16)
    back_near = exchange(back_sent, "seq", 1)
    back_far = exchange((back_kept[1].astype(F32) + back_near[1].astype(F32)).astype(BF16), "seq", 2)
    input_gradient = input_grad(x, attended_grad, back_kept, back_near, back_far)
    qkv_blocks = from_slices(combine(qkv, tokens=(back_far,)))
    mlp_blocks = from_slices(mlp_part)
    gain_one, gain_two = norm_one[:, None], norm_two[:, None]
    if aligned:
        qkv_gradient, gain_grad1 = finish(
            finish_qkv_kernel, "finish_qkv", spot, qkv_blocks, qkv_weight, gain_one, ((share, 3 * width), (1, share))
        )
        attn_gradient, in_gradient, gain_grad2, out_gradient = finish(
            finish_feed_kernel, "finish_feed", spot, mlp_blocks, mlp_in_weight, gain_two,
            ((share, width), (share, 2 * hidden_size), (1, share), (hidden_share, width)),
        )
    else:
        ordered = in_order(qkv_blocks, here)
        summed = jnp.concatenate(
            [b[:, c * span : (c + 1) * span] for c in range(3) for b in ordered], axis=1
        ).astype(F32)
        gain_grad1 = jnp.sum(qkv_weight.astype(F32) * summed, axis=1)
        qkv_gradient = summed * gain_one.astype(F32)
        ordered = in_order(mlp_blocks, here)
        summed = jnp.concatenate(
            [jnp.concatenate([ordered[core], ordered[2 + core]], axis=1) for core in range(2)], axis=0
        ).astype(F32)
        attn_gradient = summed[:share]
        first_out = share * (1 + blocks)
        out_gradient = summed[first_out : first_out + hidden_share]
        summed = jnp.concatenate([summed[share * (1 + c) : share * (2 + c)] for c in range(blocks)], axis=1)
        gain_grad2 = jnp.sum(mlp_in_weight.astype(F32) * summed, axis=1)
        in_gradient = summed * gain_two.astype(F32)
    return (
        result,
        input_gradient,
        gain_grad1.reshape(share),
        qkv_gradient,
        attn_gradient,
        gain_grad2.reshape(share),
        in_gradient,
        out_gradient,
    )


def solution(mesh):
    tokens = P("fsdp", "seq", None)
    vector = P("fsdp")
    matrix = P("fsdp", None)
    return jax.shard_map(
        body,
        mesh=mesh,
        in_specs=(tokens, vector, matrix, matrix, vector, matrix, matrix, tokens),
        out_specs=(tokens, tokens, vector, matrix, matrix, vector, matrix, matrix),
        check_vma=False,
    )
```

```python
import functools
import jax, jax.numpy as jnp
from jax import lax
from jax.experimental import pallas as pl
from jax.experimental.pallas import tpu as pltpu

from jax.sharding import PartitionSpec as P

HEADS = 12
HEAD = 64
PAD = 128
EPSILON = 1e-05
MIB = 1 << 20
LOG2E = 1.4426950408889634
F32 = jnp.float32
BF16 = jnp.bfloat16


def _dot(a, b, ca, cb):
    return lax.dot_general(a, b, (((ca,), (cb,)), ((), ())), preferred_element_type=F32)


def _normalize(values):
    centred = values - jnp.mean(values, axis=1, keepdims=True)
    variance = jnp.mean(centred * centred, axis=1, keepdims=True)
    scale_inv = lax.rsqrt(variance + EPSILON)
    return centred * scale_inv, scale_inv


def _norm_back(grad_hat, normed, scale_inv):
    return scale_inv * (
        grad_hat
        - jnp.mean(grad_hat, axis=1, keepdims=True)
        - normed * jnp.mean(grad_hat * normed, axis=1, keepdims=True)
    )


def _tables(table_ref, heads):
    spread = lambda part: jnp.concatenate([part] * (2 * heads), axis=1)
    return spread(table_ref[:, :HEAD]), spread(table_ref[:, HEAD:])


def _half_turn(v):
    lane = lax.broadcasted_iota(jnp.int32, v.shape, 1)
    ahead = pltpu.roll(v, v.shape[1] - HEAD // 2, 1)
    behind = pltpu.roll(v, HEAD // 2, 1)
    return jnp.where(lane % HEAD < HEAD // 2, ahead, behind)


def _parts(v):
    high = v.astype(BF16)
    rest = v - high.astype(F32)
    mid = rest.astype(BF16)
    low = (rest - mid.astype(F32)).astype(BF16)
    return high, mid, low


def _with_parts(base, v):
    rows = base.shape[0]
    high, mid, low = _parts(v)
    lane = lax.broadcasted_iota(jnp.int32, (rows, PAD - HEAD), 1)
    f = lambda p: p.astype(F32)
    tail = jnp.where(lane == 0, f(high), jnp.where(lane == 1, f(mid), jnp.where(lane == 2, f(low), 0.0)))
    return jnp.concatenate([base[:, :HEAD], tail.astype(BF16)], axis=1)


def _params(mib):
    return pltpu.CompilerParams(vmem_limit_bytes=mib * MIB)


def _row(block, n, first=0):
    return pl.BlockSpec((block, n), lambda i, *_: (i + first, 0))


def _whole(a):
    rank = len(a.shape)
    return pl.BlockSpec(a.shape, lambda i, *_: (0,) * rank)


def _unread(tokens):
    return [pl.BlockSpec(memory_space=pl.ANY) for _ in tokens]


def _shape(shape, dtype=BF16):
    return jax.ShapeDtypeStruct(shape, dtype)


def _cost(flops, size, transcendentals=0):
    return pl.CostEstimate(flops=int(flops), bytes_accessed=int(size), transcendentals=int(transcendentals))


def project_kernel(heads, spots, x0, x1, x2, x3, even_ref, odd_ref, table_ref, w_ref, normed_ref, q_ref, k_ref, v_ref, x_scr):
    step = pl.program_id(0)
    owners = w_ref.shape[0] // even_ref.shape[1]
    share = even_ref.shape[1]

    @pl.when(step == 0)
    def _():
        for i in range(owners):
            at = slice(i * share, (i + 1) * share)
            spot = spots[i]
            if owners == 1:
                w_ref[at] = even_ref[0]
            else:
                half = owners // 2

                @pl.when(spot < half)
                def _():
                    w_ref[at] = even_ref[spot]

                @pl.when(spot >= half)
                def _():
                    w_ref[at] = odd_ref[spot - half]

    for j, ref in enumerate((x0, x1, x2, x3)):

        @pl.when(step == j)
        def _(ref=ref):
            x_scr[...] = ref[...]

    normed = _normalize(x_scr[...].astype(F32))[0].astype(BF16)
    normed_ref[...] = normed
    qkv = _dot(normed, w_ref[...], 1, 0)
    span = heads * HEAD
    qk = qkv[:, : 2 * span]
    cos, sin = _tables(table_ref, heads)
    qk = qk * cos + _half_turn(qk) * sin
    rows = x0.shape[0]
    zeros = jnp.zeros((rows, PAD - HEAD), BF16)
    ones = jnp.where(lax.broadcasted_iota(jnp.int32, (rows, PAD - HEAD), 1) < 3, 1.0, 0.0).astype(BF16)
    for h in range(heads):
        at = slice(h * PAD, (h + 1) * PAD)
        lo = h * HEAD
        q_ref[:, at] = jnp.concatenate([(qk[:, lo : lo + HEAD] * (LOG2E * HEAD ** -0.5)).astype(BF16), zeros], axis=1)
        k_ref[:, at] = jnp.concatenate([qk[:, span + lo : span + lo + HEAD].astype(BF16), ones], axis=1)
        v_ref[:, at] = jnp.concatenate([qkv[:, 2 * span + lo : 2 * span + lo + HEAD].astype(BF16), ones], axis=1)


def project(spots, xs, even, odd, table, heads):
    rows, width = xs[0].shape
    length = rows * len(xs)
    columns = even.shape[2]
    w_shape = _shape((width, columns))
    return pl.pallas_call(
        functools.partial(project_kernel, heads),
        grid_spec=pltpu.PrefetchScalarGridSpec(
            num_scalar_prefetch=1,
            grid=(len(xs),),
            in_specs=[_whole(x) for x in xs] + [_whole(even), _whole(odd), _row(rows, table.shape[1])],
            out_specs=[_whole(w_shape), _row(rows, width)] + [_row(rows, heads * PAD)] * 3,
            scratch_shapes=[pltpu.VMEM((rows, width), BF16)],
        ),
        out_shape=[w_shape, _shape((length, width))] + [_shape((length, heads * PAD))] * 3,
        compiler_params=_params(12),
        cost_estimate=_cost(2 * length * width * columns, 12 << 20),
        name="project",
    )(spots, *xs, even, odd, table)


def forward_kernel(heads, sub, q_ref, k_ref, v_ref, ctx0_ref, ctx1_ref, qx_ref):
    step = pl.program_id(0)
    for r in range(q_ref.shape[0] // sub):
        part = slice(r * sub, (r + 1) * sub)
        outs = []
        for h in range(heads):
            at = slice(h * PAD, (h + 1) * PAD)
            q = q_ref[part, at]
            scores = _dot(q, k_ref[:, at], 1, 1)
            top = jnp.max(scores, axis=1, keepdims=True)
            weights = jnp.exp2(scores - top).astype(BF16)
            sums = _dot(weights, v_ref[:, at], 1, 0)
            total = sums[:, HEAD : HEAD + 1]
            outs.append(sums[:, :HEAD] / total)
            qx_ref[part, at] = _with_parts(q, -(top + jnp.log2(total)))
        out = jnp.concatenate(outs, axis=1).astype(BF16)

        @pl.when(step == 0)
        def _(part=part, out=out):
            ctx0_ref[part] = out

        @pl.when(step == 1)
        def _(part=part, out=out):
            ctx1_ref[part] = out


def attend_forward(q, k, v, heads, block, first):
    length = k.shape[0]
    span = heads * HEAD
    ctx = _shape((block, span))
    return pl.pallas_call(
        functools.partial(forward_kernel, heads, min(256, block)),
        grid=(2,),
        in_specs=[_row(block, heads * PAD, first), _whole(k), _whole(v)],
        out_specs=[_whole(ctx), _whole(ctx), _row(block, heads * PAD)],
        out_shape=[ctx, ctx, _shape((2 * block, heads * PAD))],
        compiler_params=_params(10),
        cost_estimate=_cost(16 * heads * 2 * block * length * HEAD, 6 << 20, heads * 2 * block * length),
        name="attend_forward",
    )(q, k, v)


def backward_kernel(heads, sub, count, added, k_ref, v_ref, *refs):
    items = [refs[3 * i : 3 * i + 3] for i in range(count)]
    before = refs[3 * count : 3 * count + 2] if added else (None, None)
    dq_refs, (dk_ref, dv_ref, dk_acc, dv_acc) = refs[-4 - count : -4], refs[-4:]
    fresh = True
    for (q_ref, ctx_ref, do_ref), dq_ref in zip(items, dq_refs):
        do_all = do_ref[...]
        prod = do_all.astype(F32) * ctx_ref[...].astype(F32)
        for r in range(q_ref.shape[0] // sub):
            part = slice(r * sub, (r + 1) * sub)
            dqs = []
            for h in range(heads):
                at = slice(h * PAD, (h + 1) * PAD)
                lo = h * HEAD
                q, k, v = q_ref[part, at], k_ref[:, at], v_ref[:, at]
                delta = jnp.sum(prod[part, lo : lo + HEAD], axis=1, keepdims=True)
                do = _with_parts(do_all[part, lo : lo + HEAD], -delta)
                probs = jnp.exp2(_dot(q, k, 1, 1))
                back = _dot(do, v, 1, 1)
                score_back = (probs * back).astype(BF16)
                dv = _dot(do, probs.astype(BF16), 0, 0)
                dk = _dot(q, score_back, 0, 0)
                dv_acc[at] = dv if fresh else dv_acc[at] + dv
                dk_acc[at] = dk if fresh else dk_acc[at] + dk
                dqs.append(_dot(score_back, k, 1, 0)[:, :HEAD])
            dq_ref[part] = (jnp.concatenate(dqs, axis=1) * HEAD ** -0.5).astype(BF16)
            fresh = False

    def write(ref, acc, scale, before):
        value = jnp.concatenate([(acc[h * PAD : h * PAD + HEAD] * scale).T for h in range(heads)], axis=1)
        ref[...] = (value if before is None else value + before[...].astype(F32)).astype(BF16)

    write(dk_ref, dk_acc, 1 / LOG2E, before[0])
    write(dv_ref, dv_acc, 1.0, before[1])


def attend_backward(k, v, items, heads, before=(), tokens=()):
    length = k.shape[0]
    block, span = items[0][3].shape
    whole, rows = _shape((length, span)), _shape((block, span))
    specs, operands = [], []
    for q, first, context, do in items:
        specs += [_row(block, heads * PAD, first), _whole(context), _whole(do)]
        operands += [q, context, do]
    count = len(items)
    return pl.pallas_call(
        functools.partial(backward_kernel, heads, min(256, block), count, len(before) > 0),
        grid=(1,),
        in_specs=[_whole(k), _whole(v)] + specs + [_whole(a) for a in before] + _unread(tokens),
        out_specs=[_whole(rows)] * count + [_whole(whole)] * 2,
        out_shape=[rows] * count + [whole] * 2,
        scratch_shapes=[pltpu.VMEM((heads * PAD, length), F32)] * 2,
        compiler_params=_params(16),
        cost_estimate=_cost(40 * heads * count * block * length * HEAD, 8 << 20, heads * count * block * length),
        name="attend_backward",
    )(k, v, *operands, *before, *tokens)


def _gelu(first):
    cumulative = 0.5 * (1.0 + lax.erf(first * 0.5 ** 0.5))
    density = jnp.exp(-0.5 * first * first) * 0.3989422804014327
    return first * cumulative, cumulative + first * density


def feed_kernel(share, group, here, x_ref, cot_ref, own_ref, near_ref, far_ref, diag_ref, w_ref, result_ref, back_ref, grad0, grad1, grad2, *refs):
    kept, sent = refs[:2], refs[2:4]
    ctx_all, n2_all, hidden_all, gates_all, branch_all, attn_scr, in_scr, out_scr, attn_grad, sems = refs[4:]
    rows, width = x_ref.shape
    owners, hidden_share = out_scr.shape[:2]
    hidden_size = owners * hidden_share
    span = width // group
    blocks = in_scr.shape[0]
    step = pl.program_id(0)
    at = pl.ds(pl.multiple_of(step * rows, rows), rows)
    copies = []
    for g in range(group):
        if owners % group == 0:
            each = owners // group
            source, target = w_ref.at[pl.ds((here[0] ^ g) * each, each), :share], attn_scr.at[pl.ds(g * each, each)]
        else:
            source = w_ref.at[:, pl.ds(pl.multiple_of((here[0] ^ g) * span, span), span)]
            target = attn_scr.at[:, pl.ds(g * span, span)]
        copies.append(pltpu.make_async_copy(source, target, sems.at[g]))
    for c in range(blocks):
        copies.append(pltpu.make_async_copy(w_ref.at[:, share * (1 + c) : share * (2 + c)], in_scr.at[c], sems.at[group + c]))
    first_out = share * (1 + blocks)
    copies.append(pltpu.make_async_copy(w_ref.at[:, first_out : first_out + hidden_share], out_scr, sems.at[group + blocks]))

    @pl.when(step == 0)
    def _():
        for copy in copies:
            copy.start()
        for copy in copies[:group]:
            copy.wait()

    ctx = jnp.concatenate([own_ref[...], near_ref[...], far_ref[0], diag_ref[...]], axis=1)
    ctx_all[at] = ctx
    w_attn = attn_scr[...].reshape(width, width)
    attended = x_ref[...].astype(F32) + _dot(ctx, w_attn, 1, 0)
    hat, scale = _normalize(attended)
    n2 = hat.astype(BF16)
    n2_all[at] = n2

    @pl.when(step == 0)
    def _():
        for copy in copies[group:]:
            copy.wait()

    w_in = [in_scr[c].reshape(width, width) for c in range(blocks)]
    w_out = out_scr[...].reshape(hidden_size, width)
    gate_up = jnp.concatenate([_dot(n2, w, 1, 0) for w in w_in], axis=1)
    first, second = gate_up[:, :hidden_size], gate_up[:, hidden_size:]
    gelu, slope = _gelu(first)
    hidden = (gelu * second).astype(BF16)
    hidden_all[at] = hidden
    result_ref[0] = (attended + _dot(hidden, w_out, 1, 0)).astype(BF16)
    cot = cot_ref[at]
    hidden_back = _dot(cot, w_out, 1, 1)
    gates = jnp.concatenate([hidden_back * second * slope, hidden_back * gelu], axis=1).astype(BF16)
    gates_all[at] = gates
    back = sum(_dot(gates[:, c * width : (c + 1) * width], w, 1, 1) for c, w in enumerate(w_in))
    back = cot.astype(F32) + _norm_back(back, hat, scale)
    back_ref[...] = back
    branch = back.astype(BF16)
    branch_all[at] = branch
    grads = _dot(branch, w_attn, 1, 1).astype(BF16)
    grad0[...] = grads[:, :span]
    grad1[...] = grads[:, span : 2 * span]
    grad2[0] = grads[:, 2 * span : 3 * span]
    grad2[1] = grads[:, 3 * span :]

    cut = kept[0].shape[1]
    half = cut + kept[1].shape[1]
    core = here[0] & 1

    def place(value, start, size):
        value = value.reshape(owners, size, width).astype(BF16)
        for side in range(2):
            for g, (lower, upper) in enumerate(((0, cut), (cut, half))):
                lower, upper = side * half + lower, side * half + upper
                lo, hi = max(start, lower), min(start + size, upper)
                if lo < hi:
                    part = value[:, lo - start : hi - start]
                    rows_at = slice(lo - lower, hi - lower)

                    @pl.when(core == side)
                    def _(part=part, rows_at=rows_at, g=g):
                        kept[g][:, rows_at] = part

                    @pl.when(core != side)
                    def _(part=part, rows_at=rows_at, g=g):
                        sent[g][:, rows_at] = part

    @pl.when(step == pl.num_programs(0) - 1)
    def _():
        attn = _dot(ctx_all[...], branch_all[...], 0, 0)
        for g in range(group):
            spot = pl.multiple_of((here[0] ^ g) * span, span)
            attn_grad[pl.ds(spot, span)] = attn[g * span : (g + 1) * span]
        place(attn_grad[...], 0, share)
        n2_whole = n2_all[...]
        for c in range(blocks):
            place(_dot(n2_whole, gates_all[:, c * width : (c + 1) * width], 0, 0), share * (1 + c), share)
        place(_dot(hidden_all[...], cot_ref[...], 0, 0), first_out, hidden_share)
        last = first_out + hidden_share
        if last < 2 * half:
            place(jnp.zeros((owners * (2 * half - last), width), F32), last, 2 * half - last)


def feed(here, x, cot, own, near, far, diag, packed, share, hidden_size, half, cut, block=256):
    rows, width = x.shape
    span = own.shape[1]
    group = width // span
    blocks = 2 * hidden_size // width
    owners = packed.shape[0]
    lead = lambda n, lead_width: pl.BlockSpec((n, block, lead_width), lambda i, *_: (0, i, 0))
    parts = [_shape((owners, cut, width)), _shape((owners, half - cut, width))] * 2
    return pl.pallas_call(
        functools.partial(feed_kernel, share, group),
        grid_spec=pltpu.PrefetchScalarGridSpec(
            num_scalar_prefetch=1,
            grid=(rows // block,),
            in_specs=[_row(block, width), _whole(cot), _row(block, span), _row(block, span), lead(1, span), _row(block, span), pl.BlockSpec(memory_space=pl.ANY)],
            out_specs=[lead(1, width), _row(block, width), _row(block, span), _row(block, span), lead(2, span)] + [_whole(p) for p in parts],
            scratch_shapes=[pltpu.VMEM((rows, n), BF16) for n in (width, width, hidden_size, 2 * hidden_size, width)]
            + [
                pltpu.VMEM((owners, share, width), BF16),
                pltpu.VMEM((blocks, owners, share, width), BF16),
                pltpu.VMEM((owners, hidden_size // owners, width), BF16),
                pltpu.VMEM((width, width), F32),
                pltpu.SemaphoreType.DMA((group + blocks + 1,)),
            ],
        ),
        out_shape=[_shape((1, rows, width)), _shape((rows, width), F32), _shape((rows, span)), _shape((rows, span)), _shape((2, rows, span))] + parts,
        compiler_params=_params(36),
        cost_estimate=_cost(6 * rows * width * (width + 3 * hidden_size), 20 << 20, 2 * rows * hidden_size),
        name="feed",
    )(here, x, cot, own, near, far, diag, packed)


def qkv_grads_kernel(heads, tokens, owner, *refs):
    dqs, (dk_ref, dv_ref, table_ref, normed_ref), refs = refs[:4], refs[4:8], refs[8:]
    grads_ref, kept_ref, sent_ref, acc = refs[tokens:]
    step = pl.program_id(0)

    @pl.when(step == 0)
    def _():
        acc[...] = jnp.zeros_like(acc)

    cos, sin = _tables(table_ref, heads)
    dq = dqs[0][...].astype(F32)
    for j in range(1, 4):
        dq = jnp.where(step == j, dqs[j][...].astype(F32), dq)
    qk = jnp.concatenate([dq, dk_ref[...].astype(F32)], axis=1)
    qk = (qk * cos - _half_turn(qk) * sin).astype(BF16)
    grads = jnp.concatenate([qk, dv_ref[...]], axis=1)
    grads_ref[...] = grads
    acc[...] += _dot(normed_ref[...], grads, 0, 0)

    @pl.when(step == pl.num_programs(0) - 1)
    def _():
        pairs, share = kept_ref.shape[:2]
        for i in range(2 * pairs):
            part = acc[i * share : (i + 1) * share].astype(BF16)

            @pl.when((owner[0] & 1) == i % 2)
            def _(part=part, i=i):
                kept_ref[i // 2] = part

            @pl.when((owner[0] & 1) != i % 2)
            def _(part=part, i=i):
                sent_ref[i // 2] = part


def qkv_grads(owner, dqs, dk, dv, table, normed, heads, block, owners, tokens=()):
    length, width = normed.shape
    span = heads * HEAD
    half = _shape((owners // 2, width // owners, 3 * span))
    return pl.pallas_call(
        functools.partial(qkv_grads_kernel, heads, len(tokens)),
        grid_spec=pltpu.PrefetchScalarGridSpec(
            num_scalar_prefetch=1,
            grid=(length // block,),
            in_specs=[_whole(dqs[0])] * 4
            + [_row(block, span)] * 2
            + [_row(block, table.shape[1])]
            + [_row(block, width)]
            + _unread(tokens),
            out_specs=[_row(block, 3 * span), _whole(half), _whole(half)],
            scratch_shapes=[pltpu.VMEM((width, 3 * span), F32)],
        ),
        out_shape=[_shape((length, 3 * span)), half, half],
        compiler_params=_params(12),
        cost_estimate=_cost(2 * length * width * 3 * span, 8 << 20),
        name="qkv_grads",
    )(owner, *dqs, dk, dv, table, normed, *tokens)


def input_back_kernel(grads_ref, w_ref, *refs):
    kept_ref, sent_ref = refs[-2:]
    back = _dot(grads_ref[...], w_ref[...], 1, 1).astype(BF16)

    @pl.when(pl.program_id(0) % 2 == 0)
    def _():
        kept_ref[0] = back

    @pl.when(pl.program_id(0) % 2 == 1)
    def _():
        sent_ref[0] = back


def input_back(grads, w, block, tokens=()):
    length, columns = grads.shape
    width = w.shape[0]
    spec = pl.BlockSpec((1, block, width), lambda i: (i // 2, 0, 0))
    return pl.pallas_call(
        input_back_kernel,
        grid=(length // block,),
        in_specs=[_row(block, columns), _whole(w)] + _unread(tokens),
        out_specs=[spec, spec],
        out_shape=[_shape((length // block // 2, block, width))] * 2,
        compiler_params=_params(8),
        cost_estimate=_cost(2 * length * width * columns, 6 << 20),
        name="input_back",
    )(grads, w, *tokens)


def combine_kernel(count, *refs):
    refs[-1][...] = sum(ref[...].astype(F32) for ref in refs[:count]).astype(BF16)


def combine(addends, tokens=()):
    whole = pl.BlockSpec(memory_space=pltpu.VMEM)
    return pl.pallas_call(
        functools.partial(combine_kernel, len(addends)),
        in_specs=[whole] * len(addends) + _unread(tokens),
        out_specs=whole,
        out_shape=_shape(addends[0].shape),
        compiler_params=_params(8),
        name="combine",
    )(*addends, *tokens)


def _pick(here, blocks, group):
    value = blocks[0]
    for j in range(1, len(blocks)):
        value = jnp.where((here ^ group) == j, blocks[j], value)
    return value


def _row_sums(value):
    folded = sum(value[:, at : at + PAD] for at in range(0, value.shape[1], PAD))
    return jnp.sum(folded.T, axis=0, keepdims=True)


def finish_qkv_kernel(here, b0, b1, b2, b3, weight_ref, gain_ref, grad_ref, gain_grad_ref):
    blocks = [b[...].astype(F32) for b in (b0, b1, b2, b3)]
    ordered = [_pick(here[0], blocks, g) for g in range(4)]
    span = b0.shape[1] // 3
    summed = jnp.concatenate([o[:, c * span : (c + 1) * span] for c in range(3) for o in ordered], axis=1)
    gain_grad_ref[...] = _row_sums(weight_ref[...].astype(F32) * summed)
    grad_ref[...] = summed * gain_ref[...].astype(F32)


def finish_feed_kernel(here, b0, b1, b2, b3, weight_ref, gain_ref, attn_ref, in_ref, gain_grad_ref, out_ref):
    share, width = attn_ref.shape
    half = b0.shape[0]
    blocks = [b[...].astype(F32) for b in (b0, b1, b2, b3)]
    ordered = [_pick(here[0], blocks, g) for g in range(4)]
    rows = jnp.concatenate([jnp.concatenate([ordered[core], ordered[2 + core]], axis=1) for core in range(2)], axis=0)
    attn_ref[...] = rows[:share]
    count = in_ref.shape[1] // width
    summed = jnp.concatenate([rows[share * (1 + c) : share * (2 + c)] for c in range(count)], axis=1)
    gain_grad_ref[...] = _row_sums(weight_ref[...].astype(F32) * summed)
    in_ref[...] = summed * gain_ref[...].astype(F32)
    first = share * (1 + count)
    out_ref[...] = rows[first : first + out_ref.shape[0]]


def finish(kernel, name, here, blocks, weight, gain, shapes):
    whole = pl.BlockSpec(memory_space=pltpu.VMEM)
    return pl.pallas_call(
        kernel,
        in_specs=[pl.BlockSpec(memory_space=pltpu.SMEM)] + [whole] * 6,
        out_specs=[whole] * len(shapes),
        out_shape=[_shape(s, F32) for s in shapes],
        compiler_params=_params(8),
        name=name,
    )(here, *blocks, weight, gain)


def input_grad_kernel(x_ref, direct_ref, kept_ref, near_ref, far_ref, out_ref):
    hat, scale = _normalize(x_ref[...].astype(F32))
    back = kept_ref[0].astype(F32) + near_ref[0].astype(F32) + far_ref[...].astype(F32)
    out_ref[0] = (direct_ref[...] + _norm_back(back, hat, scale)).astype(BF16)


def input_grad(x, direct, kept, near, far, block=256):
    rows, width = x.shape
    lead = pl.BlockSpec((1, block, width), lambda i: (0, i, 0))
    return pl.pallas_call(
        input_grad_kernel,
        grid=(rows // block,),
        in_specs=[_row(block, width), _row(block, width), lead, lead, _row(block, width)],
        out_specs=lead,
        out_shape=_shape((1, rows, width)),
        compiler_params=_params(8),
        name="input_grad",
    )(x, direct, kept, near, far)


def halve_pair_kernel(columns, own, a_ref, b_ref, *refs):
    kept_ref, sent_ref = refs[-2:]
    if columns:
        half = a_ref.shape[2] // 2
        for side in range(2):
            at = slice(side * half, (side + 1) * half)
            part = (a_ref[:, :, at].astype(F32) + b_ref[:, :, at].astype(F32)).astype(BF16)

            @pl.when(own[0] == side)
            def _(part=part):
                kept_ref[...] = part

            @pl.when(own[0] != side)
            def _(part=part):
                sent_ref[...] = part

    else:
        for i in range(kept_ref.shape[0]):
            for ref, side in ((kept_ref, own[0]), (sent_ref, 1 - own[0])):
                at = 2 * i + side
                ref[i] = (a_ref[at].astype(F32) + b_ref[at].astype(F32)).astype(BF16)


def halve_pair(own, a, b, columns=False, tokens=()):
    n, rows, width = a.shape
    half = _shape((n, rows, width // 2) if columns else (n // 2, rows, width))
    whole = pl.BlockSpec(memory_space=pltpu.VMEM)
    return pl.pallas_call(
        functools.partial(halve_pair_kernel, columns),
        in_specs=[pl.BlockSpec(memory_space=pltpu.SMEM), whole, whole] + _unread(tokens),
        out_specs=[whole, whole],
        out_shape=[half, half],
        compiler_params=_params(8),
        name="halve_pair",
    )(own, a, b, *tokens)


def relay_kernel(*refs):
    pass


def relay(value, token):
    anywhere = pl.BlockSpec(memory_space=pl.ANY)
    return pl.pallas_call(
        relay_kernel,
        in_specs=[anywhere, anywhere],
        out_specs=anywhere,
        out_shape=_shape(value.shape, value.dtype),
        input_output_aliases={0: 0},
        name="relay",
    )(value, token)


def exchange(value, axis, distance):
    size = lax.axis_size(axis)
    return lax.ppermute(value, axis, [(i, i ^ distance) for i in range(size)])


def gather_halves(piece, axis, token):
    size = lax.axis_size(axis)
    pieces, order = piece[None], [0]
    distance = size // 2
    while distance > 1:
        pieces = jnp.concatenate([pieces, exchange(pieces, axis, distance)], axis=0)
        if distance == size // 2:
            pieces = relay(pieces, token)
        order = order + [place ^ distance for place in order]
        distance //= 2
    other = exchange(pieces, axis, 1)
    order = order + [place ^ 1 for place in order]
    where = jnp.asarray([order.index(place) for place in range(size)], jnp.int32)
    return pieces, other, where[lax.axis_index(axis) ^ jnp.arange(size)]


def halve(addends, axis, bit, take):
    own = (lax.axis_index(axis) >> bit) & 1
    sent = sum(take(a, 1 - own).astype(F32) for a in addends).astype(BF16)
    return [take(a, own) for a in addends] + [exchange(sent, axis, 1 << bit)]


def split_owners(addends, axis):
    bits = lax.axis_size(axis).bit_length() - 1
    return [a.reshape((2,) * bits + a.shape[1:]) for a in addends]


def halve_owners(addends, axis, bit):
    dim = lax.axis_size(axis).bit_length() - 2 - bit
    return halve(addends, axis, bit, lambda a, at: lax.dynamic_index_in_dim(a, at, dim, keepdims=False))


def scatter_rows(addends, axis, first=0):
    for bit in range(first, lax.axis_size(axis).bit_length() - 1):
        addends = halve_owners(addends, axis, bit)
    return addends


def total(addends):
    return sum(a.astype(F32) for a in addends)


ROPE_BASE = 160000.0


def rope_tables(places):
    half = HEAD // 2
    inverse = ROPE_BASE ** (-(jnp.arange(half, dtype=F32) * 2.0 / HEAD))
    angles = places[:, None] * inverse[None, :]
    cosine, sine = lax.optimization_barrier((jnp.cos(angles), jnp.sin(angles)))
    return jnp.concatenate([cosine, cosine, -sine, sine], axis=1), sine


def from_slices(block):
    far = exchange(block, "seq", 2)
    return [block, exchange(block, "seq", 1), far, exchange(far, "seq", 1)]


def step(pair, axis, bit, columns=False, tokens=()):
    own = jnp.reshape((lax.axis_index(axis) >> bit) & 1, (1,)).astype(jnp.int32)
    kept, sent = halve_pair(own, *pair, columns, tokens)
    return [kept, exchange(sent, axis, 1 << bit)]


def in_order(blocks, here):
    stacked = jnp.stack(blocks)
    return [lax.dynamic_index_in_dim(stacked, here ^ i, 0, keepdims=False) for i in range(len(blocks))]


def up16(n):
    return -(-n // 16) * 16


def body(
    inputs,
    norm_one,
    qkv_weight,
    attn_out_weight,
    norm_two,
    mlp_in_weight,
    mlp_out_weight,
    cotangent,
):
    here = lax.axis_index("seq")
    slices = lax.axis_size("seq")
    owners = lax.axis_size("fsdp")
    heads = HEADS // slices
    span = heads * HEAD
    rows, width = inputs.shape[1:]
    share = qkv_weight.shape[0]
    hidden_share = mlp_out_weight.shape[0]
    hidden_size = hidden_share * owners
    blocks = 2 * hidden_size // width
    aligned = share % 16 == 0 and hidden_share % 16 == 0
    spot = jnp.reshape(here, (1,)).astype(jnp.int32)

    x = inputs[0]
    scaled_qkv = (qkv_weight.astype(F32) * norm_one.astype(F32)[:, None]).astype(BF16)
    scaled_in = (mlp_in_weight.astype(F32) * norm_two.astype(F32)[:, None]).astype(BF16)
    x_far = exchange(x, "seq", 2)
    own_columns = jnp.concatenate(
        [lax.dynamic_slice_in_dim(scaled_qkv, c * width + here * span, span, 1) for c in range(3)], axis=1
    )
    order = here ^ jnp.arange(slices)
    places = (order[:, None] * rows + jnp.arange(rows)[None, :]).reshape(-1).astype(F32)
    table, sine = rope_tables(places)
    even, odd, spots = gather_halves(own_columns, "fsdp", sine)
    x_far = relay(x_far, even)
    xs = [x, exchange(x, "seq", 1), x_far, exchange(x_far, "seq", 1)]
    if not aligned:
        pieces = jnp.concatenate([even, odd], axis=0)
        even = jnp.take(pieces, spots, axis=0).reshape(1, width, 3 * span)
        odd, spots = even, jnp.zeros((1,), jnp.int32)

    shard = [attn_out_weight] + [scaled_in[:, c * width : (c + 1) * width] for c in range(blocks)] + [mlp_out_weight]
    shard_rows = share * (1 + blocks) + hidden_share
    part = -(-shard_rows // (8 * slices)) * 8
    shard = jnp.concatenate(shard + [jnp.zeros((part * slices - shard_rows, width), BF16)], axis=0)
    packed = lax.all_gather(lax.dynamic_slice_in_dim(shard, here * part, part, 0), ("fsdp", "seq"), axis=0, tiled=True)
    packed = packed.reshape(owners, part * slices, width)
    packed_share = share
    if not aligned:
        cuts = [share * c for c in range(2 + blocks)] + [shard_rows]
        packed = jnp.concatenate([packed[:, a:b].reshape(-1, width) for a, b in zip(cuts, cuts[1:])], axis=0)[None]
        packed_share = width

    w_qkv, normed_all, query, key, value = project(spots, xs, even, odd, table, heads)
    context_2, context_3, query_far = attend_forward(query, key, value, heads, rows, 2)
    context_far = exchange(jnp.stack([context_2, context_3]), "seq", 2)
    context_0, context_1, query_near = attend_forward(query, key, value, heads, rows, 0)
    from_1 = exchange(context_1, "seq", 1)
    from_3 = exchange(context_far[1], "seq", 1)

    cot = cotangent[0]
    grad_rows = up16(-(-shard_rows // 2))
    cut = up16(grad_rows // 2)
    packed_rows = packed_share * (1 + blocks) + hidden_size // packed.shape[0]
    cuts = (grad_rows, cut) if aligned else (packed_rows // 2, packed_rows // 4)
    result, attended_grad, grad0, grad1, grad23, *mlp_grads = feed(
        spot, x, cot, context_0, from_1, context_far, from_3, packed, packed_share, hidden_size, *cuts
    )
    grad23 = exchange(grad23, "seq", 2)
    grad1 = exchange(grad1, "seq", 1)
    grad3 = exchange(grad23[1], "seq", 1)

    kept_one, kept_two, sent_one, sent_two = mlp_grads
    if not aligned:
        core = here & 1
        kept, sent = jnp.concatenate(mlp_grads[:2], axis=1), jnp.concatenate(mlp_grads[2:], axis=1)
        both = jnp.where(core == 0, jnp.concatenate([kept, sent], axis=1), jnp.concatenate([sent, kept], axis=1))[0]
        edges = [width * c for c in range(2 + blocks)] + [packed_rows]
        both = jnp.concatenate([both[a:b].reshape(owners, -1, width) for a, b in zip(edges, edges[1:])], axis=1)
        both = jnp.pad(both, ((0, 0), (0, 2 * grad_rows - shard_rows), (0, 0)))
        kept = lax.dynamic_slice_in_dim(both, core * grad_rows, grad_rows, 1)
        sent = lax.dynamic_slice_in_dim(both, (1 - core) * grad_rows, grad_rows, 1)
        kept_one, kept_two, sent_one, sent_two = kept[:, :cut], kept[:, cut:], sent[:, :cut], sent[:, cut:]
    one = [kept_one, exchange(sent_one, "seq", 1)]
    two = [kept_two, exchange(sent_two, "seq", 1)]

    dq_0, *back = attend_backward(key, value, [(query_near, 0, context_0, grad0)], heads)
    tokens = (one[1], two[1])
    one = step(one, "seq", 1, columns=True, tokens=(dq_0,))
    two = step(two, "fsdp", 0, tokens=(dq_0,))
    dq_1, dq_2, *back = attend_backward(
        key, value, [(query_near, 1, context_1, grad1), (query_far, 0, context_2, grad23[0])], heads, back, tokens
    )
    tokens = (one[1], two[1])
    one = step(one, "fsdp", 0, tokens=(dq_1,))
    two = step(two, "fsdp", 1, tokens=(dq_1,))
    dq_3, *back = attend_backward(key, value, [(query_far, 1, context_3, grad3)], heads, back, tokens)
    tokens = (one[1], two[1])
    one = step(one, "fsdp", 1, tokens=(dq_3,))
    two = step(two, "fsdp", 2, tokens=(dq_3,))
    owner = jnp.reshape(lax.axis_index("fsdp"), (1,)).astype(jnp.int32)
    qkv_back, qkv_kept, qkv_sent = qkv_grads(
        owner, (dq_0, dq_1, dq_2, dq_3), *back, table, normed_all, heads, rows,
        owners if aligned else 2, tokens=tokens
    )
    back_kept, back_sent = input_back(qkv_back, w_qkv, rows, tokens=(one[1], two[1]))
    bits = owners.bit_length() - 1
    if aligned:
        qkv = [qkv_kept, exchange(qkv_sent, "fsdp", 1)]
        qkv = step(qkv, "fsdp", 1, tokens=(back_kept,))
        for bit in range(2, bits):
            qkv = step(qkv, "fsdp", bit)
        qkv = [a.reshape(share, 3 * span) for a in qkv]
    else:
        side = owner[0] & 1
        qkv = jnp.where(side == 0, jnp.concatenate([qkv_kept, qkv_sent]), jnp.concatenate([qkv_sent, qkv_kept]))
        qkv = scatter_rows(split_owners([qkv.reshape(owners, share, 3 * span)], "fsdp"), "fsdp")
    for bit in range(2, bits):
        one = step(one, "fsdp", bit)
    for bit in range(3, bits):
        two = step(two, "fsdp", bit)
    two = step(two, "seq", 1, columns=True)
    mlp_part = jnp.concatenate([total(one)[0], total(two)[0]], axis=0).astype(BF16)
    back_near = exchange(back_sent, "seq", 1)
    back_far = exchange((back_kept[1].astype(F32) + back_near[1].astype(F32)).astype(BF16), "seq", 2)
    input_gradient = input_grad(x, attended_grad, back_kept, back_near, back_far)
    mlp_blocks = from_slices(mlp_part)
    gain_one, gain_two = norm_one[:, None], norm_two[:, None]
    if aligned:
        attn_gradient, in_gradient, gain_grad2, out_gradient = finish(
            finish_feed_kernel, "finish_feed", spot, mlp_blocks, mlp_in_weight, gain_two,
            ((share, width), (share, 2 * hidden_size), (1, share), (hidden_share, width)),
        )
        qkv_blocks = from_slices(combine(qkv, tokens=(input_gradient, gain_grad2)))
        qkv_gradient, gain_grad1 = finish(
            finish_qkv_kernel, "finish_qkv", spot, qkv_blocks, qkv_weight, gain_one, ((share, 3 * width), (1, share))
        )
    else:
        qkv_blocks = from_slices(total(qkv).astype(BF16))
        ordered = in_order(qkv_blocks, here)
        summed = jnp.concatenate(
            [b[:, c * span : (c + 1) * span] for c in range(3) for b in ordered], axis=1
        ).astype(F32)
        gain_grad1 = jnp.sum(qkv_weight.astype(F32) * summed, axis=1)
        qkv_gradient = summed * gain_one.astype(F32)
        ordered = in_order(mlp_blocks, here)
        summed = jnp.concatenate(
            [jnp.concatenate([ordered[core], ordered[2 + core]], axis=1) for core in range(2)], axis=0
        ).astype(F32)
        attn_gradient = summed[:share]
        first_out = share * (1 + blocks)
        out_gradient = summed[first_out : first_out + hidden_share]
        summed = jnp.concatenate([summed[share * (1 + c) : share * (2 + c)] for c in range(blocks)], axis=1)
        gain_grad2 = jnp.sum(mlp_in_weight.astype(F32) * summed, axis=1)
        in_gradient = summed * gain_two.astype(F32)
    return (
        result,
        input_gradient,
        gain_grad1.reshape(share),
        qkv_gradient,
        attn_gradient,
        gain_grad2.reshape(share),
        in_gradient,
        out_gradient,
    )


def solution(mesh):
    tokens = P("fsdp", "seq", None)
    vector = P("fsdp")
    matrix = P("fsdp", None)
    return jax.shard_map(
        body,
        mesh=mesh,
        in_specs=(tokens, vector, matrix, matrix, vector, matrix, matrix, tokens),
        out_specs=(tokens, tokens, vector, matrix, matrix, vector, matrix, matrix),
        check_vma=False,
    )
```

```python
import functools
import jax, jax.numpy as jnp
from jax import lax
from jax.experimental import pallas as pl
from jax.experimental.pallas import tpu as pltpu

from jax.sharding import PartitionSpec as P

HEADS = 12
HEAD = 64
PAD = 128
EPSILON = 1e-05
MIB = 1 << 20
LOG2E = 1.4426950408889634
F32 = jnp.float32
BF16 = jnp.bfloat16


def _dot(a, b, ca, cb):
    return lax.dot_general(a, b, (((ca,), (cb,)), ((), ())), preferred_element_type=F32)


def _normalize(values):
    centred = values - jnp.mean(values, axis=1, keepdims=True)
    variance = jnp.mean(centred * centred, axis=1, keepdims=True)
    scale_inv = lax.rsqrt(variance + EPSILON)
    return centred * scale_inv, scale_inv


def _norm_back(grad_hat, normed, scale_inv):
    return scale_inv * (
        grad_hat
        - jnp.mean(grad_hat, axis=1, keepdims=True)
        - normed * jnp.mean(grad_hat * normed, axis=1, keepdims=True)
    )


def _tables(table_ref, heads):
    spread = lambda part: jnp.concatenate([part] * (2 * heads), axis=1)
    return spread(table_ref[:, :HEAD]), spread(table_ref[:, HEAD:])


def _half_turn(v):
    lane = lax.broadcasted_iota(jnp.int32, v.shape, 1)
    ahead = -pltpu.roll(v, v.shape[1] - HEAD // 2, 1)
    behind = pltpu.roll(v, HEAD // 2, 1)
    return jnp.where(lane % HEAD < HEAD // 2, ahead, behind)


def _parts(v):
    high = v.astype(BF16)
    rest = v - high.astype(F32)
    mid = rest.astype(BF16)
    low = (rest - mid.astype(F32)).astype(BF16)
    return high, mid, low


def _with_parts(base, v):
    rows = base.shape[0]
    high, mid, low = _parts(v)
    lane = lax.broadcasted_iota(jnp.int32, (rows, PAD - HEAD), 1)
    f = lambda p: p.astype(F32)
    tail = jnp.where(lane == 0, f(high), jnp.where(lane == 1, f(mid), jnp.where(lane == 2, f(low), 0.0)))
    return jnp.concatenate([base[:, :HEAD], tail.astype(BF16)], axis=1)


def _params(mib):
    return pltpu.CompilerParams(vmem_limit_bytes=mib * MIB)


def _row(block, n, first=0):
    return pl.BlockSpec((block, n), lambda i, *_: (i + first, 0))


def _whole(a):
    rank = len(a.shape)
    return pl.BlockSpec(a.shape, lambda i, *_: (0,) * rank)


def _entry(array, at):
    if at is None:
        return _whole(array)
    return pl.BlockSpec((None,) + array.shape[1:], lambda i, *_: (at,) + (0,) * (len(array.shape) - 1))


def _unread(tokens):
    return [pl.BlockSpec(memory_space=pl.ANY) for _ in tokens]


def _shape(shape, dtype=BF16):
    return jax.ShapeDtypeStruct(shape, dtype)


def _cost(flops, size, transcendentals=0):
    return pl.CostEstimate(flops=int(flops), bytes_accessed=int(size), transcendentals=int(transcendentals))


def project_kernel(heads, spots, x0, x1, x2, x3, even_ref, odd_ref, table_ref, w_ref, normed_ref, q_ref, k_ref, v_ref, x_scr):
    step = pl.program_id(0)
    owners = w_ref.shape[0] // even_ref.shape[1]
    share = even_ref.shape[1]

    @pl.when(step == 0)
    def _():
        for i in range(owners):
            at = slice(i * share, (i + 1) * share)
            spot = spots[i]
            if owners == 1:
                w_ref[at] = even_ref[0]
            else:
                half = owners // 2

                @pl.when(spot < half)
                def _():
                    w_ref[at] = even_ref[spot]

                @pl.when(spot >= half)
                def _():
                    w_ref[at] = odd_ref[spot - half]

    for j, ref in enumerate((x0, x1, x2, x3)):

        @pl.when(step == j)
        def _(ref=ref):
            x_scr[...] = ref[...]

    normed = _normalize(x_scr[...].astype(F32))[0].astype(BF16)
    normed_ref[...] = normed
    qkv = _dot(normed, w_ref[...], 1, 0)
    span = heads * HEAD
    qk = qkv[:, : 2 * span]
    cos, sin = _tables(table_ref, heads)
    qk = qk * cos + _half_turn(qk) * sin
    rows = x0.shape[0]
    zeros = jnp.zeros((rows, PAD - HEAD), BF16)
    ones = jnp.where(lax.broadcasted_iota(jnp.int32, (rows, PAD - HEAD), 1) < 3, 1.0, 0.0).astype(BF16)
    for h in range(heads):
        at = slice(h * PAD, (h + 1) * PAD)
        lo = h * HEAD
        q_ref[:, at] = jnp.concatenate([(qk[:, lo : lo + HEAD] * (LOG2E * HEAD ** -0.5)).astype(BF16), zeros], axis=1)
        k_ref[:, at] = jnp.concatenate([qk[:, span + lo : span + lo + HEAD].astype(BF16), ones], axis=1)
        v_ref[:, at] = jnp.concatenate([qkv[:, 2 * span + lo : 2 * span + lo + HEAD].astype(BF16), ones], axis=1)


def project(spots, xs, even, odd, table, heads):
    rows, width = xs[0].shape
    length = rows * len(xs)
    columns = even.shape[2]
    w_shape = _shape((width, columns))
    return pl.pallas_call(
        functools.partial(project_kernel, heads),
        grid_spec=pltpu.PrefetchScalarGridSpec(
            num_scalar_prefetch=1,
            grid=(len(xs),),
            in_specs=[_whole(x) for x in xs] + [_whole(even), _whole(odd), _row(rows, table.shape[1])],
            out_specs=[_whole(w_shape), _row(rows, width)] + [_row(rows, heads * PAD)] * 3,
            scratch_shapes=[pltpu.VMEM((rows, width), BF16)],
        ),
        out_shape=[w_shape, _shape((length, width))] + [_shape((length, heads * PAD))] * 3,
        compiler_params=_params(12),
        cost_estimate=_cost(2 * length * width * columns, 12 << 20),
        name="project",
    )(spots, *xs, even, odd, table)


def forward_kernel(heads, sub, q_ref, k_ref, v_ref, *refs):
    ctx_refs, qx_ref = refs[:-1], refs[-1]
    step = pl.program_id(0)
    for r in range(q_ref.shape[0] // sub):
        part = slice(r * sub, (r + 1) * sub)
        outs = []
        for h in range(heads):
            at = slice(h * PAD, (h + 1) * PAD)
            q = q_ref[part, at]
            scores = _dot(q, k_ref[:, at], 1, 1)
            top = jnp.max(scores, axis=1, keepdims=True)
            weights = jnp.exp2(scores - top).astype(BF16)
            sums = _dot(weights, v_ref[:, at], 1, 0)
            total = sums[:, HEAD : HEAD + 1]
            outs.append(sums[:, :HEAD] / total)
            qx_ref[part, at] = _with_parts(q, -(top + jnp.log2(total)))
        out = jnp.concatenate(outs, axis=1).astype(BF16)

        for j, ref in enumerate(ctx_refs):

            @pl.when((step == j) | (len(ctx_refs) == 1))
            def _(part=part, out=out, ref=ref):
                ref[part] = out


def attend_forward(q, k, v, heads, block, first, stacked):
    length = k.shape[0]
    span = heads * HEAD
    ctx = _shape((block, span))
    return pl.pallas_call(
        functools.partial(forward_kernel, heads, min(256, block)),
        grid=(2,),
        in_specs=[_row(block, heads * PAD, first), _whole(k), _whole(v)],
        out_specs=([pl.BlockSpec((None, block, span), lambda i: (i, 0, 0))] if stacked else [_whole(ctx)] * 2)
        + [_row(block, heads * PAD)],
        out_shape=([_shape((2, block, span))] if stacked else [ctx] * 2) + [_shape((2 * block, heads * PAD))],
        compiler_params=_params(10),
        cost_estimate=_cost(16 * heads * 2 * block * length * HEAD, 6 << 20, heads * 2 * block * length),
        name="attend_forward",
    )(q, k, v)


def backward_kernel(heads, sub, count, added, k_ref, v_ref, *refs):
    items = [refs[3 * i : 3 * i + 3] for i in range(count)]
    before = refs[3 * count : 3 * count + 2] if added else (None, None)
    dq_refs, (dk_ref, dv_ref, dk_acc, dv_acc) = refs[-4 - count : -4], refs[-4:]
    fresh = True
    for (q_ref, ctx_ref, do_ref), dq_ref in zip(items, dq_refs):
        do_all = do_ref[...]
        prod = do_all.astype(F32) * ctx_ref[...].astype(F32)
        for r in range(q_ref.shape[0] // sub):
            part = slice(r * sub, (r + 1) * sub)
            dqs = []
            for h in range(heads):
                at = slice(h * PAD, (h + 1) * PAD)
                lo = h * HEAD
                q, k, v = q_ref[part, at], k_ref[:, at], v_ref[:, at]
                delta = jnp.sum(prod[part, lo : lo + HEAD], axis=1, keepdims=True)
                do = _with_parts(do_all[part, lo : lo + HEAD], -delta)
                probs = jnp.exp2(_dot(q, k, 1, 1))
                back = _dot(do, v, 1, 1)
                score_back = (probs * back).astype(BF16)
                dv = _dot(do, probs.astype(BF16), 0, 0)
                dk = _dot(q, score_back, 0, 0)
                dv_acc[at] = dv if fresh else dv_acc[at] + dv
                dk_acc[at] = dk if fresh else dk_acc[at] + dk
                dqs.append(_dot(score_back, k, 1, 0)[:, :HEAD])
            dq_ref[part] = (jnp.concatenate(dqs, axis=1) * HEAD ** -0.5).astype(BF16)
            fresh = False

    def write(ref, acc, scale, before):
        value = jnp.concatenate([(acc[h * PAD : h * PAD + HEAD] * scale).T for h in range(heads)], axis=1)
        ref[...] = (value if before is None else value + before[...].astype(F32)).astype(BF16)

    write(dk_ref, dk_acc, 1 / LOG2E, before[0])
    write(dv_ref, dv_acc, 1.0, before[1])


def attend_backward(k, v, items, heads, before=(), tokens=()):
    length = k.shape[0]
    block, span = items[0][4].shape[-2:]
    whole, rows = _shape((length, span)), _shape((block, span))
    specs, operands = [], []
    for q, first, context, context_at, do, do_at in items:
        specs += [_row(block, heads * PAD, first), _entry(context, context_at), _entry(do, do_at)]
        operands += [q, context, do]
    count = len(items)
    return pl.pallas_call(
        functools.partial(backward_kernel, heads, min(256, block), count, len(before) > 0),
        grid=(1,),
        in_specs=[_whole(k), _whole(v)] + specs + [_whole(a) for a in before] + _unread(tokens),
        out_specs=[_whole(rows)] * count + [_whole(whole)] * 2,
        out_shape=[rows] * count + [whole] * 2,
        scratch_shapes=[pltpu.VMEM((heads * PAD, length), F32)] * 2,
        compiler_params=_params(16),
        cost_estimate=_cost(40 * heads * count * block * length * HEAD, 8 << 20, heads * count * block * length),
        name="attend_backward",
    )(k, v, *operands, *before, *tokens)


def _gelu(first):
    cumulative = 0.5 * (1.0 + lax.erf(first * 0.5 ** 0.5))
    density = jnp.exp(-0.5 * first * first) * 0.3989422804014327
    return first * cumulative, cumulative + first * density


def feed_kernel(share, group, here, x_ref, cot_ref, own_ref, near_ref, far_ref, diag_ref, w_ref, result_ref, back_ref, grad0, grad1, grad2, *refs):
    kept, sent = refs[:2], refs[2:4]
    ctx_all, n2_all, hidden_all, gates_all, branch_all, attn_scr, in_scr, out_scr, attn_grad, sems = refs[4:]
    rows, width = x_ref.shape
    owners, hidden_share = out_scr.shape[:2]
    hidden_size = owners * hidden_share
    span = width // group
    blocks = in_scr.shape[0]
    step = pl.program_id(0)
    at = pl.ds(pl.multiple_of(step * rows, rows), rows)
    copies = []
    for g in range(group):
        if owners % group == 0:
            each = owners // group
            source, target = w_ref.at[pl.ds((here[0] ^ g) * each, each), :share], attn_scr.at[pl.ds(g * each, each)]
        else:
            source = w_ref.at[:, pl.ds(pl.multiple_of((here[0] ^ g) * span, span), span)]
            target = attn_scr.at[:, pl.ds(g * span, span)]
        copies.append(pltpu.make_async_copy(source, target, sems.at[g]))
    for c in range(blocks):
        copies.append(pltpu.make_async_copy(w_ref.at[:, share * (1 + c) : share * (2 + c)], in_scr.at[c], sems.at[group + c]))
    first_out = share * (1 + blocks)
    copies.append(pltpu.make_async_copy(w_ref.at[:, first_out : first_out + hidden_share], out_scr, sems.at[group + blocks]))

    @pl.when(step == 0)
    def _():
        for copy in copies:
            copy.start()
        for copy in copies[:group]:
            copy.wait()

    ctx = jnp.concatenate([own_ref[...], near_ref[...], far_ref[...], diag_ref[...]], axis=1)
    ctx_all[at] = ctx
    w_attn = attn_scr[...].reshape(width, width)
    attended = x_ref[...].astype(F32) + _dot(ctx, w_attn, 1, 0)
    hat, scale = _normalize(attended)
    n2 = hat.astype(BF16)
    n2_all[at] = n2

    @pl.when(step == 0)
    def _():
        for copy in copies[group:]:
            copy.wait()

    w_in = [in_scr[c].reshape(width, width) for c in range(blocks)]
    w_out = out_scr[...].reshape(hidden_size, width)
    gate_up = jnp.concatenate([_dot(n2, w, 1, 0) for w in w_in], axis=1)
    first, second = gate_up[:, :hidden_size], gate_up[:, hidden_size:]
    gelu, slope = _gelu(first)
    hidden = (gelu * second).astype(BF16)
    hidden_all[at] = hidden
    result_ref[0] = (attended + _dot(hidden, w_out, 1, 0)).astype(BF16)
    cot = cot_ref[at]
    hidden_back = _dot(cot, w_out, 1, 1)
    gates = jnp.concatenate([hidden_back * second * slope, hidden_back * gelu], axis=1).astype(BF16)
    gates_all[at] = gates
    back = sum(_dot(gates[:, c * width : (c + 1) * width], w, 1, 1) for c, w in enumerate(w_in))
    back = cot.astype(F32) + _norm_back(back, hat, scale)
    back_ref[...] = back
    branch = back.astype(BF16)
    branch_all[at] = branch
    grads = _dot(branch, w_attn, 1, 1).astype(BF16)
    grad0[...] = grads[:, :span]
    grad1[...] = grads[:, span : 2 * span]
    grad2[0] = grads[:, 2 * span : 3 * span]
    grad2[1] = grads[:, 3 * span :]

    cut = kept[0].shape[1]
    half = cut + kept[1].shape[1]
    core = here[0] & 1

    def place(value, start, size):
        value = value.reshape(owners, size, width).astype(BF16)
        for side in range(2):
            for g, (lower, upper) in enumerate(((0, cut), (cut, half))):
                lower, upper = side * half + lower, side * half + upper
                lo, hi = max(start, lower), min(start + size, upper)
                if lo < hi:
                    part = value[:, lo - start : hi - start]
                    rows_at = slice(lo - lower, hi - lower)

                    @pl.when(core == side)
                    def _(part=part, rows_at=rows_at, g=g):
                        kept[g][:, rows_at] = part

                    @pl.when(core != side)
                    def _(part=part, rows_at=rows_at, g=g):
                        sent[g][:, rows_at] = part

    @pl.when(step == pl.num_programs(0) - 1)
    def _():
        attn = _dot(ctx_all[...], branch_all[...], 0, 0)
        for g in range(group):
            spot = pl.multiple_of((here[0] ^ g) * span, span)
            attn_grad[pl.ds(spot, span)] = attn[g * span : (g + 1) * span]
        place(attn_grad[...], 0, share)
        n2_whole = n2_all[...]
        for c in range(blocks):
            place(_dot(n2_whole, gates_all[:, c * width : (c + 1) * width], 0, 0), share * (1 + c), share)
        place(_dot(hidden_all[...], cot_ref[...], 0, 0), first_out, hidden_share)
        last = first_out + hidden_share
        if last < 2 * half:
            place(jnp.zeros((owners * (2 * half - last), width), F32), last, 2 * half - last)


def feed(here, x, cot, own, near, far, diag, packed, share, hidden_size, half, cut, block=256):
    rows, width = x.shape
    span = own.shape[1]
    group = width // span
    blocks = 2 * hidden_size // width
    owners = packed.shape[0]
    lead = lambda n, lead_width: pl.BlockSpec((n, block, lead_width), lambda i, *_: (0, i, 0))
    half_at = lambda at: pl.BlockSpec((None, block, span), lambda i, *_: (at, i, 0))
    parts = [_shape((owners, cut, width)), _shape((owners, half - cut, width))] * 2
    return pl.pallas_call(
        functools.partial(feed_kernel, share, group),
        grid_spec=pltpu.PrefetchScalarGridSpec(
            num_scalar_prefetch=1,
            grid=(rows // block,),
            in_specs=[_row(block, width), _whole(cot), _row(block, span), _row(block, span), half_at(0), half_at(1), pl.BlockSpec(memory_space=pl.ANY)],
            out_specs=[lead(1, width), _row(block, width), _row(block, span), _row(block, span), lead(2, span)] + [_whole(p) for p in parts],
            scratch_shapes=[pltpu.VMEM((rows, n), BF16) for n in (width, width, hidden_size, 2 * hidden_size, width)]
            + [
                pltpu.VMEM((owners, share, width), BF16),
                pltpu.VMEM((blocks, owners, share, width), BF16),
                pltpu.VMEM((owners, hidden_size // owners, width), BF16),
                pltpu.VMEM((width, width), F32),
                pltpu.SemaphoreType.DMA((group + blocks + 1,)),
            ],
        ),
        out_shape=[_shape((1, rows, width)), _shape((rows, width), F32), _shape((rows, span)), _shape((rows, span)), _shape((2, rows, span))] + parts,
        compiler_params=_params(36),
        cost_estimate=_cost(6 * rows * width * (width + 3 * hidden_size), 20 << 20, 2 * rows * hidden_size),
        name="feed",
    )(here, x, cot, own, near, far, diag, packed)


def qkv_grads_kernel(heads, tokens, owner, *refs):
    dqs, (dk_ref, dv_ref, table_ref, normed_ref), refs = refs[:4], refs[4:8], refs[8:]
    grads_ref, kept_ref, sent_ref, acc = refs[tokens:]
    step = pl.program_id(0)

    @pl.when(step == 0)
    def _():
        acc[...] = jnp.zeros_like(acc)

    cos, sin = _tables(table_ref, heads)
    dq = dqs[0][...].astype(F32)
    for j in range(1, 4):
        dq = jnp.where(step == j, dqs[j][...].astype(F32), dq)
    qk = jnp.concatenate([dq, dk_ref[...].astype(F32)], axis=1)
    qk = (qk * cos - _half_turn(qk) * sin).astype(BF16)
    grads = jnp.concatenate([qk, dv_ref[...]], axis=1)
    grads_ref[...] = grads
    acc[...] += _dot(normed_ref[...], grads, 0, 0)

    @pl.when(step == pl.num_programs(0) - 1)
    def _():
        pairs, share = kept_ref.shape[:2]
        for i in range(2 * pairs):
            part = acc[i * share : (i + 1) * share].astype(BF16)

            @pl.when((owner[0] & 1) == i % 2)
            def _(part=part, i=i):
                kept_ref[i // 2] = part

            @pl.when((owner[0] & 1) != i % 2)
            def _(part=part, i=i):
                sent_ref[i // 2] = part


def qkv_grads(owner, dqs, dk, dv, table, normed, heads, block, owners, tokens=()):
    length, width = normed.shape
    span = heads * HEAD
    half = _shape((owners // 2, width // owners, 3 * span))
    return pl.pallas_call(
        functools.partial(qkv_grads_kernel, heads, len(tokens)),
        grid_spec=pltpu.PrefetchScalarGridSpec(
            num_scalar_prefetch=1,
            grid=(length // block,),
            in_specs=[_whole(dqs[0])] * 4
            + [_row(block, span)] * 2
            + [_row(block, table.shape[1])]
            + [_row(block, width)]
            + _unread(tokens),
            out_specs=[_row(block, 3 * span), _whole(half), _whole(half)],
            scratch_shapes=[pltpu.VMEM((width, 3 * span), F32)],
        ),
        out_shape=[_shape((length, 3 * span)), half, half],
        compiler_params=_params(12),
        cost_estimate=_cost(2 * length * width * 3 * span, 8 << 20),
        name="qkv_grads",
    )(owner, *dqs, dk, dv, table, normed, *tokens)


def input_back_kernel(grads_ref, w_ref, *refs):
    kept_ref, sent_ref = refs[-2:]
    back = _dot(grads_ref[...], w_ref[...], 1, 1).astype(BF16)

    @pl.when(pl.program_id(0) % 2 == 0)
    def _():
        kept_ref[0] = back

    @pl.when(pl.program_id(0) % 2 == 1)
    def _():
        sent_ref[0] = back


def input_back(grads, w, block, tokens=()):
    length, columns = grads.shape
    width = w.shape[0]
    spec = pl.BlockSpec((1, block, width), lambda i: (i // 2, 0, 0))
    return pl.pallas_call(
        input_back_kernel,
        grid=(length // block,),
        in_specs=[_row(block, columns), _whole(w)] + _unread(tokens),
        out_specs=[spec, spec],
        out_shape=[_shape((length // block // 2, block, width))] * 2,
        compiler_params=_params(8),
        cost_estimate=_cost(2 * length * width * columns, 6 << 20),
        name="input_back",
    )(grads, w, *tokens)


def combine_kernel(counts, *refs):
    out, at, first = refs[-1], 0, 0
    for count in counts:
        part = sum(ref[...].astype(F32) for ref in refs[at : at + count]).astype(BF16)
        out[first : first + part.shape[0]] = part
        at, first = at + count, first + part.shape[0]


def combine(groups, tokens=()):
    flat = [pair for group in groups for pair in group]
    rows = sum(group[0][0].shape[-2] for group in groups)
    out = _shape((rows, flat[0][0].shape[-1]))
    return pl.pallas_call(
        functools.partial(combine_kernel, [len(group) for group in groups]),
        grid=(1,),
        in_specs=[_entry(*pair) for pair in flat] + _unread(tokens),
        out_specs=_whole(out),
        out_shape=out,
        compiler_params=_params(8),
        name="combine",
    )(*[array for array, _ in flat], *tokens)


def join_kernel(a_ref, b_ref, out_ref):
    count = a_ref.shape[0]
    out_ref[:count] = a_ref[...]
    out_ref[count:] = b_ref[...]


def join(a, b):
    whole = pl.BlockSpec(memory_space=pltpu.VMEM)
    return pl.pallas_call(
        join_kernel,
        in_specs=[whole, whole],
        out_specs=whole,
        out_shape=_shape((a.shape[0] + b.shape[0],) + a.shape[1:]),
        compiler_params=_params(8),
        name="join",
    )(a, b)


def _pick(here, blocks, group):
    value = blocks[0]
    for j in range(1, len(blocks)):
        value = jnp.where((here ^ group) == j, blocks[j], value)
    return value


def _row_sums(value):
    folded = sum(value[:, at : at + PAD] for at in range(0, value.shape[1], PAD))
    return jnp.sum(folded.T, axis=0, keepdims=True)


def finish_qkv_kernel(here, b0, b1, b2, b3, weight_ref, gain_ref, grad_ref, gain_grad_ref):
    blocks = [b[...].astype(F32) for b in (b0, b1, b2, b3)]
    ordered = [_pick(here[0], blocks, g) for g in range(4)]
    span = b0.shape[1] // 3
    summed = jnp.concatenate([o[:, c * span : (c + 1) * span] for c in range(3) for o in ordered], axis=1)
    gain_grad_ref[...] = _row_sums(weight_ref[...].astype(F32) * summed)
    grad_ref[...] = summed * gain_ref[...].astype(F32)


def finish_feed_kernel(here, b0, b1, b2, b3, weight_ref, gain_ref, attn_ref, in_ref, gain_grad_ref, out_ref):
    share, width = attn_ref.shape
    half = b0.shape[0]
    blocks = [b[...].astype(F32) for b in (b0, b1, b2, b3)]
    ordered = [_pick(here[0], blocks, g) for g in range(4)]
    rows = jnp.concatenate([jnp.concatenate([ordered[core], ordered[2 + core]], axis=1) for core in range(2)], axis=0)
    attn_ref[...] = rows[:share]
    count = in_ref.shape[1] // width
    summed = jnp.concatenate([rows[share * (1 + c) : share * (2 + c)] for c in range(count)], axis=1)
    gain_grad_ref[...] = _row_sums(weight_ref[...].astype(F32) * summed)
    in_ref[...] = summed * gain_ref[...].astype(F32)
    first = share * (1 + count)
    out_ref[...] = rows[first : first + out_ref.shape[0]]


def finish(kernel, name, here, blocks, weight, gain, shapes):
    whole = pl.BlockSpec(memory_space=pltpu.VMEM)
    return pl.pallas_call(
        kernel,
        in_specs=[pl.BlockSpec(memory_space=pltpu.SMEM)] + [whole] * 6,
        out_specs=[whole] * len(shapes),
        out_shape=[_shape(s, F32) for s in shapes],
        compiler_params=_params(8),
        name=name,
    )(here, *blocks, weight, gain)


def input_grad_kernel(x_ref, direct_ref, kept_ref, near_ref, far_ref, out_ref):
    hat, scale = _normalize(x_ref[...].astype(F32))
    back = kept_ref[0].astype(F32) + near_ref[0].astype(F32) + far_ref[...].astype(F32)
    out_ref[0] = (direct_ref[...] + _norm_back(back, hat, scale)).astype(BF16)


def input_grad(x, direct, kept, near, far, block=256):
    rows, width = x.shape
    lead = pl.BlockSpec((1, block, width), lambda i: (0, i, 0))
    return pl.pallas_call(
        input_grad_kernel,
        grid=(rows // block,),
        in_specs=[_row(block, width), _row(block, width), lead, lead, _row(block, width)],
        out_specs=lead,
        out_shape=_shape((1, rows, width)),
        compiler_params=_params(8),
        name="input_grad",
    )(x, direct, kept, near, far)


def halve_pair_kernel(columns, own, a_ref, b_ref, *refs):
    kept_ref, sent_ref = refs[-2:]
    if columns:
        half = a_ref.shape[2] // 2
        for side in range(2):
            at = slice(side * half, (side + 1) * half)
            part = (a_ref[:, :, at].astype(F32) + b_ref[:, :, at].astype(F32)).astype(BF16)

            @pl.when(own[0] == side)
            def _(part=part):
                kept_ref[...] = part

            @pl.when(own[0] != side)
            def _(part=part):
                sent_ref[...] = part

    else:
        for i in range(kept_ref.shape[0]):
            for ref, side in ((kept_ref, own[0]), (sent_ref, 1 - own[0])):
                at = 2 * i + side
                ref[i] = (a_ref[at].astype(F32) + b_ref[at].astype(F32)).astype(BF16)


def halve_pair(own, a, b, columns=False, tokens=()):
    n, rows, width = a.shape
    half = _shape((n, rows, width // 2) if columns else (n // 2, rows, width))
    whole = pl.BlockSpec(memory_space=pltpu.VMEM)
    return pl.pallas_call(
        functools.partial(halve_pair_kernel, columns),
        in_specs=[pl.BlockSpec(memory_space=pltpu.SMEM), whole, whole] + _unread(tokens),
        out_specs=[whole, whole],
        out_shape=[half, half],
        compiler_params=_params(8),
        name="halve_pair",
    )(own, a, b, *tokens)


def relay_kernel(*refs):
    pass


def relay(value, token):
    anywhere = pl.BlockSpec(memory_space=pl.ANY)
    return pl.pallas_call(
        relay_kernel,
        in_specs=[anywhere, anywhere],
        out_specs=anywhere,
        out_shape=_shape(value.shape, value.dtype),
        input_output_aliases={0: 0},
        name="relay",
    )(value, token)


def exchange(value, axis, distance):
    size = lax.axis_size(axis)
    return lax.ppermute(value, axis, [(i, i ^ distance) for i in range(size)])


def gather_halves(piece, axis, token):
    size = lax.axis_size(axis)
    pieces, order = piece[None], [0]
    distance = size // 2
    while distance > 1:
        pieces = join(pieces, exchange(pieces, axis, distance))
        if distance == size // 2:
            pieces = relay(pieces, token)
        order = order + [place ^ distance for place in order]
        distance //= 2
    other = exchange(pieces, axis, 1)
    order = order + [place ^ 1 for place in order]
    where = jnp.asarray([order.index(place) for place in range(size)], jnp.int32)
    return pieces, other, where[lax.axis_index(axis) ^ jnp.arange(size)]


def halve(addends, axis, bit, take):
    own = (lax.axis_index(axis) >> bit) & 1
    sent = sum(take(a, 1 - own).astype(F32) for a in addends).astype(BF16)
    return [take(a, own) for a in addends] + [exchange(sent, axis, 1 << bit)]


def split_owners(addends, axis):
    bits = lax.axis_size(axis).bit_length() - 1
    return [a.reshape((2,) * bits + a.shape[1:]) for a in addends]


def halve_owners(addends, axis, bit):
    dim = lax.axis_size(axis).bit_length() - 2 - bit
    return halve(addends, axis, bit, lambda a, at: lax.dynamic_index_in_dim(a, at, dim, keepdims=False))


def scatter_rows(addends, axis, first=0):
    for bit in range(first, lax.axis_size(axis).bit_length() - 1):
        addends = halve_owners(addends, axis, bit)
    return addends


def total(addends):
    return sum(a.astype(F32) for a in addends)


ROPE_BASE = 160000.0


def rope_tables(places):
    half = HEAD // 2
    inverse = ROPE_BASE ** (-(jnp.arange(half, dtype=F32) * 2.0 / HEAD))
    angles = places[:, None] * inverse[None, :]
    cosine, sine = lax.optimization_barrier((jnp.cos(angles), jnp.sin(angles)))
    return jnp.concatenate([cosine, cosine, sine, sine], axis=1), sine


def from_slices(block):
    far = exchange(block, "seq", 2)
    return [block, exchange(block, "seq", 1), far, exchange(far, "seq", 1)]


def step(pair, axis, bit, columns=False, tokens=()):
    own = jnp.reshape((lax.axis_index(axis) >> bit) & 1, (1,)).astype(jnp.int32)
    kept, sent = halve_pair(own, *pair, columns, tokens)
    return [kept, exchange(sent, axis, 1 << bit)]


def in_order(blocks, here):
    stacked = jnp.stack(blocks)
    return [lax.dynamic_index_in_dim(stacked, here ^ i, 0, keepdims=False) for i in range(len(blocks))]


def up16(n):
    return -(-n // 16) * 16


def body(
    inputs,
    norm_one,
    qkv_weight,
    attn_out_weight,
    norm_two,
    mlp_in_weight,
    mlp_out_weight,
    cotangent,
):
    here = lax.axis_index("seq")
    slices = lax.axis_size("seq")
    owners = lax.axis_size("fsdp")
    heads = HEADS // slices
    span = heads * HEAD
    rows, width = inputs.shape[1:]
    share = qkv_weight.shape[0]
    hidden_share = mlp_out_weight.shape[0]
    hidden_size = hidden_share * owners
    blocks = 2 * hidden_size // width
    aligned = share % 16 == 0 and hidden_share % 16 == 0
    spot = jnp.reshape(here, (1,)).astype(jnp.int32)

    x = inputs[0]
    scaled_qkv = (qkv_weight.astype(F32) * norm_one.astype(F32)[:, None]).astype(BF16)
    scaled_in = (mlp_in_weight.astype(F32) * norm_two.astype(F32)[:, None]).astype(BF16)
    x_far = exchange(x, "seq", 2)
    own_columns = jnp.concatenate(
        [lax.dynamic_slice_in_dim(scaled_qkv, c * width + here * span, span, 1) for c in range(3)], axis=1
    )
    order = here ^ jnp.arange(slices)
    places = (order[:, None] * rows + jnp.arange(rows)[None, :]).reshape(-1).astype(F32)
    table, sine = rope_tables(places)
    even, odd, spots = gather_halves(own_columns, "fsdp", sine)
    x_far = relay(x_far, even)
    xs = [x, exchange(x, "seq", 1), x_far, exchange(x_far, "seq", 1)]
    if not aligned:
        pieces = jnp.concatenate([even, odd], axis=0)
        even = jnp.take(pieces, spots, axis=0).reshape(1, width, 3 * span)
        odd, spots = even, jnp.zeros((1,), jnp.int32)

    shard = [attn_out_weight] + [scaled_in[:, c * width : (c + 1) * width] for c in range(blocks)] + [mlp_out_weight]
    shard_rows = share * (1 + blocks) + hidden_share
    part = -(-shard_rows // (8 * slices)) * 8
    shard = jnp.concatenate(shard + [jnp.zeros((part * slices - shard_rows, width), BF16)], axis=0)
    packed = lax.all_gather(lax.dynamic_slice_in_dim(shard, here * part, part, 0), ("fsdp", "seq"), axis=0, tiled=True)
    packed = packed.reshape(owners, part * slices, width)
    packed_share = share
    if not aligned:
        cuts = [share * c for c in range(2 + blocks)] + [shard_rows]
        packed = jnp.concatenate([packed[:, a:b].reshape(-1, width) for a, b in zip(cuts, cuts[1:])], axis=0)[None]
        packed_share = width

    w_qkv, normed_all, query, key, value = project(spots, xs, even, odd, table, heads)
    context_23, query_far = attend_forward(query, key, value, heads, rows, 2, True)
    from_2 = exchange(context_23, "seq", 2)
    context_0, context_1, query_near = attend_forward(query, key, value, heads, rows, 0, False)
    from_1 = exchange(context_1, "seq", 1)
    from_2 = relay(from_2, context_0)
    from_3 = exchange(from_2, "seq", 1)

    cot = cotangent[0]
    grad_rows = up16(-(-shard_rows // 2))
    cut = up16(grad_rows // 2)
    packed_rows = packed_share * (1 + blocks) + hidden_size // packed.shape[0]
    cuts = (grad_rows, cut) if aligned else (packed_rows // 2, packed_rows // 4)
    result, attended_grad, grad0, grad1, grad23, *mlp_grads = feed(
        spot, x, cot, context_0, from_1, from_2, from_3, packed, packed_share, hidden_size, *cuts
    )
    grad23 = exchange(grad23, "seq", 2)
    grad1 = exchange(grad1, "seq", 1)
    grad3 = exchange(grad23, "seq", 1)

    kept_one, kept_two, sent_one, sent_two = mlp_grads
    if not aligned:
        core = here & 1
        kept, sent = jnp.concatenate(mlp_grads[:2], axis=1), jnp.concatenate(mlp_grads[2:], axis=1)
        both = jnp.where(core == 0, jnp.concatenate([kept, sent], axis=1), jnp.concatenate([sent, kept], axis=1))[0]
        edges = [width * c for c in range(2 + blocks)] + [packed_rows]
        both = jnp.concatenate([both[a:b].reshape(owners, -1, width) for a, b in zip(edges, edges[1:])], axis=1)
        both = jnp.pad(both, ((0, 0), (0, 2 * grad_rows - shard_rows), (0, 0)))
        kept = lax.dynamic_slice_in_dim(both, core * grad_rows, grad_rows, 1)
        sent = lax.dynamic_slice_in_dim(both, (1 - core) * grad_rows, grad_rows, 1)
        kept_one, kept_two, sent_one, sent_two = kept[:, :cut], kept[:, cut:], sent[:, :cut], sent[:, cut:]
    one = [kept_one, exchange(sent_one, "seq", 1)]
    two = [kept_two, exchange(sent_two, "seq", 1)]

    dq_0, *back = attend_backward(key, value, [(query_near, 0, context_0, None, grad0, None)], heads)
    tokens = (one[1], two[1])
    one = step(one, "seq", 1, columns=True, tokens=(dq_0,))
    two = step(two, "fsdp", 0, tokens=(dq_0,))
    dq_1, dq_2, *back = attend_backward(
        key, value, [(query_near, 1, context_1, None, grad1, None), (query_far, 0, context_23, 0, grad23, 0)],
        heads, back, tokens,
    )
    tokens = (one[1], two[1])
    one = step(one, "fsdp", 0, tokens=(dq_1,))
    two = step(two, "fsdp", 1, tokens=(dq_1,))
    dq_3, *back = attend_backward(key, value, [(query_far, 1, context_23, 1, grad3, 1)], heads, back, tokens)
    tokens = (one[1], two[1])
    one = step(one, "fsdp", 1, tokens=(dq_3,))
    two = step(two, "fsdp", 2, tokens=(dq_3,))
    owner = jnp.reshape(lax.axis_index("fsdp"), (1,)).astype(jnp.int32)
    qkv_back, qkv_kept, qkv_sent = qkv_grads(
        owner, (dq_0, dq_1, dq_2, dq_3), *back, table, normed_all, heads, rows,
        owners if aligned else 2, tokens=tokens
    )
    back_kept, back_sent = input_back(qkv_back, w_qkv, rows, tokens=(one[1], two[1]))
    bits = owners.bit_length() - 1
    for bit in range(2, bits):
        one = step(one, "fsdp", bit)
    for bit in range(3, bits):
        two = step(two, "fsdp", bit)
    two = step(two, "seq", 1, columns=True)
    if aligned:
        qkv = [qkv_kept, exchange(qkv_sent, "fsdp", 1)]
        qkv = step(qkv, "fsdp", 1, tokens=(back_kept, one[1]))
        for bit in range(2, bits):
            qkv = step(qkv, "fsdp", bit)
    else:
        side = owner[0] & 1
        qkv = jnp.where(side == 0, jnp.concatenate([qkv_kept, qkv_sent]), jnp.concatenate([qkv_sent, qkv_kept]))
        qkv = scatter_rows(split_owners([qkv.reshape(owners, share, 3 * span)], "fsdp"), "fsdp")
    mlp_part = combine([[(a, 0) for a in one], [(a, 0) for a in two]], tokens=(qkv[1],))
    back_near = exchange(back_sent, "seq", 1)
    back_far = exchange(combine([[(back_kept, 1), (back_near, 1)]], tokens=(two[1],)), "seq", 2)
    input_gradient = input_grad(x, attended_grad, back_kept, back_near, back_far)
    mlp_blocks = from_slices(mlp_part)
    gain_one, gain_two = norm_one[:, None], norm_two[:, None]
    if aligned:
        attn_gradient, in_gradient, gain_grad2, out_gradient = finish(
            finish_feed_kernel, "finish_feed", spot, mlp_blocks, mlp_in_weight, gain_two,
            ((share, width), (share, 2 * hidden_size), (1, share), (hidden_share, width)),
        )
        qkv_blocks = from_slices(combine([[(a, 0) for a in qkv]], tokens=(input_gradient,)))
        qkv_gradient, gain_grad1 = finish(
            finish_qkv_kernel, "finish_qkv", spot, qkv_blocks, qkv_weight, gain_one, ((share, 3 * width), (1, share))
        )
    else:
        qkv_blocks = from_slices(total(qkv).astype(BF16))
        ordered = in_order(qkv_blocks, here)
        summed = jnp.concatenate(
            [b[:, c * span : (c + 1) * span] for c in range(3) for b in ordered], axis=1
        ).astype(F32)
        gain_grad1 = jnp.sum(qkv_weight.astype(F32) * summed, axis=1)
        qkv_gradient = summed * gain_one.astype(F32)
        ordered = in_order(mlp_blocks, here)
        summed = jnp.concatenate(
            [jnp.concatenate([ordered[core], ordered[2 + core]], axis=1) for core in range(2)], axis=0
        ).astype(F32)
        attn_gradient = summed[:share]
        first_out = share * (1 + blocks)
        out_gradient = summed[first_out : first_out + hidden_share]
        summed = jnp.concatenate([summed[share * (1 + c) : share * (2 + c)] for c in range(blocks)], axis=1)
        gain_grad2 = jnp.sum(mlp_in_weight.astype(F32) * summed, axis=1)
        in_gradient = summed * gain_two.astype(F32)
    return (
        result,
        input_gradient,
        gain_grad1.reshape(share),
        qkv_gradient,
        attn_gradient,
        gain_grad2.reshape(share),
        in_gradient,
        out_gradient,
    )


def solution(mesh):
    tokens = P("fsdp", "seq", None)
    vector = P("fsdp")
    matrix = P("fsdp", None)
    return jax.shard_map(
        body,
        mesh=mesh,
        in_specs=(tokens, vector, matrix, matrix, vector, matrix, matrix, tokens),
        out_specs=(tokens, tokens, vector, matrix, matrix, vector, matrix, matrix),
        check_vma=False,
    )
```

```python
import functools
import jax, jax.numpy as jnp
from jax import lax
from jax.experimental import pallas as pl
from jax.experimental.pallas import tpu as pltpu

from jax.sharding import PartitionSpec as P

HEADS = 12
HEAD = 64
PAD = 128
EPSILON = 1e-05
MIB = 1 << 20
LOG2E = 1.4426950408889634
F32 = jnp.float32
BF16 = jnp.bfloat16


def _dot(a, b, ca, cb):
    return lax.dot_general(a, b, (((ca,), (cb,)), ((), ())), preferred_element_type=F32)


def _normalize(values):
    centred = values - jnp.mean(values, axis=1, keepdims=True)
    variance = jnp.mean(centred * centred, axis=1, keepdims=True)
    scale_inv = lax.rsqrt(variance + EPSILON)
    return centred * scale_inv, scale_inv


def _norm_back(grad_hat, normed, scale_inv):
    return scale_inv * (
        grad_hat
        - jnp.mean(grad_hat, axis=1, keepdims=True)
        - normed * jnp.mean(grad_hat * normed, axis=1, keepdims=True)
    )


def _tables(table_ref, heads):
    spread = lambda part: jnp.concatenate([part] * (2 * heads), axis=1)
    return spread(table_ref[:, :HEAD]), spread(table_ref[:, HEAD:])


def _half_turn(v):
    lane = lax.broadcasted_iota(jnp.int32, v.shape, 1)
    ahead = -pltpu.roll(v, v.shape[1] - HEAD // 2, 1)
    behind = pltpu.roll(v, HEAD // 2, 1)
    return jnp.where(lane % HEAD < HEAD // 2, ahead, behind)


def _parts(v):
    high = v.astype(BF16)
    rest = v - high.astype(F32)
    mid = rest.astype(BF16)
    low = (rest - mid.astype(F32)).astype(BF16)
    return high, mid, low


def _with_parts(base, v):
    rows = base.shape[0]
    high, mid, low = _parts(v)
    lane = lax.broadcasted_iota(jnp.int32, (rows, PAD - HEAD), 1)
    f = lambda p: p.astype(F32)
    tail = jnp.where(lane == 0, f(high), jnp.where(lane == 1, f(mid), jnp.where(lane == 2, f(low), 0.0)))
    return jnp.concatenate([base[:, :HEAD], tail.astype(BF16)], axis=1)


def _params(mib):
    return pltpu.CompilerParams(vmem_limit_bytes=mib * MIB)


def _row(block, n, first=0):
    return pl.BlockSpec((block, n), lambda i, *_: (i + first, 0))


def _whole(a):
    rank = len(a.shape)
    return pl.BlockSpec(a.shape, lambda i, *_: (0,) * rank)


def _entry(array, at):
    if at is None:
        return _whole(array)
    return pl.BlockSpec((None,) + array.shape[1:], lambda i, *_: (at,) + (0,) * (len(array.shape) - 1))


def _unread(tokens):
    return [pl.BlockSpec(memory_space=pl.ANY) for _ in tokens]


def _shape(shape, dtype=BF16):
    return jax.ShapeDtypeStruct(shape, dtype)


def _cost(flops, size, transcendentals=0):
    return pl.CostEstimate(flops=int(flops), bytes_accessed=int(size), transcendentals=int(transcendentals))


def _reversed_bits(value, size):
    bits = size.bit_length() - 1
    return sum((((value >> bit) & 1) << (bits - 1 - bit) for bit in range(bits)), jnp.int32(0))


def project_kernel(heads, places, x0, x1, x2, x3, even_ref, odd_ref, table_ref, w_ref, normed_ref, q_ref, k_ref, v_ref, x_scr):
    step = pl.program_id(0)
    owners = w_ref.shape[0] // even_ref.shape[1]
    share = even_ref.shape[1]

    @pl.when(step == 0)
    def _():
        for i in range(owners):
            at = slice(i * share, (i + 1) * share)
            spot = _reversed_bits(places[1] ^ i, owners)
            if owners == 1:
                w_ref[at] = even_ref[0]
            else:
                half = owners // 2

                @pl.when(spot < half)
                def _():
                    w_ref[at] = even_ref[spot]

                @pl.when(spot >= half)
                def _():
                    w_ref[at] = odd_ref[spot - half]

    for j, ref in enumerate((x0, x1, x2, x3)):

        @pl.when(step == j)
        def _(ref=ref):
            x_scr[...] = ref[...]

    normed = _normalize(x_scr[...].astype(F32))[0].astype(BF16)
    normed_ref[...] = normed
    qkv = _dot(normed, w_ref[...], 1, 0)
    span = heads * HEAD
    qk = qkv[:, : 2 * span]
    cos, sin = _tables(table_ref, heads)
    qk = qk * cos + _half_turn(qk) * sin
    rows = x0.shape[0]
    zeros = jnp.zeros((rows, PAD - HEAD), BF16)
    ones = jnp.where(lax.broadcasted_iota(jnp.int32, (rows, PAD - HEAD), 1) < 3, 1.0, 0.0).astype(BF16)
    for h in range(heads):
        at = slice(h * PAD, (h + 1) * PAD)
        lo = h * HEAD
        q_ref[:, at] = jnp.concatenate([(qk[:, lo : lo + HEAD] * (LOG2E * HEAD ** -0.5)).astype(BF16), zeros], axis=1)
        k_ref[:, at] = jnp.concatenate([qk[:, span + lo : span + lo + HEAD].astype(BF16), ones], axis=1)
        v_ref[:, at] = jnp.concatenate([qkv[:, 2 * span + lo : 2 * span + lo + HEAD].astype(BF16), ones], axis=1)


def project(places, xs, even, odd, table, heads):
    rows, width = xs[0].shape
    length = rows * len(xs)
    columns = even.shape[2]
    w_shape = _shape((width, columns))
    return pl.pallas_call(
        functools.partial(project_kernel, heads),
        grid_spec=pltpu.PrefetchScalarGridSpec(
            num_scalar_prefetch=1,
            grid=(len(xs),),
            in_specs=[_whole(x) for x in xs] + [_whole(even), _whole(odd), _row(rows, table.shape[1])],
            out_specs=[_whole(w_shape), _row(rows, width)] + [_row(rows, heads * PAD)] * 3,
            scratch_shapes=[pltpu.VMEM((rows, width), BF16)],
        ),
        out_shape=[w_shape, _shape((length, width))] + [_shape((length, heads * PAD))] * 3,
        compiler_params=_params(12),
        cost_estimate=_cost(2 * length * width * columns, 12 << 20),
        name="project",
    )(places, *xs, even, odd, table)


def forward_kernel(heads, sub, q_ref, k_ref, v_ref, *refs):
    ctx_refs, qx_ref = refs[:-1], refs[-1]
    step = pl.program_id(0)
    for r in range(q_ref.shape[0] // sub):
        part = slice(r * sub, (r + 1) * sub)
        outs = []
        for h in range(heads):
            at = slice(h * PAD, (h + 1) * PAD)
            q = q_ref[part, at]
            scores = _dot(q, k_ref[:, at], 1, 1)
            top = jnp.max(scores, axis=1, keepdims=True)
            weights = jnp.exp2(scores - top).astype(BF16)
            sums = _dot(weights, v_ref[:, at], 1, 0)
            total = sums[:, HEAD : HEAD + 1]
            outs.append(sums[:, :HEAD] / total)
            qx_ref[part, at] = _with_parts(q, -(top + jnp.log2(total)))
        out = jnp.concatenate(outs, axis=1).astype(BF16)

        for j, ref in enumerate(ctx_refs):

            @pl.when((step == j) | (len(ctx_refs) == 1))
            def _(part=part, out=out, ref=ref):
                ref[part] = out


def attend_forward(q, k, v, heads, block, first, stacked):
    length = k.shape[0]
    span = heads * HEAD
    ctx = _shape((block, span))
    return pl.pallas_call(
        functools.partial(forward_kernel, heads, min(256, block)),
        grid=(2,),
        in_specs=[_row(block, heads * PAD, first), _whole(k), _whole(v)],
        out_specs=([pl.BlockSpec((None, block, span), lambda i: (i, 0, 0))] if stacked else [_whole(ctx)] * 2)
        + [_row(block, heads * PAD)],
        out_shape=([_shape((2, block, span))] if stacked else [ctx] * 2) + [_shape((2 * block, heads * PAD))],
        compiler_params=_params(10),
        cost_estimate=_cost(16 * heads * 2 * block * length * HEAD, 6 << 20, heads * 2 * block * length),
        name="attend_forward",
    )(q, k, v)


def backward_kernel(heads, sub, count, added, k_ref, v_ref, *refs):
    items = [refs[3 * i : 3 * i + 3] for i in range(count)]
    before = refs[3 * count : 3 * count + 2] if added else (None, None)
    dq_refs, (dk_ref, dv_ref, dk_acc, dv_acc) = refs[-4 - count : -4], refs[-4:]
    fresh = True
    for (q_ref, ctx_ref, do_ref), dq_ref in zip(items, dq_refs):
        do_all = do_ref[...]
        prod = do_all.astype(F32) * ctx_ref[...].astype(F32)
        for r in range(q_ref.shape[0] // sub):
            part = slice(r * sub, (r + 1) * sub)
            dqs = []
            for h in range(heads):
                at = slice(h * PAD, (h + 1) * PAD)
                lo = h * HEAD
                q, k, v = q_ref[part, at], k_ref[:, at], v_ref[:, at]
                delta = jnp.sum(prod[part, lo : lo + HEAD], axis=1, keepdims=True)
                do = _with_parts(do_all[part, lo : lo + HEAD], -delta)
                probs = jnp.exp2(_dot(q, k, 1, 1))
                back = _dot(do, v, 1, 1)
                score_back = (probs * back).astype(BF16)
                dv = _dot(do, probs.astype(BF16), 0, 0)
                dk = _dot(q, score_back, 0, 0)
                dv_acc[at] = dv if fresh else dv_acc[at] + dv
                dk_acc[at] = dk if fresh else dk_acc[at] + dk
                dqs.append(_dot(score_back, k, 1, 0)[:, :HEAD])
            dq_ref[part] = (jnp.concatenate(dqs, axis=1) * HEAD ** -0.5).astype(BF16)
            fresh = False

    def write(ref, acc, scale, before):
        value = jnp.concatenate([(acc[h * PAD : h * PAD + HEAD] * scale).T for h in range(heads)], axis=1)
        ref[...] = (value if before is None else value + before[...].astype(F32)).astype(BF16)

    write(dk_ref, dk_acc, 1 / LOG2E, before[0])
    write(dv_ref, dv_acc, 1.0, before[1])


def attend_backward(k, v, items, heads, before=(), tokens=()):
    length = k.shape[0]
    block, span = items[0][4].shape[-2:]
    whole, rows = _shape((length, span)), _shape((block, span))
    specs, operands = [], []
    for q, first, context, context_at, do, do_at in items:
        specs += [_row(block, heads * PAD, first), _entry(context, context_at), _entry(do, do_at)]
        operands += [q, context, do]
    count = len(items)
    return pl.pallas_call(
        functools.partial(backward_kernel, heads, min(256, block), count, len(before) > 0),
        grid=(1,),
        in_specs=[_whole(k), _whole(v)] + specs + [_whole(a) for a in before] + _unread(tokens),
        out_specs=[_whole(rows)] * count + [_whole(whole)] * 2,
        out_shape=[rows] * count + [whole] * 2,
        scratch_shapes=[pltpu.VMEM((heads * PAD, length), F32)] * 2,
        compiler_params=_params(16),
        cost_estimate=_cost(40 * heads * count * block * length * HEAD, 8 << 20, heads * count * block * length),
        name="attend_backward",
    )(k, v, *operands, *before, *tokens)


def _gelu(first):
    cumulative = 0.5 * (1.0 + lax.erf(first * 0.5 ** 0.5))
    density = jnp.exp(-0.5 * first * first) * 0.3989422804014327
    return first * cumulative, cumulative + first * density


def feed_kernel(share, group, here, x_ref, cot_ref, own_ref, near_ref, far_ref, diag_ref, w_ref, result_ref, back_ref, grad0, grad1, grad2, *refs):
    kept, sent = refs[:2], refs[2:4]
    ctx_all, n2_all, hidden_all, gates_all, branch_all, attn_scr, in_scr, out_scr, attn_grad, sems = refs[4:]
    rows, width = x_ref.shape
    owners, hidden_share = out_scr.shape[:2]
    hidden_size = owners * hidden_share
    span = width // group
    blocks = in_scr.shape[0]
    step = pl.program_id(0)
    at = pl.ds(pl.multiple_of(step * rows, rows), rows)
    copies = []
    for g in range(group):
        if owners % group == 0:
            each = owners // group
            source, target = w_ref.at[pl.ds((here[0] ^ g) * each, each), :share], attn_scr.at[pl.ds(g * each, each)]
        else:
            source = w_ref.at[:, pl.ds(pl.multiple_of((here[0] ^ g) * span, span), span)]
            target = attn_scr.at[:, pl.ds(g * span, span)]
        copies.append(pltpu.make_async_copy(source, target, sems.at[g]))
    for c in range(blocks):
        copies.append(pltpu.make_async_copy(w_ref.at[:, share * (1 + c) : share * (2 + c)], in_scr.at[c], sems.at[group + c]))
    first_out = share * (1 + blocks)
    copies.append(pltpu.make_async_copy(w_ref.at[:, first_out : first_out + hidden_share], out_scr, sems.at[group + blocks]))

    @pl.when(step == 0)
    def _():
        for copy in copies:
            copy.start()
        for copy in copies[:group]:
            copy.wait()

    ctx = jnp.concatenate([own_ref[...], near_ref[...], far_ref[...], diag_ref[...]], axis=1)
    ctx_all[at] = ctx
    w_attn = attn_scr[...].reshape(width, width)
    attended = x_ref[...].astype(F32) + _dot(ctx, w_attn, 1, 0)
    hat, scale = _normalize(attended)
    n2 = hat.astype(BF16)
    n2_all[at] = n2

    @pl.when(step == 0)
    def _():
        for copy in copies[group:]:
            copy.wait()

    w_in = [in_scr[c].reshape(width, width) for c in range(blocks)]
    w_out = out_scr[...].reshape(hidden_size, width)
    gate_up = jnp.concatenate([_dot(n2, w, 1, 0) for w in w_in], axis=1)
    first, second = gate_up[:, :hidden_size], gate_up[:, hidden_size:]
    gelu, slope = _gelu(first)
    hidden = (gelu * second).astype(BF16)
    hidden_all[at] = hidden
    result_ref[0] = (attended + _dot(hidden, w_out, 1, 0)).astype(BF16)
    cot = cot_ref[at]
    hidden_back = _dot(cot, w_out, 1, 1)
    gates = jnp.concatenate([hidden_back * second * slope, hidden_back * gelu], axis=1).astype(BF16)
    gates_all[at] = gates
    back = sum(_dot(gates[:, c * width : (c + 1) * width], w, 1, 1) for c, w in enumerate(w_in))
    back = cot.astype(F32) + _norm_back(back, hat, scale)
    back_ref[...] = back
    branch = back.astype(BF16)
    branch_all[at] = branch
    grads = _dot(branch, w_attn, 1, 1).astype(BF16)
    grad0[...] = grads[:, :span]
    grad1[...] = grads[:, span : 2 * span]
    grad2[0] = grads[:, 2 * span : 3 * span]
    grad2[1] = grads[:, 3 * span :]

    cut = kept[0].shape[1]
    half = cut + kept[1].shape[1]
    core = here[0] & 1

    def place(value, start, size):
        value = value.reshape(owners, size, width).astype(BF16)
        for side in range(2):
            for g, (lower, upper) in enumerate(((0, cut), (cut, half))):
                lower, upper = side * half + lower, side * half + upper
                lo, hi = max(start, lower), min(start + size, upper)
                if lo < hi:
                    part = value[:, lo - start : hi - start]
                    rows_at = slice(lo - lower, hi - lower)

                    @pl.when(core == side)
                    def _(part=part, rows_at=rows_at, g=g):
                        kept[g][:, rows_at] = part

                    @pl.when(core != side)
                    def _(part=part, rows_at=rows_at, g=g):
                        sent[g][:, rows_at] = part

    @pl.when(step == pl.num_programs(0) - 1)
    def _():
        attn = _dot(ctx_all[...], branch_all[...], 0, 0)
        for g in range(group):
            spot = pl.multiple_of((here[0] ^ g) * span, span)
            attn_grad[pl.ds(spot, span)] = attn[g * span : (g + 1) * span]
        place(attn_grad[...], 0, share)
        n2_whole = n2_all[...]
        for c in range(blocks):
            place(_dot(n2_whole, gates_all[:, c * width : (c + 1) * width], 0, 0), share * (1 + c), share)
        place(_dot(hidden_all[...], cot_ref[...], 0, 0), first_out, hidden_share)
        last = first_out + hidden_share
        if last < 2 * half:
            place(jnp.zeros((owners * (2 * half - last), width), F32), last, 2 * half - last)


def feed(here, x, cot, own, near, far, diag, packed, share, hidden_size, half, cut, block=256):
    rows, width = x.shape
    span = own.shape[1]
    group = width // span
    blocks = 2 * hidden_size // width
    owners = packed.shape[0]
    lead = lambda n, lead_width: pl.BlockSpec((n, block, lead_width), lambda i, *_: (0, i, 0))
    half_at = lambda at: pl.BlockSpec((None, block, span), lambda i, *_: (at, i, 0))
    parts = [_shape((owners, cut, width)), _shape((owners, half - cut, width))] * 2
    return pl.pallas_call(
        functools.partial(feed_kernel, share, group),
        grid_spec=pltpu.PrefetchScalarGridSpec(
            num_scalar_prefetch=1,
            grid=(rows // block,),
            in_specs=[_row(block, width), _whole(cot), _row(block, span), _row(block, span), half_at(0), half_at(1), pl.BlockSpec(memory_space=pltpu.HBM)],
            out_specs=[lead(1, width), _row(block, width), _row(block, span), _row(block, span), lead(2, span)] + [_whole(p) for p in parts],
            scratch_shapes=[pltpu.VMEM((rows, n), BF16) for n in (width, width, hidden_size, 2 * hidden_size, width)]
            + [
                pltpu.VMEM((owners, share, width), BF16),
                pltpu.VMEM((blocks, owners, share, width), BF16),
                pltpu.VMEM((owners, hidden_size // owners, width), BF16),
                pltpu.VMEM((width, width), F32),
                pltpu.SemaphoreType.DMA((group + blocks + 1,)),
            ],
        ),
        out_shape=[_shape((1, rows, width)), _shape((rows, width), F32), _shape((rows, span)), _shape((rows, span)), _shape((2, rows, span))] + parts,
        compiler_params=_params(36),
        cost_estimate=_cost(6 * rows * width * (width + 3 * hidden_size), 20 << 20, 2 * rows * hidden_size),
        name="feed",
    )(here, x, cot, own, near, far, diag, packed)


def qkv_grads_kernel(heads, tokens, places, *refs):
    dqs, (dk_ref, dv_ref, table_ref, normed_ref), refs = refs[:4], refs[4:8], refs[8:]
    grads_ref, kept_ref, sent_ref, acc = refs[tokens:]
    step = pl.program_id(0)

    @pl.when(step == 0)
    def _():
        acc[...] = jnp.zeros_like(acc)

    cos, sin = _tables(table_ref, heads)
    dq = dqs[0][...].astype(F32)
    for j in range(1, 4):
        dq = jnp.where(step == j, dqs[j][...].astype(F32), dq)
    qk = jnp.concatenate([dq, dk_ref[...].astype(F32)], axis=1)
    qk = (qk * cos - _half_turn(qk) * sin).astype(BF16)
    grads = jnp.concatenate([qk, dv_ref[...]], axis=1)
    grads_ref[...] = grads
    acc[...] += _dot(normed_ref[...], grads, 0, 0)

    @pl.when(step == pl.num_programs(0) - 1)
    def _():
        pairs, share = kept_ref.shape[:2]
        for i in range(2 * pairs):
            part = acc[i * share : (i + 1) * share].astype(BF16)

            @pl.when((places[1] & 1) == i % 2)
            def _(part=part, i=i):
                kept_ref[i // 2] = part

            @pl.when((places[1] & 1) != i % 2)
            def _(part=part, i=i):
                sent_ref[i // 2] = part


def qkv_grads(places, dqs, dk, dv, table, normed, heads, block, owners, tokens=()):
    length, width = normed.shape
    span = heads * HEAD
    half = _shape((owners // 2, width // owners, 3 * span))
    return pl.pallas_call(
        functools.partial(qkv_grads_kernel, heads, len(tokens)),
        grid_spec=pltpu.PrefetchScalarGridSpec(
            num_scalar_prefetch=1,
            grid=(length // block,),
            in_specs=[_whole(dqs[0])] * 4
            + [_row(block, span)] * 2
            + [_row(block, table.shape[1])]
            + [_row(block, width)]
            + _unread(tokens),
            out_specs=[_row(block, 3 * span), _whole(half), _whole(half)],
            scratch_shapes=[pltpu.VMEM((width, 3 * span), F32)],
        ),
        out_shape=[_shape((length, 3 * span)), half, half],
        compiler_params=_params(12),
        cost_estimate=_cost(2 * length * width * 3 * span, 8 << 20),
        name="qkv_grads",
    )(places, *dqs, dk, dv, table, normed, *tokens)


def input_back_kernel(grads_ref, w_ref, *refs):
    kept_ref, sent_ref = refs[-2:]
    back = _dot(grads_ref[...], w_ref[...], 1, 1).astype(BF16)

    @pl.when(pl.program_id(0) % 2 == 0)
    def _():
        kept_ref[0] = back

    @pl.when(pl.program_id(0) % 2 == 1)
    def _():
        sent_ref[0] = back


def input_back(grads, w, block, tokens=()):
    length, columns = grads.shape
    width = w.shape[0]
    spec = pl.BlockSpec((1, block, width), lambda i: (i // 2, 0, 0))
    return pl.pallas_call(
        input_back_kernel,
        grid=(length // block,),
        in_specs=[_row(block, columns), _whole(w)] + _unread(tokens),
        out_specs=[spec, spec],
        out_shape=[_shape((length // block // 2, block, width))] * 2,
        compiler_params=_params(8),
        cost_estimate=_cost(2 * length * width * columns, 6 << 20),
        name="input_back",
    )(grads, w, *tokens)


def combine_kernel(counts, *refs):
    out, at, first = refs[-1], 0, 0
    for count in counts:
        part = sum(ref[...].astype(F32) for ref in refs[at : at + count]).astype(BF16)
        out[first : first + part.shape[0]] = part
        at, first = at + count, first + part.shape[0]


def combine(groups, tokens=()):
    flat = [pair for group in groups for pair in group]
    rows = sum(group[0][0].shape[-2] for group in groups)
    out = _shape((rows, flat[0][0].shape[-1]))
    return pl.pallas_call(
        functools.partial(combine_kernel, [len(group) for group in groups]),
        grid=(1,),
        in_specs=[_entry(*pair) for pair in flat] + _unread(tokens),
        out_specs=_whole(out),
        out_shape=out,
        compiler_params=_params(8),
        name="combine",
    )(*[array for array, _ in flat], *tokens)


def join_kernel(a_ref, b_ref, out_ref):
    count = a_ref.shape[0]
    out_ref[:count] = a_ref[...]
    out_ref[count:] = b_ref[...]


def join(a, b):
    whole = pl.BlockSpec(memory_space=pltpu.VMEM)
    return pl.pallas_call(
        join_kernel,
        in_specs=[whole, whole],
        out_specs=whole,
        out_shape=_shape((a.shape[0] + b.shape[0],) + a.shape[1:]),
        compiler_params=_params(8),
        name="join",
    )(a, b)


def _pick(here, blocks, group):
    value = blocks[0]
    for j in range(1, len(blocks)):
        value = jnp.where((here ^ group) == j, blocks[j], value)
    return value


def _row_sums(value):
    folded = sum(value[:, at : at + PAD] for at in range(0, value.shape[1], PAD))
    return jnp.sum(folded.T, axis=0, keepdims=True)


def finish_qkv_kernel(here, b0, b1, b2, b3, weight_ref, gain_ref, grad_ref, gain_grad_ref):
    blocks = [b[...].astype(F32) for b in (b0, b1, b2, b3)]
    ordered = [_pick(here[0], blocks, g) for g in range(4)]
    span = b0.shape[1] // 3
    summed = jnp.concatenate([o[:, c * span : (c + 1) * span] for c in range(3) for o in ordered], axis=1)
    gain_grad_ref[...] = _row_sums(weight_ref[...].astype(F32) * summed)
    grad_ref[...] = summed * gain_ref[...].astype(F32)


def finish_feed_kernel(here, b0, b1, b2, b3, weight_ref, gain_ref, attn_ref, in_ref, gain_grad_ref, out_ref):
    share, width = attn_ref.shape
    half = b0.shape[0]
    blocks = [b[...].astype(F32) for b in (b0, b1, b2, b3)]
    ordered = [_pick(here[0], blocks, g) for g in range(4)]
    rows = jnp.concatenate([jnp.concatenate([ordered[core], ordered[2 + core]], axis=1) for core in range(2)], axis=0)
    attn_ref[...] = rows[:share]
    count = in_ref.shape[1] // width
    summed = jnp.concatenate([rows[share * (1 + c) : share * (2 + c)] for c in range(count)], axis=1)
    gain_grad_ref[...] = _row_sums(weight_ref[...].astype(F32) * summed)
    in_ref[...] = summed * gain_ref[...].astype(F32)
    first = share * (1 + count)
    out_ref[...] = rows[first : first + out_ref.shape[0]]


def finish(kernel, name, here, blocks, weight, gain, shapes):
    whole = pl.BlockSpec(memory_space=pltpu.VMEM)
    return pl.pallas_call(
        kernel,
        in_specs=[pl.BlockSpec(memory_space=pltpu.SMEM)] + [whole] * 6,
        out_specs=[whole] * len(shapes),
        out_shape=[_shape(s, F32) for s in shapes],
        compiler_params=_params(8),
        name=name,
    )(here, *blocks, weight, gain)


def input_grad_kernel(x_ref, direct_ref, kept_ref, near_ref, far_ref, out_ref, done_ref):
    done_ref[...] = jnp.zeros_like(done_ref)
    hat, scale = _normalize(x_ref[...].astype(F32))
    back = kept_ref[0].astype(F32) + near_ref[0].astype(F32) + far_ref[...].astype(F32)
    out_ref[0] = (direct_ref[...] + _norm_back(back, hat, scale)).astype(BF16)


def input_grad(x, direct, kept, near, far, block=256):
    rows, width = x.shape
    lead = pl.BlockSpec((1, block, width), lambda i: (0, i, 0))
    return pl.pallas_call(
        input_grad_kernel,
        grid=(rows // block,),
        in_specs=[_row(block, width), _row(block, width), lead, lead, _row(block, width)],
        out_specs=[lead, _whole(_shape((8, PAD)))],
        out_shape=[_shape((1, rows, width)), _shape((8, PAD), F32)],
        compiler_params=_params(8),
        name="input_grad",
    )(x, direct, kept, near, far)


def halve_pair_kernel(columns, axis, bit, places, a_ref, b_ref, *refs):
    kept_ref, sent_ref = refs[-2:]
    own = (places[axis] >> bit) & 1
    if columns:
        half = a_ref.shape[2] // 2
        for side in range(2):
            at = slice(side * half, (side + 1) * half)
            part = (a_ref[:, :, at].astype(F32) + b_ref[:, :, at].astype(F32)).astype(BF16)

            @pl.when(own == side)
            def _(part=part):
                kept_ref[...] = part

            @pl.when(own != side)
            def _(part=part):
                sent_ref[...] = part

    else:
        for i in range(kept_ref.shape[0]):
            for ref, side in ((kept_ref, own), (sent_ref, 1 - own)):
                at = 2 * i + side
                ref[i] = (a_ref[at].astype(F32) + b_ref[at].astype(F32)).astype(BF16)


def halve_pair(places, axis, bit, a, b, columns=False, tokens=()):
    n, rows, width = a.shape
    half = _shape((n, rows, width // 2) if columns else (n // 2, rows, width))
    whole = pl.BlockSpec(memory_space=pltpu.VMEM)
    return pl.pallas_call(
        functools.partial(halve_pair_kernel, columns, axis, bit),
        in_specs=[pl.BlockSpec(memory_space=pltpu.SMEM), whole, whole] + _unread(tokens),
        out_specs=[whole, whole],
        out_shape=[half, half],
        compiler_params=_params(8),
        name="halve_pair",
    )(places, a, b, *tokens)


def relay_kernel(value_ref, *refs):
    refs[-1][...] = value_ref[...]


def relay(value, *tokens, late=()):
    whole = pl.BlockSpec(memory_space=pltpu.VMEM)
    return pl.pallas_call(
        relay_kernel,
        in_specs=[whole] + _unread(tokens) + [pl.BlockSpec(memory_space=pltpu.HBM) for _ in late],
        out_specs=whole,
        out_shape=_shape(value.shape, value.dtype),
        compiler_params=_params(8),
        name="relay",
    )(value, *tokens, *late)


def exchange(value, axis, distance):
    size = lax.axis_size(axis)
    return lax.ppermute(value, axis, [(i, i ^ distance) for i in range(size)])


def gather_halves(piece, axis, token):
    size = lax.axis_size(axis)
    pieces = piece[None]
    distance = size // 2
    while distance > 1:
        pieces = join(pieces, exchange(pieces, axis, distance))
        if distance == size // 2:
            pieces = relay(pieces, token)
        distance //= 2
    other = exchange(pieces, axis, 1)
    return pieces, other


def halve(addends, axis, bit, take):
    own = (lax.axis_index(axis) >> bit) & 1
    sent = sum(take(a, 1 - own).astype(F32) for a in addends).astype(BF16)
    return [take(a, own) for a in addends] + [exchange(sent, axis, 1 << bit)]


def split_owners(addends, axis):
    bits = lax.axis_size(axis).bit_length() - 1
    return [a.reshape((2,) * bits + a.shape[1:]) for a in addends]


def halve_owners(addends, axis, bit):
    dim = lax.axis_size(axis).bit_length() - 2 - bit
    return halve(addends, axis, bit, lambda a, at: lax.dynamic_index_in_dim(a, at, dim, keepdims=False))


def scatter_rows(addends, axis, first=0):
    for bit in range(first, lax.axis_size(axis).bit_length() - 1):
        addends = halve_owners(addends, axis, bit)
    return addends


def total(addends):
    return sum(a.astype(F32) for a in addends)


ROPE_BASE = 160000.0


def rope_tables(places):
    half = HEAD // 2
    inverse = ROPE_BASE ** (-(jnp.arange(half, dtype=F32) * 2.0 / HEAD))
    angles = places[:, None] * inverse[None, :]
    cosine, sine = lax.optimization_barrier((jnp.cos(angles), jnp.sin(angles)))
    return jnp.concatenate([cosine, cosine, sine, sine], axis=1), sine


def from_slices(block):
    far = exchange(block, "seq", 2)
    return [block, exchange(block, "seq", 1), far, exchange(far, "seq", 1)]


def step(places, pair, axis, bit, columns=False, tokens=()):
    kept, sent = halve_pair(places, ("seq", "fsdp").index(axis), bit, *pair, columns, tokens)
    return [kept, exchange(sent, axis, 1 << bit)]


def in_order(blocks, here):
    stacked = jnp.stack(blocks)
    return [lax.dynamic_index_in_dim(stacked, here ^ i, 0, keepdims=False) for i in range(len(blocks))]


def up16(n):
    return -(-n // 16) * 16


def body(
    inputs,
    norm_one,
    qkv_weight,
    attn_out_weight,
    norm_two,
    mlp_in_weight,
    mlp_out_weight,
    cotangent,
):
    here = lax.axis_index("seq")
    slices = lax.axis_size("seq")
    owners = lax.axis_size("fsdp")
    heads = HEADS // slices
    span = heads * HEAD
    rows, width = inputs.shape[1:]
    share = qkv_weight.shape[0]
    hidden_share = mlp_out_weight.shape[0]
    hidden_size = hidden_share * owners
    blocks = 2 * hidden_size // width
    aligned = share % 16 == 0 and hidden_share % 16 == 0
    owner = lax.axis_index("fsdp")
    places = lax.optimization_barrier(jnp.stack([here, owner]).astype(jnp.int32))
    spot = places

    x = inputs[0]
    scaled_qkv = (qkv_weight.astype(F32) * norm_one.astype(F32)[:, None]).astype(BF16)
    scaled_in = (mlp_in_weight.astype(F32) * norm_two.astype(F32)[:, None]).astype(BF16)
    x_far = exchange(x, "seq", 2)
    own_columns = jnp.concatenate(
        [lax.dynamic_slice_in_dim(scaled_qkv, c * width + here * span, span, 1) for c in range(3)], axis=1
    )
    order = here ^ jnp.arange(slices)
    positions = (order[:, None] * rows + jnp.arange(rows)[None, :]).reshape(-1).astype(F32)
    table, sine = rope_tables(positions)
    even, odd = gather_halves(own_columns, "fsdp", sine)
    x_far = relay(x_far, even)
    xs = [x, exchange(x, "seq", 1), x_far, exchange(x_far, "seq", 1)]
    if not aligned:
        bits = owners.bit_length() - 1
        distance = owner ^ jnp.arange(owners)
        spots = sum(((distance >> bit) & 1) << (bits - 1 - bit) for bit in range(bits))
        pieces = jnp.concatenate([even, odd], axis=0)
        even = jnp.take(pieces, spots, axis=0).reshape(1, width, 3 * span)
        odd = even

    shard = [attn_out_weight] + [scaled_in[:, c * width : (c + 1) * width] for c in range(blocks)] + [mlp_out_weight]
    shard_rows = share * (1 + blocks) + hidden_share
    part = -(-shard_rows // (8 * slices)) * 8
    shard = jnp.concatenate(shard + [jnp.zeros((part * slices - shard_rows, width), BF16)], axis=0)
    packed = lax.all_gather(lax.dynamic_slice_in_dim(shard, here * part, part, 0), ("fsdp", "seq"), axis=0, tiled=True)
    packed = packed.reshape(owners, part * slices, width)
    packed_share = share
    if not aligned:
        cuts = [share * c for c in range(2 + blocks)] + [shard_rows]
        packed = jnp.concatenate([packed[:, a:b].reshape(-1, width) for a, b in zip(cuts, cuts[1:])], axis=0)[None]
        packed_share = width

    w_qkv, normed_all, query, key, value = project(places, xs, even, odd, table, heads)
    context_23, query_far = attend_forward(query, key, value, heads, rows, 2, True)
    from_2 = exchange(context_23, "seq", 2)
    context_0, context_1, query_near = attend_forward(query, key, value, heads, rows, 0, False)
    from_1 = exchange(context_1, "seq", 1)
    from_2 = relay(from_2, context_0, late=(packed,))
    from_3 = exchange(from_2, "seq", 1)

    cot = cotangent[0]
    grad_rows = up16(-(-shard_rows // 2))
    cut = up16(grad_rows // 2)
    packed_rows = packed_share * (1 + blocks) + hidden_size // packed.shape[0]
    cuts = (grad_rows, cut) if aligned else (packed_rows // 2, packed_rows // 4)
    result, attended_grad, grad0, grad1, grad23, *mlp_grads = feed(
        spot, x, cot, context_0, from_1, from_2, from_3, packed, packed_share, hidden_size, *cuts
    )
    grad23 = exchange(grad23, "seq", 2)
    grad1 = exchange(grad1, "seq", 1)
    grad3 = exchange(grad23, "seq", 1)

    kept_one, kept_two, sent_one, sent_two = mlp_grads
    if not aligned:
        core = here & 1
        kept, sent = jnp.concatenate(mlp_grads[:2], axis=1), jnp.concatenate(mlp_grads[2:], axis=1)
        both = jnp.where(core == 0, jnp.concatenate([kept, sent], axis=1), jnp.concatenate([sent, kept], axis=1))[0]
        edges = [width * c for c in range(2 + blocks)] + [packed_rows]
        both = jnp.concatenate([both[a:b].reshape(owners, -1, width) for a, b in zip(edges, edges[1:])], axis=1)
        both = jnp.pad(both, ((0, 0), (0, 2 * grad_rows - shard_rows), (0, 0)))
        kept = lax.dynamic_slice_in_dim(both, core * grad_rows, grad_rows, 1)
        sent = lax.dynamic_slice_in_dim(both, (1 - core) * grad_rows, grad_rows, 1)
        kept_one, kept_two, sent_one, sent_two = kept[:, :cut], kept[:, cut:], sent[:, :cut], sent[:, cut:]
    one = [kept_one, exchange(sent_one, "seq", 1)]
    two = [kept_two, exchange(sent_two, "seq", 1)]

    dq_0, *back = attend_backward(key, value, [(query_near, 0, context_0, None, grad0, None)], heads)
    tokens = (one[1], two[1])
    one = step(places, one, "seq", 1, columns=True, tokens=(dq_0,))
    two = step(places, two, "fsdp", 0, tokens=(dq_0,))
    dq_1, dq_2, *back = attend_backward(
        key, value, [(query_near, 1, context_1, None, grad1, None), (query_far, 0, context_23, 0, grad23, 0)],
        heads, back, tokens,
    )
    tokens = (one[1], two[1])
    one = step(places, one, "fsdp", 0, tokens=(dq_1,))
    two = step(places, two, "fsdp", 1, tokens=(dq_1,))
    dq_3, *back = attend_backward(key, value, [(query_far, 1, context_23, 1, grad3, 1)], heads, back, tokens)
    tokens = (one[1], two[1])
    one = step(places, one, "fsdp", 1, tokens=(dq_3,))
    two = step(places, two, "fsdp", 2, tokens=(dq_3,))
    qkv_back, qkv_kept, qkv_sent = qkv_grads(
        places, (dq_0, dq_1, dq_2, dq_3), *back, table, normed_all, heads, rows,
        owners if aligned else 2, tokens=tokens
    )
    back_kept, back_sent = input_back(qkv_back, w_qkv, rows, tokens=(one[1], two[1]))
    bits = owners.bit_length() - 1
    for bit in range(2, bits):
        one = step(places, one, "fsdp", bit)
    for bit in range(3, bits):
        two = step(places, two, "fsdp", bit)
    two = step(places, two, "seq", 1, columns=True)
    if aligned:
        qkv = [qkv_kept, exchange(qkv_sent, "fsdp", 1)]
        qkv = step(places, qkv, "fsdp", 1, tokens=(back_kept, one[1]))
        for bit in range(2, bits):
            qkv = step(places, qkv, "fsdp", bit)
    else:
        side = owner & 1
        qkv = jnp.where(side == 0, jnp.concatenate([qkv_kept, qkv_sent]), jnp.concatenate([qkv_sent, qkv_kept]))
        qkv = scatter_rows(split_owners([qkv.reshape(owners, share, 3 * span)], "fsdp"), "fsdp")
    mlp_part = combine([[(a, 0) for a in one], [(a, 0) for a in two]], tokens=(qkv[1],))
    back_near = exchange(back_sent, "seq", 1)
    back_far = exchange(combine([[(back_kept, 1), (back_near, 1)]], tokens=(two[1],)), "seq", 2)
    input_gradient, input_done = input_grad(x, attended_grad, back_kept, back_near, back_far)
    mlp_blocks = from_slices(mlp_part)
    gain_one, gain_two = norm_one[:, None], norm_two[:, None]
    if aligned:
        attn_gradient, in_gradient, gain_grad2, out_gradient = finish(
            finish_feed_kernel, "finish_feed", spot, mlp_blocks, mlp_in_weight, gain_two,
            ((share, width), (share, 2 * hidden_size), (1, share), (hidden_share, width)),
        )
        qkv_blocks = from_slices(combine([[(a, 0) for a in qkv]], tokens=(input_done,)))
        qkv_gradient, gain_grad1 = finish(
            finish_qkv_kernel, "finish_qkv", spot, qkv_blocks, qkv_weight, gain_one, ((share, 3 * width), (1, share))
        )
    else:
        qkv_blocks = from_slices(total(qkv).astype(BF16))
        ordered = in_order(qkv_blocks, here)
        summed = jnp.concatenate(
            [b[:, c * span : (c + 1) * span] for c in range(3) for b in ordered], axis=1
        ).astype(F32)
        gain_grad1 = jnp.sum(qkv_weight.astype(F32) * summed, axis=1)
        qkv_gradient = summed * gain_one.astype(F32)
        ordered = in_order(mlp_blocks, here)
        summed = jnp.concatenate(
            [jnp.concatenate([ordered[core], ordered[2 + core]], axis=1) for core in range(2)], axis=0
        ).astype(F32)
        attn_gradient = summed[:share]
        first_out = share * (1 + blocks)
        out_gradient = summed[first_out : first_out + hidden_share]
        summed = jnp.concatenate([summed[share * (1 + c) : share * (2 + c)] for c in range(blocks)], axis=1)
        gain_grad2 = jnp.sum(mlp_in_weight.astype(F32) * summed, axis=1)
        in_gradient = summed * gain_two.astype(F32)
    return (
        result,
        input_gradient,
        gain_grad1.reshape(share),
        qkv_gradient,
        attn_gradient,
        gain_grad2.reshape(share),
        in_gradient,
        out_gradient,
    )


def solution(mesh):
    tokens = P("fsdp", "seq", None)
    vector = P("fsdp")
    matrix = P("fsdp", None)
    return jax.shard_map(
        body,
        mesh=mesh,
        in_specs=(tokens, vector, matrix, matrix, vector, matrix, matrix, tokens),
        out_specs=(tokens, tokens, vector, matrix, matrix, vector, matrix, matrix),
        check_vma=False,
    )
```

```python
import functools
import jax, jax.numpy as jnp
from jax import lax
from jax.experimental import pallas as pl
from jax.experimental.pallas import tpu as pltpu

from jax.sharding import PartitionSpec as P

HEADS = 12
HEAD = 64
PAD = 128
EPSILON = 1e-05
MIB = 1 << 20
LOG2E = 1.4426950408889634
F32 = jnp.float32
BF16 = jnp.bfloat16


def _dot(a, b, ca, cb):
    return lax.dot_general(a, b, (((ca,), (cb,)), ((), ())), preferred_element_type=F32)


def _normalize(values):
    centred = values - jnp.mean(values, axis=1, keepdims=True)
    variance = jnp.mean(centred * centred, axis=1, keepdims=True)
    scale_inv = lax.rsqrt(variance + EPSILON)
    return centred * scale_inv, scale_inv


def _norm_back(grad_hat, normed, scale_inv):
    return scale_inv * (
        grad_hat
        - jnp.mean(grad_hat, axis=1, keepdims=True)
        - normed * jnp.mean(grad_hat * normed, axis=1, keepdims=True)
    )


def _tables(table_ref, heads):
    spread = lambda part: jnp.concatenate([part] * (2 * heads), axis=1)
    return spread(table_ref[:, :HEAD]), spread(table_ref[:, HEAD:])


def _half_turn(v):
    lane = lax.broadcasted_iota(jnp.int32, v.shape, 1)
    ahead = -pltpu.roll(v, v.shape[1] - HEAD // 2, 1)
    behind = pltpu.roll(v, HEAD // 2, 1)
    return jnp.where(lane % HEAD < HEAD // 2, ahead, behind)


def _parts(v):
    high = v.astype(BF16)
    rest = v - high.astype(F32)
    mid = rest.astype(BF16)
    low = (rest - mid.astype(F32)).astype(BF16)
    return high, mid, low


def _with_parts(base, v):
    rows = base.shape[0]
    high, mid, low = _parts(v)
    lane = lax.broadcasted_iota(jnp.int32, (rows, PAD - HEAD), 1)
    f = lambda p: p.astype(F32)
    tail = jnp.where(lane == 0, f(high), jnp.where(lane == 1, f(mid), jnp.where(lane == 2, f(low), 0.0)))
    return jnp.concatenate([base[:, :HEAD], tail.astype(BF16)], axis=1)


def _params(mib):
    return pltpu.CompilerParams(vmem_limit_bytes=mib * MIB)


def _row(block, n, first=0):
    return pl.BlockSpec((block, n), lambda i, *_: (i + first, 0))


def _whole(a):
    rank = len(a.shape)
    return pl.BlockSpec(a.shape, lambda i, *_: (0,) * rank)


def _entry(array, at):
    if at is None:
        return _whole(array)
    return pl.BlockSpec((None,) + array.shape[1:], lambda i, *_: (at,) + (0,) * (len(array.shape) - 1))


def _unread(tokens):
    return [pl.BlockSpec(memory_space=pl.ANY) for _ in tokens]


def _shape(shape, dtype=BF16):
    return jax.ShapeDtypeStruct(shape, dtype)


def _cost(flops, size, transcendentals=0):
    return pl.CostEstimate(flops=int(flops), bytes_accessed=int(size), transcendentals=int(transcendentals))


def _reversed_bits(value, size):
    bits = size.bit_length() - 1
    return sum((((value >> bit) & 1) << (bits - 1 - bit) for bit in range(bits)), jnp.int32(0))


def project_kernel(heads, places, x0, x1, x2, x3, even_ref, odd_ref, table_ref, w_ref, normed_ref, q_ref, k_ref, v_ref, x_scr):
    step = pl.program_id(0)
    owners = w_ref.shape[0] // even_ref.shape[1]
    share = even_ref.shape[1]

    @pl.when(step == 0)
    def _():
        for i in range(owners):
            at = slice(i * share, (i + 1) * share)
            spot = _reversed_bits(places[1] ^ i, owners)
            if owners == 1:
                w_ref[at] = even_ref[0]
            else:
                half = owners // 2

                @pl.when(spot < half)
                def _():
                    w_ref[at] = even_ref[spot]

                @pl.when(spot >= half)
                def _():
                    w_ref[at] = odd_ref[spot - half]

    for j, ref in enumerate((x0, x1, x2, x3)):

        @pl.when(step == j)
        def _(ref=ref):
            x_scr[...] = ref[...]

    normed = _normalize(x_scr[...].astype(F32))[0].astype(BF16)
    normed_ref[...] = normed
    qkv = _dot(normed, w_ref[...], 1, 0)
    span = heads * HEAD
    qk = qkv[:, : 2 * span]
    cos, sin = _tables(table_ref, heads)
    qk = qk * cos + _half_turn(qk) * sin
    rows = x0.shape[0]
    zeros = jnp.zeros((rows, PAD - HEAD), BF16)
    ones = jnp.where(lax.broadcasted_iota(jnp.int32, (rows, PAD - HEAD), 1) < 3, 1.0, 0.0).astype(BF16)
    for h in range(heads):
        at = slice(h * PAD, (h + 1) * PAD)
        lo = h * HEAD
        q_ref[:, at] = jnp.concatenate([(qk[:, lo : lo + HEAD] * (LOG2E * HEAD ** -0.5)).astype(BF16), zeros], axis=1)
        k_ref[:, at] = jnp.concatenate([qk[:, span + lo : span + lo + HEAD].astype(BF16), ones], axis=1)
        v_ref[:, at] = jnp.concatenate([qkv[:, 2 * span + lo : 2 * span + lo + HEAD].astype(BF16), ones], axis=1)


def project(places, xs, even, odd, table, heads):
    rows, width = xs[0].shape
    length = rows * len(xs)
    columns = even.shape[2]
    w_shape = _shape((width, columns))
    return pl.pallas_call(
        functools.partial(project_kernel, heads),
        grid_spec=pltpu.PrefetchScalarGridSpec(
            num_scalar_prefetch=1,
            grid=(len(xs),),
            in_specs=[_whole(x) for x in xs] + [_whole(even), _whole(odd), _row(rows, table.shape[1])],
            out_specs=[_whole(w_shape), _row(rows, width)] + [_row(rows, heads * PAD)] * 3,
            scratch_shapes=[pltpu.VMEM((rows, width), BF16)],
        ),
        out_shape=[w_shape, _shape((length, width))] + [_shape((length, heads * PAD))] * 3,
        compiler_params=_params(12),
        cost_estimate=_cost(2 * length * width * columns, 12 << 20),
        name="project",
    )(places, *xs, even, odd, table)


def forward_kernel(heads, sub, q_ref, k_ref, v_ref, *refs):
    ctx_refs, qx_ref = refs[:-1], refs[-1]
    step = pl.program_id(0)
    for r in range(q_ref.shape[0] // sub):
        part = slice(r * sub, (r + 1) * sub)
        outs = []
        for h in range(heads):
            at = slice(h * PAD, (h + 1) * PAD)
            q = q_ref[part, at]
            scores = _dot(q, k_ref[:, at], 1, 1)
            top = jnp.max(scores, axis=1, keepdims=True)
            weights = jnp.exp2(scores - top).astype(BF16)
            sums = _dot(weights, v_ref[:, at], 1, 0)
            total = sums[:, HEAD : HEAD + 1]
            outs.append(sums[:, :HEAD] / total)
            qx_ref[part, at] = _with_parts(q, -(top + jnp.log2(total)))
        out = jnp.concatenate(outs, axis=1).astype(BF16)

        for j, ref in enumerate(ctx_refs):

            @pl.when((step == j) | (len(ctx_refs) == 1))
            def _(part=part, out=out, ref=ref):
                ref[part] = out


def attend_forward(q, k, v, heads, block, first, stacked):
    length = k.shape[0]
    span = heads * HEAD
    ctx = _shape((block, span))
    return pl.pallas_call(
        functools.partial(forward_kernel, heads, min(256, block)),
        grid=(2,),
        in_specs=[_row(block, heads * PAD, first), _whole(k), _whole(v)],
        out_specs=([pl.BlockSpec((None, block, span), lambda i: (i, 0, 0))] if stacked else [_whole(ctx)] * 2)
        + [_row(block, heads * PAD)],
        out_shape=([_shape((2, block, span))] if stacked else [ctx] * 2) + [_shape((2 * block, heads * PAD))],
        compiler_params=_params(10),
        cost_estimate=_cost(16 * heads * 2 * block * length * HEAD, 6 << 20, heads * 2 * block * length),
        name="attend_forward",
    )(q, k, v)


def backward_kernel(heads, sub, count, added, k_ref, v_ref, *refs):
    items = [refs[3 * i : 3 * i + 3] for i in range(count)]
    before = refs[3 * count : 3 * count + 2] if added else (None, None)
    dq_refs, (dk_ref, dv_ref, dk_acc, dv_acc) = refs[-4 - count : -4], refs[-4:]
    fresh = True
    for (q_ref, ctx_ref, do_ref), dq_ref in zip(items, dq_refs):
        do_all = do_ref[...]
        prod = do_all.astype(F32) * ctx_ref[...].astype(F32)
        for r in range(q_ref.shape[0] // sub):
            part = slice(r * sub, (r + 1) * sub)
            dqs = []
            for h in range(heads):
                at = slice(h * PAD, (h + 1) * PAD)
                lo = h * HEAD
                q, k, v = q_ref[part, at], k_ref[:, at], v_ref[:, at]
                delta = jnp.sum(prod[part, lo : lo + HEAD], axis=1, keepdims=True)
                do = _with_parts(do_all[part, lo : lo + HEAD], -delta)
                probs = jnp.exp2(_dot(q, k, 1, 1))
                back = _dot(do, v, 1, 1)
                score_back = (probs * back).astype(BF16)
                dv = _dot(do, probs.astype(BF16), 0, 0)
                dk = _dot(q, score_back, 0, 0)
                dv_acc[at] = dv if fresh else dv_acc[at] + dv
                dk_acc[at] = dk if fresh else dk_acc[at] + dk
                dqs.append(_dot(score_back, k, 1, 0)[:, :HEAD])
            dq_ref[part] = (jnp.concatenate(dqs, axis=1) * HEAD ** -0.5).astype(BF16)
            fresh = False

    def write(ref, acc, scale, before):
        value = jnp.concatenate([(acc[h * PAD : h * PAD + HEAD] * scale).T for h in range(heads)], axis=1)
        ref[...] = (value if before is None else value + before[...].astype(F32)).astype(BF16)

    write(dk_ref, dk_acc, 1 / LOG2E, before[0])
    write(dv_ref, dv_acc, 1.0, before[1])


def attend_backward(k, v, items, heads, before=(), tokens=()):
    length = k.shape[0]
    block, span = items[0][4].shape[-2:]
    whole, rows = _shape((length, span)), _shape((block, span))
    specs, operands = [], []
    for q, first, context, context_at, do, do_at in items:
        specs += [_row(block, heads * PAD, first), _entry(context, context_at), _entry(do, do_at)]
        operands += [q, context, do]
    count = len(items)
    return pl.pallas_call(
        functools.partial(backward_kernel, heads, min(256, block), count, len(before) > 0),
        grid=(1,),
        in_specs=[_whole(k), _whole(v)] + specs + [_whole(a) for a in before] + _unread(tokens),
        out_specs=[_whole(rows)] * count + [_whole(whole)] * 2,
        out_shape=[rows] * count + [whole] * 2,
        scratch_shapes=[pltpu.VMEM((heads * PAD, length), F32)] * 2,
        compiler_params=_params(16),
        cost_estimate=_cost(40 * heads * count * block * length * HEAD, 8 << 20, heads * count * block * length),
        name="attend_backward",
    )(k, v, *operands, *before, *tokens)


def _gelu(first):
    cumulative = 0.5 * (1.0 + lax.erf(first * 0.5 ** 0.5))
    density = jnp.exp(-0.5 * first * first) * 0.3989422804014327
    return first * cumulative, cumulative + first * density


def feed_kernel(share, group, here, x_ref, cot_ref, own_ref, near_ref, far_ref, diag_ref, w_ref, result_ref, back_ref, grad0, grad1, grad2, *refs):
    kept, sent = refs[:2], refs[2:4]
    ctx_all, n2_all, hidden_all, gates_all, branch_all, attn_scr, in_scr, out_scr, attn_grad, sems = refs[4:]
    rows, width = x_ref.shape
    owners, hidden_share = out_scr.shape[:2]
    hidden_size = owners * hidden_share
    span = width // group
    blocks = in_scr.shape[0]
    step = pl.program_id(0)
    at = pl.ds(pl.multiple_of(step * rows, rows), rows)
    copies = []
    for g in range(group):
        if owners % group == 0:
            each = owners // group
            source, target = w_ref.at[pl.ds((here[0] ^ g) * each, each), :share], attn_scr.at[pl.ds(g * each, each)]
        else:
            source = w_ref.at[:, pl.ds(pl.multiple_of((here[0] ^ g) * span, span), span)]
            target = attn_scr.at[:, pl.ds(g * span, span)]
        copies.append(pltpu.make_async_copy(source, target, sems.at[g]))
    for c in range(blocks):
        copies.append(pltpu.make_async_copy(w_ref.at[:, share * (1 + c) : share * (2 + c)], in_scr.at[c], sems.at[group + c]))
    first_out = share * (1 + blocks)
    copies.append(pltpu.make_async_copy(w_ref.at[:, first_out : first_out + hidden_share], out_scr, sems.at[group + blocks]))

    @pl.when(step == 0)
    def _():
        for copy in copies:
            copy.start()
        for copy in copies[:group]:
            copy.wait()

    ctx = jnp.concatenate([own_ref[...], near_ref[...], far_ref[...], diag_ref[...]], axis=1)
    ctx_all[at] = ctx
    w_attn = attn_scr[...].reshape(width, width)
    attended = x_ref[...].astype(F32) + _dot(ctx, w_attn, 1, 0)
    hat, scale = _normalize(attended)
    n2 = hat.astype(BF16)
    n2_all[at] = n2

    @pl.when(step == 0)
    def _():
        for copy in copies[group:]:
            copy.wait()

    w_in = [in_scr[c].reshape(width, width) for c in range(blocks)]
    w_out = out_scr[...].reshape(hidden_size, width)
    gate_up = jnp.concatenate([_dot(n2, w, 1, 0) for w in w_in], axis=1)
    first, second = gate_up[:, :hidden_size], gate_up[:, hidden_size:]
    gelu, slope = _gelu(first)
    hidden = (gelu * second).astype(BF16)
    hidden_all[at] = hidden
    result_ref[0] = (attended + _dot(hidden, w_out, 1, 0)).astype(BF16)
    cot = cot_ref[at]
    hidden_back = _dot(cot, w_out, 1, 1)
    gates = jnp.concatenate([hidden_back * second * slope, hidden_back * gelu], axis=1).astype(BF16)
    gates_all[at] = gates
    back = sum(_dot(gates[:, c * width : (c + 1) * width], w, 1, 1) for c, w in enumerate(w_in))
    back = cot.astype(F32) + _norm_back(back, hat, scale)
    back_ref[...] = back
    branch = back.astype(BF16)
    branch_all[at] = branch
    grads = _dot(branch, w_attn, 1, 1).astype(BF16)
    grad0[...] = grads[:, :span]
    grad1[...] = grads[:, span : 2 * span]
    grad2[0] = grads[:, 2 * span : 3 * span]
    grad2[1] = grads[:, 3 * span :]

    cut = kept[0].shape[1]
    half = cut + kept[1].shape[1]
    core = here[0] & 1

    def place(value, start, size):
        value = value.reshape(owners, size, width).astype(BF16)
        for side in range(2):
            for g, (lower, upper) in enumerate(((0, cut), (cut, half))):
                lower, upper = side * half + lower, side * half + upper
                lo, hi = max(start, lower), min(start + size, upper)
                if lo < hi:
                    part = value[:, lo - start : hi - start]
                    rows_at = slice(lo - lower, hi - lower)

                    @pl.when(core == side)
                    def _(part=part, rows_at=rows_at, g=g):
                        kept[g][:, rows_at] = part

                    @pl.when(core != side)
                    def _(part=part, rows_at=rows_at, g=g):
                        sent[g][:, rows_at] = part

    @pl.when(step == pl.num_programs(0) - 1)
    def _():
        attn = _dot(ctx_all[...], branch_all[...], 0, 0)
        for g in range(group):
            spot = pl.multiple_of((here[0] ^ g) * span, span)
            attn_grad[pl.ds(spot, span)] = attn[g * span : (g + 1) * span]
        place(attn_grad[...], 0, share)
        n2_whole = n2_all[...]
        for c in range(blocks):
            place(_dot(n2_whole, gates_all[:, c * width : (c + 1) * width], 0, 0), share * (1 + c), share)
        place(_dot(hidden_all[...], cot_ref[...], 0, 0), first_out, hidden_share)
        last = first_out + hidden_share
        if last < 2 * half:
            place(jnp.zeros((owners * (2 * half - last), width), F32), last, 2 * half - last)


def feed(here, x, cot, own, near, far, diag, packed, share, hidden_size, half, cut, block=256):
    rows, width = x.shape
    span = own.shape[1]
    group = width // span
    blocks = 2 * hidden_size // width
    owners = packed.shape[0]
    lead = lambda n, lead_width: pl.BlockSpec((n, block, lead_width), lambda i, *_: (0, i, 0))
    half_at = lambda at: pl.BlockSpec((None, block, span), lambda i, *_: (at, i, 0))
    parts = [_shape((owners, cut, width)), _shape((owners, half - cut, width))] * 2
    return pl.pallas_call(
        functools.partial(feed_kernel, share, group),
        grid_spec=pltpu.PrefetchScalarGridSpec(
            num_scalar_prefetch=1,
            grid=(rows // block,),
            in_specs=[_row(block, width), _whole(cot), _row(block, span), _row(block, span), half_at(0), half_at(1), pl.BlockSpec(memory_space=pltpu.HBM)],
            out_specs=[lead(1, width), _row(block, width), _row(block, span), _row(block, span), lead(2, span)] + [_whole(p) for p in parts],
            scratch_shapes=[pltpu.VMEM((rows, n), BF16) for n in (width, width, hidden_size, 2 * hidden_size, width)]
            + [
                pltpu.VMEM((owners, share, width), BF16),
                pltpu.VMEM((blocks, owners, share, width), BF16),
                pltpu.VMEM((owners, hidden_size // owners, width), BF16),
                pltpu.VMEM((width, width), F32),
                pltpu.SemaphoreType.DMA((group + blocks + 1,)),
            ],
        ),
        out_shape=[_shape((1, rows, width)), _shape((rows, width), F32), _shape((rows, span)), _shape((rows, span)), _shape((2, rows, span))] + parts,
        compiler_params=_params(36),
        cost_estimate=_cost(6 * rows * width * (width + 3 * hidden_size), 20 << 20, 2 * rows * hidden_size),
        name="feed",
    )(here, x, cot, own, near, far, diag, packed)


def qkv_grads_kernel(heads, tokens, places, *refs):
    dqs, (dk_ref, dv_ref, table_ref, normed_ref), refs = refs[:4], refs[4:8], refs[8:]
    grads_ref, kept_ref, sent_ref, acc = refs[tokens:]
    step = pl.program_id(0)

    @pl.when(step == 0)
    def _():
        acc[...] = jnp.zeros_like(acc)

    cos, sin = _tables(table_ref, heads)
    dq = dqs[0][...].astype(F32)
    for j in range(1, 4):
        dq = jnp.where(step == j, dqs[j][...].astype(F32), dq)
    qk = jnp.concatenate([dq, dk_ref[...].astype(F32)], axis=1)
    qk = (qk * cos - _half_turn(qk) * sin).astype(BF16)
    grads = jnp.concatenate([qk, dv_ref[...]], axis=1)
    grads_ref[...] = grads
    acc[...] += _dot(normed_ref[...], grads, 0, 0)

    @pl.when(step == pl.num_programs(0) - 1)
    def _():
        pairs, share = kept_ref.shape[:2]
        for i in range(2 * pairs):
            part = acc[i * share : (i + 1) * share].astype(BF16)

            @pl.when((places[1] & 1) == i % 2)
            def _(part=part, i=i):
                kept_ref[i // 2] = part

            @pl.when((places[1] & 1) != i % 2)
            def _(part=part, i=i):
                sent_ref[i // 2] = part


def qkv_grads(places, dqs, dk, dv, table, normed, heads, block, owners, tokens=()):
    length, width = normed.shape
    span = heads * HEAD
    half = _shape((owners // 2, width // owners, 3 * span))
    return pl.pallas_call(
        functools.partial(qkv_grads_kernel, heads, len(tokens)),
        grid_spec=pltpu.PrefetchScalarGridSpec(
            num_scalar_prefetch=1,
            grid=(length // block,),
            in_specs=[_whole(dqs[0])] * 4
            + [_row(block, span)] * 2
            + [_row(block, table.shape[1])]
            + [_row(block, width)]
            + _unread(tokens),
            out_specs=[_row(block, 3 * span), _whole(half), _whole(half)],
            scratch_shapes=[pltpu.VMEM((width, 3 * span), F32)],
        ),
        out_shape=[_shape((length, 3 * span)), half, half],
        compiler_params=_params(12),
        cost_estimate=_cost(2 * length * width * 3 * span, 8 << 20),
        name="qkv_grads",
    )(places, *dqs, dk, dv, table, normed, *tokens)


def input_back_kernel(grads_ref, w_ref, *refs):
    kept_ref, sent_ref = refs[-2:]
    back = _dot(grads_ref[...], w_ref[...], 1, 1).astype(BF16)

    @pl.when(pl.program_id(0) % 2 == 0)
    def _():
        kept_ref[0] = back

    @pl.when(pl.program_id(0) % 2 == 1)
    def _():
        sent_ref[0] = back


def input_back(grads, w, block, tokens=()):
    length, columns = grads.shape
    width = w.shape[0]
    spec = pl.BlockSpec((1, block, width), lambda i: (i // 2, 0, 0))
    return pl.pallas_call(
        input_back_kernel,
        grid=(length // block,),
        in_specs=[_row(block, columns), _whole(w)] + _unread(tokens),
        out_specs=[spec, spec],
        out_shape=[_shape((length // block // 2, block, width))] * 2,
        compiler_params=_params(8),
        cost_estimate=_cost(2 * length * width * columns, 6 << 20),
        name="input_back",
    )(grads, w, *tokens)


def combine_kernel(counts, *refs):
    out, at, first = refs[-1], 0, 0
    for count in counts:
        part = sum(ref[...].astype(F32) for ref in refs[at : at + count]).astype(BF16)
        out[first : first + part.shape[0]] = part
        at, first = at + count, first + part.shape[0]


def combine(groups, tokens=()):
    flat = [pair for group in groups for pair in group]
    rows = sum(group[0][0].shape[-2] for group in groups)
    out = _shape((rows, flat[0][0].shape[-1]))
    return pl.pallas_call(
        functools.partial(combine_kernel, [len(group) for group in groups]),
        grid=(1,),
        in_specs=[_entry(*pair) for pair in flat] + _unread(tokens),
        out_specs=_whole(out),
        out_shape=out,
        compiler_params=_params(8),
        name="combine",
    )(*[array for array, _ in flat], *tokens)


def join_kernel(a_ref, b_ref, out_ref):
    count = a_ref.shape[0]
    out_ref[:count] = a_ref[...]
    out_ref[count:] = b_ref[...]


def join(a, b):
    whole = pl.BlockSpec(memory_space=pltpu.VMEM)
    return pl.pallas_call(
        join_kernel,
        in_specs=[whole, whole],
        out_specs=whole,
        out_shape=_shape((a.shape[0] + b.shape[0],) + a.shape[1:]),
        compiler_params=_params(8),
        name="join",
    )(a, b)


def _pick(here, blocks, group):
    value = blocks[0]
    for j in range(1, len(blocks)):
        value = jnp.where((here ^ group) == j, blocks[j], value)
    return value


def _row_sums(value):
    folded = sum(value[:, at : at + PAD] for at in range(0, value.shape[1], PAD))
    return jnp.sum(folded.T, axis=0, keepdims=True)


def finish_qkv_kernel(here, b0, b1, b2, b3, weight_ref, gain_ref, grad_ref, gain_grad_ref):
    blocks = [b[...].astype(F32) for b in (b0, b1, b2, b3)]
    ordered = [_pick(here[0], blocks, g) for g in range(4)]
    span = b0.shape[1] // 3
    summed = jnp.concatenate([o[:, c * span : (c + 1) * span] for c in range(3) for o in ordered], axis=1)
    gain_grad_ref[...] = _row_sums(weight_ref[...].astype(F32) * summed)
    grad_ref[...] = summed * gain_ref[...].astype(F32)


def finish_feed_kernel(here, b0, b1, b2, b3, weight_ref, gain_ref, attn_ref, in_ref, gain_grad_ref, out_ref):
    share, width = attn_ref.shape
    half = b0.shape[0]
    blocks = [b[...].astype(F32) for b in (b0, b1, b2, b3)]
    ordered = [_pick(here[0], blocks, g) for g in range(4)]
    rows = jnp.concatenate([jnp.concatenate([ordered[core], ordered[2 + core]], axis=1) for core in range(2)], axis=0)
    attn_ref[...] = rows[:share]
    count = in_ref.shape[1] // width
    summed = jnp.concatenate([rows[share * (1 + c) : share * (2 + c)] for c in range(count)], axis=1)
    gain_grad_ref[...] = _row_sums(weight_ref[...].astype(F32) * summed)
    in_ref[...] = summed * gain_ref[...].astype(F32)
    first = share * (1 + count)
    out_ref[...] = rows[first : first + out_ref.shape[0]]


def finish(kernel, name, here, blocks, weight, gain, shapes):
    whole = pl.BlockSpec(memory_space=pltpu.VMEM)
    return pl.pallas_call(
        kernel,
        in_specs=[pl.BlockSpec(memory_space=pltpu.SMEM)] + [whole] * 6,
        out_specs=[whole] * len(shapes),
        out_shape=[_shape(s, F32) for s in shapes],
        compiler_params=_params(8),
        name=name,
    )(here, *blocks, weight, gain)


def input_grad_kernel(x_ref, direct_ref, kept_ref, near_ref, far_ref, out_ref, done_ref):
    done_ref[...] = jnp.zeros_like(done_ref)
    hat, scale = _normalize(x_ref[...].astype(F32))
    back = kept_ref[0].astype(F32) + near_ref[0].astype(F32) + far_ref[...].astype(F32)
    out_ref[0] = (direct_ref[...] + _norm_back(back, hat, scale)).astype(BF16)


def input_grad(x, direct, kept, near, far, block=256):
    rows, width = x.shape
    lead = pl.BlockSpec((1, block, width), lambda i: (0, i, 0))
    return pl.pallas_call(
        input_grad_kernel,
        grid=(rows // block,),
        in_specs=[_row(block, width), _row(block, width), lead, lead, _row(block, width)],
        out_specs=[lead, _whole(_shape((8, PAD)))],
        out_shape=[_shape((1, rows, width)), _shape((8, PAD), F32)],
        compiler_params=_params(8),
        name="input_grad",
    )(x, direct, kept, near, far)


def halve_pair_kernel(columns, axis, bit, places, a_ref, b_ref, *refs):
    kept_ref, sent_ref = refs[-2:]
    own = (places[axis] >> bit) & 1
    if columns:
        half = a_ref.shape[2] // 2
        for side in range(2):
            at = slice(side * half, (side + 1) * half)
            part = (a_ref[:, :, at].astype(F32) + b_ref[:, :, at].astype(F32)).astype(BF16)

            @pl.when(own == side)
            def _(part=part):
                kept_ref[...] = part

            @pl.when(own != side)
            def _(part=part):
                sent_ref[...] = part

    else:
        for i in range(kept_ref.shape[0]):
            for ref, side in ((kept_ref, own), (sent_ref, 1 - own)):
                at = 2 * i + side
                ref[i] = (a_ref[at].astype(F32) + b_ref[at].astype(F32)).astype(BF16)


def halve_pair(places, axis, bit, a, b, columns=False, tokens=()):
    n, rows, width = a.shape
    half = _shape((n, rows, width // 2) if columns else (n // 2, rows, width))
    whole = pl.BlockSpec(memory_space=pltpu.VMEM)
    return pl.pallas_call(
        functools.partial(halve_pair_kernel, columns, axis, bit),
        in_specs=[pl.BlockSpec(memory_space=pltpu.SMEM), whole, whole] + _unread(tokens),
        out_specs=[whole, whole],
        out_shape=[half, half],
        compiler_params=_params(8),
        name="halve_pair",
    )(places, a, b, *tokens)


def relay_kernel(value_ref, *refs):
    refs[-1][...] = value_ref[...]


def relay(value, *tokens, late=()):
    whole = pl.BlockSpec(memory_space=pltpu.VMEM)
    return pl.pallas_call(
        relay_kernel,
        in_specs=[whole] + _unread(tokens) + [pl.BlockSpec(memory_space=pltpu.HBM) for _ in late],
        out_specs=whole,
        out_shape=_shape(value.shape, value.dtype),
        compiler_params=_params(8),
        name="relay",
    )(value, *tokens, *late)


def exchange(value, axis, distance):
    size = lax.axis_size(axis)
    return lax.ppermute(value, axis, [(i, i ^ distance) for i in range(size)])


def gather_halves(piece, axis, token):
    size = lax.axis_size(axis)
    pieces = piece[None]
    distance = size // 2
    while distance > 1:
        pieces = join(pieces, exchange(pieces, axis, distance))
        if distance == size // 2:
            pieces = relay(pieces, token)
        distance //= 2
    other = exchange(pieces, axis, 1)
    return pieces, other


def halve(addends, axis, bit, take):
    own = (lax.axis_index(axis) >> bit) & 1
    sent = sum(take(a, 1 - own).astype(F32) for a in addends).astype(BF16)
    return [take(a, own) for a in addends] + [exchange(sent, axis, 1 << bit)]


def split_owners(addends, axis):
    bits = lax.axis_size(axis).bit_length() - 1
    return [a.reshape((2,) * bits + a.shape[1:]) for a in addends]


def halve_owners(addends, axis, bit):
    dim = lax.axis_size(axis).bit_length() - 2 - bit
    return halve(addends, axis, bit, lambda a, at: lax.dynamic_index_in_dim(a, at, dim, keepdims=False))


def scatter_rows(addends, axis, first=0):
    for bit in range(first, lax.axis_size(axis).bit_length() - 1):
        addends = halve_owners(addends, axis, bit)
    return addends


def total(addends):
    return sum(a.astype(F32) for a in addends)


ROPE_BASE = 160000.0


def rope_tables(places):
    half = HEAD // 2
    inverse = ROPE_BASE ** (-(jnp.arange(half, dtype=F32) * 2.0 / HEAD))
    angles = places[:, None] * inverse[None, :]
    cosine, sine = lax.optimization_barrier((jnp.cos(angles), jnp.sin(angles)))
    return jnp.concatenate([cosine, cosine, sine, sine], axis=1), sine


def from_slices(block):
    far = exchange(block, "seq", 2)
    return [block, exchange(block, "seq", 1), far, exchange(far, "seq", 1)]


def step(places, pair, axis, bit, columns=False, tokens=()):
    kept, sent = halve_pair(places, ("seq", "fsdp").index(axis), bit, *pair, columns, tokens)
    return [kept, exchange(sent, axis, 1 << bit)]


def in_order(blocks, here):
    stacked = jnp.stack(blocks)
    return [lax.dynamic_index_in_dim(stacked, here ^ i, 0, keepdims=False) for i in range(len(blocks))]


def up16(n):
    return -(-n // 16) * 16


def body(
    inputs,
    norm_one,
    qkv_weight,
    attn_out_weight,
    norm_two,
    mlp_in_weight,
    mlp_out_weight,
    cotangent,
):
    here = lax.axis_index("seq")
    slices = lax.axis_size("seq")
    owners = lax.axis_size("fsdp")
    heads = HEADS // slices
    span = heads * HEAD
    rows, width = inputs.shape[1:]
    share = qkv_weight.shape[0]
    hidden_share = mlp_out_weight.shape[0]
    hidden_size = hidden_share * owners
    blocks = 2 * hidden_size // width
    aligned = share % 16 == 0 and hidden_share % 16 == 0
    owner = lax.axis_index("fsdp")
    places = lax.optimization_barrier(jnp.stack([here, owner]).astype(jnp.int32))
    spot = places

    x = inputs[0]
    scaled_qkv = (qkv_weight.astype(F32) * norm_one.astype(F32)[:, None]).astype(BF16)
    scaled_in = (mlp_in_weight.astype(F32) * norm_two.astype(F32)[:, None]).astype(BF16)
    x_far = exchange(x, "seq", 2)
    own_columns = jnp.concatenate(
        [lax.dynamic_slice_in_dim(scaled_qkv, c * width + here * span, span, 1) for c in range(3)], axis=1
    )
    order = here ^ jnp.arange(slices)
    positions = (order[:, None] * rows + jnp.arange(rows)[None, :]).reshape(-1).astype(F32)
    table, sine = rope_tables(positions)
    even, odd = gather_halves(own_columns, "fsdp", sine)
    x_far = relay(x_far, even)
    xs = [x, exchange(x, "seq", 1), x_far, exchange(x_far, "seq", 1)]
    if not aligned:
        bits = owners.bit_length() - 1
        distance = owner ^ jnp.arange(owners)
        spots = sum(((distance >> bit) & 1) << (bits - 1 - bit) for bit in range(bits))
        pieces = jnp.concatenate([even, odd], axis=0)
        even = jnp.take(pieces, spots, axis=0).reshape(1, width, 3 * span)
        odd = even

    shard = [attn_out_weight] + [scaled_in[:, c * width : (c + 1) * width] for c in range(blocks)] + [mlp_out_weight]
    shard_rows = share * (1 + blocks) + hidden_share
    part = -(-shard_rows // (8 * slices)) * 8
    shard = jnp.concatenate(shard + [jnp.zeros((part * slices - shard_rows, width), BF16)], axis=0)
    packed = lax.all_gather(lax.dynamic_slice_in_dim(shard, here * part, part, 0), ("fsdp", "seq"), axis=0, tiled=True)
    packed = packed.reshape(owners, part * slices, width)
    packed_share = share
    if not aligned:
        cuts = [share * c for c in range(2 + blocks)] + [shard_rows]
        packed = jnp.concatenate([packed[:, a:b].reshape(-1, width) for a, b in zip(cuts, cuts[1:])], axis=0)[None]
        packed_share = width

    w_qkv, normed_all, query, key, value = project(places, xs, even, odd, table, heads)
    context_23, query_far = attend_forward(query, key, value, heads, rows, 2, True)
    from_2 = exchange(context_23, "seq", 2)
    context_0, context_1, query_near = attend_forward(query, key, value, heads, rows, 0, False)
    from_1 = exchange(context_1, "seq", 1)
    from_2 = relay(from_2, context_0, late=(packed,))
    from_3 = exchange(from_2, "seq", 1)

    cot = cotangent[0]
    grad_rows = up16(-(-shard_rows // 2))
    cut = up16(grad_rows // 2)
    packed_rows = packed_share * (1 + blocks) + hidden_size // packed.shape[0]
    cuts = (grad_rows, cut) if aligned else (packed_rows // 2, packed_rows // 4)
    result, attended_grad, grad0, grad1, grad23, *mlp_grads = feed(
        spot, x, cot, context_0, from_1, from_2, from_3, packed, packed_share, hidden_size, *cuts
    )
    grad23 = exchange(grad23, "seq", 2)
    grad1 = exchange(grad1, "seq", 1)

    kept_one, kept_two, sent_one, sent_two = mlp_grads
    if not aligned:
        core = here & 1
        kept, sent = jnp.concatenate(mlp_grads[:2], axis=1), jnp.concatenate(mlp_grads[2:], axis=1)
        both = jnp.where(core == 0, jnp.concatenate([kept, sent], axis=1), jnp.concatenate([sent, kept], axis=1))[0]
        edges = [width * c for c in range(2 + blocks)] + [packed_rows]
        both = jnp.concatenate([both[a:b].reshape(owners, -1, width) for a, b in zip(edges, edges[1:])], axis=1)
        both = jnp.pad(both, ((0, 0), (0, 2 * grad_rows - shard_rows), (0, 0)))
        kept = lax.dynamic_slice_in_dim(both, core * grad_rows, grad_rows, 1)
        sent = lax.dynamic_slice_in_dim(both, (1 - core) * grad_rows, grad_rows, 1)
        kept_one, kept_two, sent_one, sent_two = kept[:, :cut], kept[:, cut:], sent[:, :cut], sent[:, cut:]
    one = [kept_one, exchange(sent_one, "seq", 1)]
    two = [kept_two, exchange(sent_two, "seq", 1)]

    dq_0, dq_1, *back = attend_backward(
        key, value, [(query_near, 0, context_0, None, grad0, None), (query_near, 1, context_1, None, grad1, None)], heads
    )
    grad23 = relay(grad23, dq_1)
    grad3 = exchange(grad23, "seq", 1)
    one = step(places, one, "seq", 1, columns=True, tokens=(dq_1,))
    two = step(places, two, "fsdp", 0, tokens=(dq_1,))
    dq_2, dq_3, *back = attend_backward(
        key, value, [(query_far, 0, context_23, 0, grad23, 0), (query_far, 1, context_23, 1, grad3, 1)], heads, back
    )
    one = step(places, one, "fsdp", 0, tokens=(dq_3,))
    two = step(places, two, "fsdp", 1, tokens=(dq_3,))
    tokens = (one[1], two[1])
    qkv_back, qkv_kept, qkv_sent = qkv_grads(
        places, (dq_0, dq_1, dq_2, dq_3), *back, table, normed_all, heads, rows,
        owners if aligned else 2
    )
    one = step(places, one, "fsdp", 1, tokens=(qkv_kept,))
    two = step(places, two, "fsdp", 2, tokens=(qkv_kept,))
    back_kept, back_sent = input_back(qkv_back, w_qkv, rows, tokens=tokens)
    bits = owners.bit_length() - 1
    for bit in range(2, bits):
        one = step(places, one, "fsdp", bit)
    for bit in range(3, bits):
        two = step(places, two, "fsdp", bit)
    two = step(places, two, "seq", 1, columns=True)
    if aligned:
        qkv = [qkv_kept, exchange(qkv_sent, "fsdp", 1)]
        qkv = step(places, qkv, "fsdp", 1, tokens=(back_kept, one[1]))
        for bit in range(2, bits):
            qkv = step(places, qkv, "fsdp", bit)
    else:
        side = owner & 1
        qkv = jnp.where(side == 0, jnp.concatenate([qkv_kept, qkv_sent]), jnp.concatenate([qkv_sent, qkv_kept]))
        qkv = scatter_rows(split_owners([qkv.reshape(owners, share, 3 * span)], "fsdp"), "fsdp")
    mlp_part = combine([[(a, 0) for a in one], [(a, 0) for a in two]], tokens=(qkv[1],))
    back_near = exchange(back_sent, "seq", 1)
    back_far = exchange(combine([[(back_kept, 1), (back_near, 1)]]), "seq", 2)
    input_gradient, input_done = input_grad(x, attended_grad, back_kept, back_near, back_far)
    mlp_blocks = from_slices(mlp_part)
    gain_one, gain_two = norm_one[:, None], norm_two[:, None]
    if aligned:
        attn_gradient, in_gradient, gain_grad2, out_gradient = finish(
            finish_feed_kernel, "finish_feed", spot, mlp_blocks, mlp_in_weight, gain_two,
            ((share, width), (share, 2 * hidden_size), (1, share), (hidden_share, width)),
        )
        qkv_blocks = from_slices(combine([[(a, 0) for a in qkv]], tokens=(input_done,)))
        qkv_gradient, gain_grad1 = finish(
            finish_qkv_kernel, "finish_qkv", spot, qkv_blocks, qkv_weight, gain_one, ((share, 3 * width), (1, share))
        )
    else:
        qkv_blocks = from_slices(total(qkv).astype(BF16))
        ordered = in_order(qkv_blocks, here)
        summed = jnp.concatenate(
            [b[:, c * span : (c + 1) * span] for c in range(3) for b in ordered], axis=1
        ).astype(F32)
        gain_grad1 = jnp.sum(qkv_weight.astype(F32) * summed, axis=1)
        qkv_gradient = summed * gain_one.astype(F32)
        ordered = in_order(mlp_blocks, here)
        summed = jnp.concatenate(
            [jnp.concatenate([ordered[core], ordered[2 + core]], axis=1) for core in range(2)], axis=0
        ).astype(F32)
        attn_gradient = summed[:share]
        first_out = share * (1 + blocks)
        out_gradient = summed[first_out : first_out + hidden_share]
        summed = jnp.concatenate([summed[share * (1 + c) : share * (2 + c)] for c in range(blocks)], axis=1)
        gain_grad2 = jnp.sum(mlp_in_weight.astype(F32) * summed, axis=1)
        in_gradient = summed * gain_two.astype(F32)
    return (
        result,
        input_gradient,
        gain_grad1.reshape(share),
        qkv_gradient,
        attn_gradient,
        gain_grad2.reshape(share),
        in_gradient,
        out_gradient,
    )


def solution(mesh):
    tokens = P("fsdp", "seq", None)
    vector = P("fsdp")
    matrix = P("fsdp", None)
    return jax.shard_map(
        body,
        mesh=mesh,
        in_specs=(tokens, vector, matrix, matrix, vector, matrix, matrix, tokens),
        out_specs=(tokens, tokens, vector, matrix, matrix, vector, matrix, matrix),
        check_vma=False,
    )
```

```python
import functools
import jax, jax.numpy as jnp
from jax import lax
from jax.experimental import pallas as pl
from jax.experimental.pallas import tpu as pltpu

from jax.sharding import PartitionSpec as P

HEADS = 12
HEAD = 64
PAD = 128
EPSILON = 1e-05
MIB = 1 << 20
LOG2E = 1.4426950408889634
F32 = jnp.float32
BF16 = jnp.bfloat16


def _dot(a, b, ca, cb):
    return lax.dot_general(a, b, (((ca,), (cb,)), ((), ())), preferred_element_type=F32)


def _normalize(values):
    centred = values - jnp.mean(values, axis=1, keepdims=True)
    variance = jnp.mean(centred * centred, axis=1, keepdims=True)
    scale_inv = lax.rsqrt(variance + EPSILON)
    return centred * scale_inv, scale_inv


def _norm_back(grad_hat, normed, scale_inv):
    return scale_inv * (
        grad_hat
        - jnp.mean(grad_hat, axis=1, keepdims=True)
        - normed * jnp.mean(grad_hat * normed, axis=1, keepdims=True)
    )


def _tables(table_ref, heads):
    spread = lambda part: jnp.concatenate([part] * (2 * heads), axis=1)
    return spread(table_ref[:, :HEAD]), spread(table_ref[:, HEAD:])


def _half_turn(v):
    lane = lax.broadcasted_iota(jnp.int32, v.shape, 1)
    ahead = -pltpu.roll(v, v.shape[1] - HEAD // 2, 1)
    behind = pltpu.roll(v, HEAD // 2, 1)
    return jnp.where(lane % HEAD < HEAD // 2, ahead, behind)


def _parts(v):
    high = v.astype(BF16)
    rest = v - high.astype(F32)
    mid = rest.astype(BF16)
    low = (rest - mid.astype(F32)).astype(BF16)
    return high, mid, low


def _with_parts(base, v):
    rows = base.shape[0]
    high, mid, low = _parts(v)
    lane = lax.broadcasted_iota(jnp.int32, (rows, PAD - HEAD), 1)
    f = lambda p: p.astype(F32)
    tail = jnp.where(lane == 0, f(high), jnp.where(lane == 1, f(mid), jnp.where(lane == 2, f(low), 0.0)))
    return jnp.concatenate([base[:, :HEAD], tail.astype(BF16)], axis=1)


def _params(mib):
    return pltpu.CompilerParams(vmem_limit_bytes=mib * MIB)


def _row(block, n, first=0):
    return pl.BlockSpec((block, n), lambda i, *_: (i + first, 0))


def _whole(a):
    rank = len(a.shape)
    return pl.BlockSpec(a.shape, lambda i, *_: (0,) * rank)


def _entry(array, at):
    if at is None:
        return _whole(array)
    return pl.BlockSpec((None,) + array.shape[1:], lambda i, *_: (at,) + (0,) * (len(array.shape) - 1))


def _unread(tokens):
    return [pl.BlockSpec(memory_space=pl.ANY) for _ in tokens]


def _shape(shape, dtype=BF16):
    return jax.ShapeDtypeStruct(shape, dtype)


def _cost(flops, size, transcendentals=0):
    return pl.CostEstimate(flops=int(flops), bytes_accessed=int(size), transcendentals=int(transcendentals))


def _reversed_bits(value, size):
    bits = size.bit_length() - 1
    return sum((((value >> bit) & 1) << (bits - 1 - bit) for bit in range(bits)), jnp.int32(0))


def project_kernel(heads, places, x0, x1, x2, x3, even_ref, odd_ref, table_ref, w_ref, normed_ref, q_ref, k_ref, v_ref, x_scr):
    step = pl.program_id(0)
    owners = w_ref.shape[0] // even_ref.shape[1]
    share = even_ref.shape[1]

    @pl.when(step == 0)
    def _():
        for i in range(owners):
            at = slice(i * share, (i + 1) * share)
            spot = _reversed_bits(places[1] ^ i, owners)
            if owners == 1:
                w_ref[at] = even_ref[0]
            else:
                half = owners // 2

                @pl.when(spot < half)
                def _():
                    w_ref[at] = even_ref[spot]

                @pl.when(spot >= half)
                def _():
                    w_ref[at] = odd_ref[spot - half]

    for j, ref in enumerate((x0, x1, x2, x3)):

        @pl.when(step == j)
        def _(ref=ref):
            x_scr[...] = ref[...]

    normed = _normalize(x_scr[...].astype(F32))[0].astype(BF16)
    normed_ref[...] = normed
    qkv = _dot(normed, w_ref[...], 1, 0)
    span = heads * HEAD
    qk = qkv[:, : 2 * span]
    cos, sin = _tables(table_ref, heads)
    qk = qk * cos + _half_turn(qk) * sin
    rows = x0.shape[0]
    zeros = jnp.zeros((rows, PAD - HEAD), BF16)
    ones = jnp.where(lax.broadcasted_iota(jnp.int32, (rows, PAD - HEAD), 1) < 3, 1.0, 0.0).astype(BF16)
    for h in range(heads):
        at = slice(h * PAD, (h + 1) * PAD)
        lo = h * HEAD
        q_ref[:, at] = jnp.concatenate([(qk[:, lo : lo + HEAD] * (LOG2E * HEAD ** -0.5)).astype(BF16), zeros], axis=1)
        k_ref[:, at] = jnp.concatenate([qk[:, span + lo : span + lo + HEAD].astype(BF16), ones], axis=1)
        v_ref[:, at] = jnp.concatenate([qkv[:, 2 * span + lo : 2 * span + lo + HEAD].astype(BF16), ones], axis=1)


def project(places, xs, even, odd, table, heads):
    rows, width = xs[0].shape
    length = rows * len(xs)
    columns = even.shape[2]
    w_shape = _shape((width, columns))
    return pl.pallas_call(
        functools.partial(project_kernel, heads),
        grid_spec=pltpu.PrefetchScalarGridSpec(
            num_scalar_prefetch=1,
            grid=(len(xs),),
            in_specs=[_whole(x) for x in xs] + [_whole(even), _whole(odd), _row(rows, table.shape[1])],
            out_specs=[_whole(w_shape), _row(rows, width)] + [_row(rows, heads * PAD)] * 3,
            scratch_shapes=[pltpu.VMEM((rows, width), BF16)],
        ),
        out_shape=[w_shape, _shape((length, width))] + [_shape((length, heads * PAD))] * 3,
        compiler_params=_params(12),
        cost_estimate=_cost(2 * length * width * columns, 12 << 20),
        name="project",
    )(places, *xs, even, odd, table)


def forward_kernel(heads, sub, q_ref, k_ref, v_ref, *refs):
    ctx_refs, qx_ref = refs[:-1], refs[-1]
    step = pl.program_id(0)
    for r in range(q_ref.shape[0] // sub):
        part = slice(r * sub, (r + 1) * sub)
        outs = []
        for h in range(heads):
            at = slice(h * PAD, (h + 1) * PAD)
            q = q_ref[part, at]
            scores = _dot(q, k_ref[:, at], 1, 1)
            top = jnp.max(scores, axis=1, keepdims=True)
            weights = jnp.exp2(scores - top).astype(BF16)
            sums = _dot(weights, v_ref[:, at], 1, 0)
            total = sums[:, HEAD : HEAD + 1]
            outs.append(sums[:, :HEAD] / total)
            qx_ref[part, at] = _with_parts(q, -(top + jnp.log2(total)))
        out = jnp.concatenate(outs, axis=1).astype(BF16)

        for j, ref in enumerate(ctx_refs):

            @pl.when((step == j) | (len(ctx_refs) == 1))
            def _(part=part, out=out, ref=ref):
                ref[part] = out


def attend_forward(q, k, v, heads, block, first, stacked):
    length = k.shape[0]
    span = heads * HEAD
    ctx = _shape((block, span))
    return pl.pallas_call(
        functools.partial(forward_kernel, heads, min(256, block)),
        grid=(2,),
        in_specs=[_row(block, heads * PAD, first), _whole(k), _whole(v)],
        out_specs=([pl.BlockSpec((None, block, span), lambda i: (i, 0, 0))] if stacked else [_whole(ctx)] * 2)
        + [_row(block, heads * PAD)],
        out_shape=([_shape((2, block, span))] if stacked else [ctx] * 2) + [_shape((2 * block, heads * PAD))],
        compiler_params=_params(10),
        cost_estimate=_cost(16 * heads * 2 * block * length * HEAD, 6 << 20, heads * 2 * block * length),
        name="attend_forward",
    )(q, k, v)


def backward_kernel(heads, sub, count, added, k_ref, v_ref, *refs):
    items = [refs[3 * i : 3 * i + 3] for i in range(count)]
    before = refs[3 * count : 3 * count + 2] if added else (None, None)
    dq_refs, (dk_ref, dv_ref, dk_acc, dv_acc) = refs[-4 - count : -4], refs[-4:]
    fresh = True
    for (q_ref, ctx_ref, do_ref), dq_ref in zip(items, dq_refs):
        do_all = do_ref[...]
        prod = do_all.astype(F32) * ctx_ref[...].astype(F32)
        for r in range(q_ref.shape[0] // sub):
            part = slice(r * sub, (r + 1) * sub)
            dqs = []
            for h in range(heads):
                at = slice(h * PAD, (h + 1) * PAD)
                lo = h * HEAD
                q, k, v = q_ref[part, at], k_ref[:, at], v_ref[:, at]
                delta = jnp.sum(prod[part, lo : lo + HEAD], axis=1, keepdims=True)
                do = _with_parts(do_all[part, lo : lo + HEAD], -delta)
                probs = jnp.exp2(_dot(q, k, 1, 1))
                back = _dot(do, v, 1, 1)
                score_back = (probs * back).astype(BF16)
                dv = _dot(do, probs.astype(BF16), 0, 0)
                dk = _dot(q, score_back, 0, 0)
                dv_acc[at] = dv if fresh else dv_acc[at] + dv
                dk_acc[at] = dk if fresh else dk_acc[at] + dk
                dqs.append(_dot(score_back, k, 1, 0)[:, :HEAD])
            dq_ref[part] = (jnp.concatenate(dqs, axis=1) * HEAD ** -0.5).astype(BF16)
            fresh = False

    def write(ref, acc, scale, before):
        value = jnp.concatenate([(acc[h * PAD : h * PAD + HEAD] * scale).T for h in range(heads)], axis=1)
        ref[...] = (value if before is None else value + before[...].astype(F32)).astype(BF16)

    write(dk_ref, dk_acc, 1 / LOG2E, before[0])
    write(dv_ref, dv_acc, 1.0, before[1])


def attend_backward(k, v, items, heads, before=(), tokens=()):
    length = k.shape[0]
    block, span = items[0][4].shape[-2:]
    whole, rows = _shape((length, span)), _shape((block, span))
    specs, operands = [], []
    for q, first, context, context_at, do, do_at in items:
        specs += [_row(block, heads * PAD, first), _entry(context, context_at), _entry(do, do_at)]
        operands += [q, context, do]
    count = len(items)
    return pl.pallas_call(
        functools.partial(backward_kernel, heads, min(256, block), count, len(before) > 0),
        grid=(1,),
        in_specs=[_whole(k), _whole(v)] + specs + [_whole(a) for a in before] + _unread(tokens),
        out_specs=[_whole(rows)] * count + [_whole(whole)] * 2,
        out_shape=[rows] * count + [whole] * 2,
        scratch_shapes=[pltpu.VMEM((heads * PAD, length), F32)] * 2,
        compiler_params=_params(16),
        cost_estimate=_cost(40 * heads * count * block * length * HEAD, 8 << 20, heads * count * block * length),
        name="attend_backward",
    )(k, v, *operands, *before, *tokens)


def _gelu(first):
    cumulative = 0.5 * (1.0 + lax.erf(first * 0.5 ** 0.5))
    density = jnp.exp(-0.5 * first * first) * 0.3989422804014327
    return first * cumulative, cumulative + first * density


def feed_kernel(share, group, here, x_ref, cot_ref, own_ref, near_ref, far_ref, diag_ref, w_ref, result_ref, back_ref, grad0, grad1, grad2, *refs):
    kept, sent = refs[:2], refs[2:4]
    ctx_all, n2_all, hidden_all, gates_all, branch_all, attn_scr, in_scr, out_scr, attn_grad, sems = refs[4:]
    rows, width = x_ref.shape
    owners, hidden_share = out_scr.shape[:2]
    hidden_size = owners * hidden_share
    span = width // group
    blocks = in_scr.shape[0]
    step = pl.program_id(0)
    at = pl.ds(pl.multiple_of(step * rows, rows), rows)
    copies = []
    for g in range(group):
        if owners % group == 0:
            each = owners // group
            source, target = w_ref.at[pl.ds((here[0] ^ g) * each, each), :share], attn_scr.at[pl.ds(g * each, each)]
        else:
            source = w_ref.at[:, pl.ds(pl.multiple_of((here[0] ^ g) * span, span), span)]
            target = attn_scr.at[:, pl.ds(g * span, span)]
        copies.append(pltpu.make_async_copy(source, target, sems.at[g]))
    for c in range(blocks):
        copies.append(pltpu.make_async_copy(w_ref.at[:, share * (1 + c) : share * (2 + c)], in_scr.at[c], sems.at[group + c]))
    first_out = share * (1 + blocks)
    copies.append(pltpu.make_async_copy(w_ref.at[:, first_out : first_out + hidden_share], out_scr, sems.at[group + blocks]))

    @pl.when(step == 0)
    def _():
        for copy in copies:
            copy.start()
        for copy in copies[:group]:
            copy.wait()

    ctx = jnp.concatenate([own_ref[...], near_ref[...], far_ref[...], diag_ref[...]], axis=1)
    ctx_all[at] = ctx
    w_attn = attn_scr[...].reshape(width, width)
    attended = x_ref[...].astype(F32) + _dot(ctx, w_attn, 1, 0)
    hat, scale = _normalize(attended)
    n2 = hat.astype(BF16)
    n2_all[at] = n2

    @pl.when(step == 0)
    def _():
        for copy in copies[group:]:
            copy.wait()

    w_in = [in_scr[c].reshape(width, width) for c in range(blocks)]
    w_out = out_scr[...].reshape(hidden_size, width)
    gate_up = jnp.concatenate([_dot(n2, w, 1, 0) for w in w_in], axis=1)
    first, second = gate_up[:, :hidden_size], gate_up[:, hidden_size:]
    gelu, slope = _gelu(first)
    hidden = (gelu * second).astype(BF16)
    hidden_all[at] = hidden
    result_ref[0] = (attended + _dot(hidden, w_out, 1, 0)).astype(BF16)
    cot = cot_ref[at]
    hidden_back = _dot(cot, w_out, 1, 1)
    gates = jnp.concatenate([hidden_back * second * slope, hidden_back * gelu], axis=1).astype(BF16)
    gates_all[at] = gates
    back = sum(_dot(gates[:, c * width : (c + 1) * width], w, 1, 1) for c, w in enumerate(w_in))
    back = cot.astype(F32) + _norm_back(back, hat, scale)
    back_ref[...] = back
    branch = back.astype(BF16)
    branch_all[at] = branch
    grads = _dot(branch, w_attn, 1, 1).astype(BF16)
    grad0[...] = grads[:, :span]
    grad1[...] = grads[:, span : 2 * span]
    grad2[0] = grads[:, 2 * span : 3 * span]
    grad2[1] = grads[:, 3 * span :]

    cut = kept[0].shape[1]
    half = cut + kept[1].shape[1]
    core = here[0] & 1

    def place(value, start, size):
        value = value.reshape(owners, size, width).astype(BF16)
        for side in range(2):
            for g, (lower, upper) in enumerate(((0, cut), (cut, half))):
                lower, upper = side * half + lower, side * half + upper
                lo, hi = max(start, lower), min(start + size, upper)
                if lo < hi:
                    part = value[:, lo - start : hi - start]
                    rows_at = slice(lo - lower, hi - lower)

                    @pl.when(core == side)
                    def _(part=part, rows_at=rows_at, g=g):
                        kept[g][:, rows_at] = part

                    @pl.when(core != side)
                    def _(part=part, rows_at=rows_at, g=g):
                        sent[g][:, rows_at] = part

    @pl.when(step == pl.num_programs(0) - 1)
    def _():
        attn = _dot(ctx_all[...], branch_all[...], 0, 0)
        for g in range(group):
            spot = pl.multiple_of((here[0] ^ g) * span, span)
            attn_grad[pl.ds(spot, span)] = attn[g * span : (g + 1) * span]
        place(attn_grad[...], 0, share)
        n2_whole = n2_all[...]
        for c in range(blocks):
            place(_dot(n2_whole, gates_all[:, c * width : (c + 1) * width], 0, 0), share * (1 + c), share)
        place(_dot(hidden_all[...], cot_ref[...], 0, 0), first_out, hidden_share)
        last = first_out + hidden_share
        if last < 2 * half:
            place(jnp.zeros((owners * (2 * half - last), width), F32), last, 2 * half - last)


def feed(here, x, cot, own, near, far, diag, packed, share, hidden_size, half, cut, block=256):
    rows, width = x.shape
    span = own.shape[1]
    group = width // span
    blocks = 2 * hidden_size // width
    owners = packed.shape[0]
    lead = lambda n, lead_width: pl.BlockSpec((n, block, lead_width), lambda i, *_: (0, i, 0))
    half_at = lambda at: pl.BlockSpec((None, block, span), lambda i, *_: (at, i, 0))
    parts = [_shape((owners, cut, width)), _shape((owners, half - cut, width))] * 2
    return pl.pallas_call(
        functools.partial(feed_kernel, share, group),
        grid_spec=pltpu.PrefetchScalarGridSpec(
            num_scalar_prefetch=1,
            grid=(rows // block,),
            in_specs=[_row(block, width), _whole(cot), _row(block, span), _row(block, span), half_at(0), half_at(1), pl.BlockSpec(memory_space=pltpu.HBM)],
            out_specs=[lead(1, width), _row(block, width), _row(block, span), _row(block, span), lead(2, span)] + [_whole(p) for p in parts],
            scratch_shapes=[pltpu.VMEM((rows, n), BF16) for n in (width, width, hidden_size, 2 * hidden_size, width)]
            + [
                pltpu.VMEM((owners, share, width), BF16),
                pltpu.VMEM((blocks, owners, share, width), BF16),
                pltpu.VMEM((owners, hidden_size // owners, width), BF16),
                pltpu.VMEM((width, width), F32),
                pltpu.SemaphoreType.DMA((group + blocks + 1,)),
            ],
        ),
        out_shape=[_shape((1, rows, width)), _shape((rows, width), F32), _shape((rows, span)), _shape((rows, span)), _shape((2, rows, span))] + parts,
        compiler_params=_params(36),
        cost_estimate=_cost(6 * rows * width * (width + 3 * hidden_size), 20 << 20, 2 * rows * hidden_size),
        name="feed",
    )(here, x, cot, own, near, far, diag, packed)


def qkv_grads_kernel(heads, tokens, places, *refs):
    dqs, (dk_ref, dv_ref, table_ref, normed_ref), refs = refs[:4], refs[4:8], refs[8:]
    grads_ref, kept_ref, sent_ref, acc = refs[tokens:]
    step = pl.program_id(0)

    @pl.when(step == 0)
    def _():
        acc[...] = jnp.zeros_like(acc)

    cos, sin = _tables(table_ref, heads)
    dq = dqs[0][...].astype(F32)
    for j in range(1, 4):
        dq = jnp.where(step == j, dqs[j][...].astype(F32), dq)
    qk = jnp.concatenate([dq, dk_ref[...].astype(F32)], axis=1)
    qk = (qk * cos - _half_turn(qk) * sin).astype(BF16)
    grads = jnp.concatenate([qk, dv_ref[...]], axis=1)
    grads_ref[...] = grads
    acc[...] += _dot(normed_ref[...], grads, 0, 0)

    @pl.when(step == pl.num_programs(0) - 1)
    def _():
        pairs, share = kept_ref.shape[:2]
        for i in range(2 * pairs):
            part = acc[i * share : (i + 1) * share].astype(BF16)

            @pl.when((places[1] & 1) == i % 2)
            def _(part=part, i=i):
                kept_ref[i // 2] = part

            @pl.when((places[1] & 1) != i % 2)
            def _(part=part, i=i):
                sent_ref[i // 2] = part


def qkv_grads(places, dqs, dk, dv, table, normed, heads, block, owners, tokens=()):
    length, width = normed.shape
    span = heads * HEAD
    half = _shape((owners // 2, width // owners, 3 * span))
    return pl.pallas_call(
        functools.partial(qkv_grads_kernel, heads, len(tokens)),
        grid_spec=pltpu.PrefetchScalarGridSpec(
            num_scalar_prefetch=1,
            grid=(length // block,),
            in_specs=[_whole(dqs[0])] * 4
            + [_row(block, span)] * 2
            + [_row(block, table.shape[1])]
            + [_row(block, width)]
            + _unread(tokens),
            out_specs=[_row(block, 3 * span), _whole(half), _whole(half)],
            scratch_shapes=[pltpu.VMEM((width, 3 * span), F32)],
        ),
        out_shape=[_shape((length, 3 * span)), half, half],
        compiler_params=_params(12),
        cost_estimate=_cost(2 * length * width * 3 * span, 8 << 20),
        name="qkv_grads",
    )(places, *dqs, dk, dv, table, normed, *tokens)


def input_back_kernel(grads_ref, w_ref, *refs):
    kept_ref, sent_ref = refs[-2:]
    back = _dot(grads_ref[...], w_ref[...], 1, 1).astype(BF16)

    @pl.when(pl.program_id(0) % 2 == 0)
    def _():
        kept_ref[0] = back

    @pl.when(pl.program_id(0) % 2 == 1)
    def _():
        sent_ref[0] = back


def input_back(grads, w, block, tokens=()):
    length, columns = grads.shape
    width = w.shape[0]
    spec = pl.BlockSpec((1, block, width), lambda i: (i // 2, 0, 0))
    return pl.pallas_call(
        input_back_kernel,
        grid=(length // block,),
        in_specs=[_row(block, columns), _whole(w)] + _unread(tokens),
        out_specs=[spec, spec],
        out_shape=[_shape((length // block // 2, block, width))] * 2,
        compiler_params=_params(8),
        cost_estimate=_cost(2 * length * width * columns, 6 << 20),
        name="input_back",
    )(grads, w, *tokens)


def combine_kernel(counts, *refs):
    out, at, first = refs[-1], 0, 0
    for count in counts:
        part = sum(ref[...].astype(F32) for ref in refs[at : at + count]).astype(BF16)
        out[first : first + part.shape[0]] = part
        at, first = at + count, first + part.shape[0]


def combine(groups, tokens=()):
    flat = [pair for group in groups for pair in group]
    rows = sum(group[0][0].shape[-2] for group in groups)
    out = _shape((rows, flat[0][0].shape[-1]))
    return pl.pallas_call(
        functools.partial(combine_kernel, [len(group) for group in groups]),
        grid=(1,),
        in_specs=[_entry(*pair) for pair in flat] + _unread(tokens),
        out_specs=_whole(out),
        out_shape=out,
        compiler_params=_params(8),
        name="combine",
    )(*[array for array, _ in flat], *tokens)


def join_kernel(a_ref, b_ref, out_ref):
    count = a_ref.shape[0]
    out_ref[:count] = a_ref[...]
    out_ref[count:] = b_ref[...]


def join(a, b):
    whole = pl.BlockSpec(memory_space=pltpu.VMEM)
    return pl.pallas_call(
        join_kernel,
        in_specs=[whole, whole],
        out_specs=whole,
        out_shape=_shape((a.shape[0] + b.shape[0],) + a.shape[1:]),
        compiler_params=_params(8),
        name="join",
    )(a, b)


def _pick(here, blocks, group):
    value = blocks[0]
    for j in range(1, len(blocks)):
        value = jnp.where((here ^ group) == j, blocks[j], value)
    return value


def _row_sums(value):
    folded = sum(value[:, at : at + PAD] for at in range(0, value.shape[1], PAD))
    return jnp.sum(folded.T, axis=0, keepdims=True)


def finish_qkv_kernel(here, b0, b1, b2, b3, weight_ref, gain_ref, grad_ref, gain_grad_ref):
    blocks = [b[...].astype(F32) for b in (b0, b1, b2, b3)]
    ordered = [_pick(here[0], blocks, g) for g in range(4)]
    span = b0.shape[1] // 3
    summed = jnp.concatenate([o[:, c * span : (c + 1) * span] for c in range(3) for o in ordered], axis=1)
    gain_grad_ref[...] = _row_sums(weight_ref[...].astype(F32) * summed)
    grad_ref[...] = summed * gain_ref[...].astype(F32)


def finish_feed_kernel(here, b0, b1, b2, b3, weight_ref, gain_ref, attn_ref, in_ref, gain_grad_ref, out_ref):
    share, width = attn_ref.shape
    half = b0.shape[0]
    blocks = [b[...].astype(F32) for b in (b0, b1, b2, b3)]
    ordered = [_pick(here[0], blocks, g) for g in range(4)]
    rows = jnp.concatenate([jnp.concatenate([ordered[core], ordered[2 + core]], axis=1) for core in range(2)], axis=0)
    attn_ref[...] = rows[:share]
    count = in_ref.shape[1] // width
    summed = jnp.concatenate([rows[share * (1 + c) : share * (2 + c)] for c in range(count)], axis=1)
    gain_grad_ref[...] = _row_sums(weight_ref[...].astype(F32) * summed)
    in_ref[...] = summed * gain_ref[...].astype(F32)
    first = share * (1 + count)
    out_ref[...] = rows[first : first + out_ref.shape[0]]


def finish(kernel, name, here, blocks, weight, gain, shapes):
    whole = pl.BlockSpec(memory_space=pltpu.VMEM)
    return pl.pallas_call(
        kernel,
        in_specs=[pl.BlockSpec(memory_space=pltpu.SMEM)] + [whole] * 6,
        out_specs=[whole] * len(shapes),
        out_shape=[_shape(s, F32) for s in shapes],
        compiler_params=_params(8),
        name=name,
    )(here, *blocks, weight, gain)


def input_grad_kernel(x_ref, direct_ref, kept_ref, near_ref, far_ref, out_ref, done_ref):
    done_ref[...] = jnp.zeros_like(done_ref)
    hat, scale = _normalize(x_ref[...].astype(F32))
    back = kept_ref[0].astype(F32) + near_ref[0].astype(F32) + far_ref[...].astype(F32)
    out_ref[0] = (direct_ref[...] + _norm_back(back, hat, scale)).astype(BF16)


def input_grad(x, direct, kept, near, far, block=256):
    rows, width = x.shape
    lead = pl.BlockSpec((1, block, width), lambda i: (0, i, 0))
    return pl.pallas_call(
        input_grad_kernel,
        grid=(rows // block,),
        in_specs=[_row(block, width), _row(block, width), lead, lead, _row(block, width)],
        out_specs=[lead, _whole(_shape((8, PAD)))],
        out_shape=[_shape((1, rows, width)), _shape((8, PAD), F32)],
        compiler_params=_params(8),
        name="input_grad",
    )(x, direct, kept, near, far)


def halve_pair_kernel(columns, axis, bit, places, a_ref, b_ref, *refs):
    kept_ref, sent_ref = refs[-2:]
    own = (places[axis] >> bit) & 1
    if columns:
        half = a_ref.shape[2] // 2
        for side in range(2):
            at = slice(side * half, (side + 1) * half)
            part = (a_ref[:, :, at].astype(F32) + b_ref[:, :, at].astype(F32)).astype(BF16)

            @pl.when(own == side)
            def _(part=part):
                kept_ref[...] = part

            @pl.when(own != side)
            def _(part=part):
                sent_ref[...] = part

    else:
        for i in range(kept_ref.shape[0]):
            for ref, side in ((kept_ref, own), (sent_ref, 1 - own)):
                at = 2 * i + side
                ref[i] = (a_ref[at].astype(F32) + b_ref[at].astype(F32)).astype(BF16)


def halve_pair(places, axis, bit, a, b, columns=False, tokens=()):
    n, rows, width = a.shape
    half = _shape((n, rows, width // 2) if columns else (n // 2, rows, width))
    whole = pl.BlockSpec(memory_space=pltpu.VMEM)
    return pl.pallas_call(
        functools.partial(halve_pair_kernel, columns, axis, bit),
        in_specs=[pl.BlockSpec(memory_space=pltpu.SMEM), whole, whole] + _unread(tokens),
        out_specs=[whole, whole],
        out_shape=[half, half],
        compiler_params=_params(8),
        name="halve_pair",
    )(places, a, b, *tokens)


def relay_kernel(value_ref, *refs):
    refs[-1][...] = value_ref[...]


def relay(value, *tokens, late=()):
    whole = pl.BlockSpec(memory_space=pltpu.VMEM)
    return pl.pallas_call(
        relay_kernel,
        in_specs=[whole] + _unread(tokens) + [pl.BlockSpec(memory_space=pltpu.HBM) for _ in late],
        out_specs=whole,
        out_shape=_shape(value.shape, value.dtype),
        compiler_params=_params(8),
        name="relay",
    )(value, *tokens, *late)


def exchange(value, axis, distance):
    size = lax.axis_size(axis)
    return lax.ppermute(value, axis, [(i, i ^ distance) for i in range(size)])


def gather_halves(piece, axis, token):
    size = lax.axis_size(axis)
    pieces = piece[None]
    distance = size // 2
    while distance > 1:
        pieces = join(pieces, exchange(pieces, axis, distance))
        if distance == size // 2:
            pieces = relay(pieces, token)
        distance //= 2
    other = exchange(pieces, axis, 1)
    return pieces, other


def halve(addends, axis, bit, take):
    own = (lax.axis_index(axis) >> bit) & 1
    sent = sum(take(a, 1 - own).astype(F32) for a in addends).astype(BF16)
    return [take(a, own) for a in addends] + [exchange(sent, axis, 1 << bit)]


def split_owners(addends, axis):
    bits = lax.axis_size(axis).bit_length() - 1
    return [a.reshape((2,) * bits + a.shape[1:]) for a in addends]


def halve_owners(addends, axis, bit):
    dim = lax.axis_size(axis).bit_length() - 2 - bit
    return halve(addends, axis, bit, lambda a, at: lax.dynamic_index_in_dim(a, at, dim, keepdims=False))


def scatter_rows(addends, axis, first=0):
    for bit in range(first, lax.axis_size(axis).bit_length() - 1):
        addends = halve_owners(addends, axis, bit)
    return addends


def total(addends):
    return sum(a.astype(F32) for a in addends)


ROPE_BASE = 160000.0


def rope_tables(places):
    half = HEAD // 2
    inverse = ROPE_BASE ** (-(jnp.arange(half, dtype=F32) * 2.0 / HEAD))
    angles = places[:, None] * inverse[None, :]
    cosine, sine = lax.optimization_barrier((jnp.cos(angles), jnp.sin(angles)))
    return jnp.concatenate([cosine, cosine, sine, sine], axis=1), sine


def from_slices(block):
    far = exchange(block, "seq", 2)
    return [block, exchange(block, "seq", 1), far, exchange(far, "seq", 1)]


def step(places, pair, axis, bit, columns=False, tokens=()):
    kept, sent = halve_pair(places, ("seq", "fsdp").index(axis), bit, *pair, columns, tokens)
    return [kept, exchange(sent, axis, 1 << bit)]


def in_order(blocks, here):
    stacked = jnp.stack(blocks)
    return [lax.dynamic_index_in_dim(stacked, here ^ i, 0, keepdims=False) for i in range(len(blocks))]


def up16(n):
    return -(-n // 16) * 16


def body(
    inputs,
    norm_one,
    qkv_weight,
    attn_out_weight,
    norm_two,
    mlp_in_weight,
    mlp_out_weight,
    cotangent,
):
    here = lax.axis_index("seq")
    slices = lax.axis_size("seq")
    owners = lax.axis_size("fsdp")
    heads = HEADS // slices
    span = heads * HEAD
    rows, width = inputs.shape[1:]
    share = qkv_weight.shape[0]
    hidden_share = mlp_out_weight.shape[0]
    hidden_size = hidden_share * owners
    blocks = 2 * hidden_size // width
    aligned = share % 16 == 0 and hidden_share % 16 == 0
    owner = lax.axis_index("fsdp")
    places = lax.optimization_barrier(jnp.stack([here, owner]).astype(jnp.int32))
    spot = places

    x = inputs[0]
    scaled_qkv = (qkv_weight.astype(F32) * norm_one.astype(F32)[:, None]).astype(BF16)
    scaled_in = (mlp_in_weight.astype(F32) * norm_two.astype(F32)[:, None]).astype(BF16)
    x_far = exchange(x, "seq", 2)
    own_columns = jnp.concatenate(
        [lax.dynamic_slice_in_dim(scaled_qkv, c * width + here * span, span, 1) for c in range(3)], axis=1
    )
    order = here ^ jnp.arange(slices)
    positions = (order[:, None] * rows + jnp.arange(rows)[None, :]).reshape(-1).astype(F32)
    table, sine = rope_tables(positions)
    even, odd = gather_halves(own_columns, "fsdp", sine)
    x_far = relay(x_far, even)
    xs = [x, exchange(x, "seq", 1), x_far, exchange(x_far, "seq", 1)]
    if not aligned:
        bits = owners.bit_length() - 1
        distance = owner ^ jnp.arange(owners)
        spots = sum(((distance >> bit) & 1) << (bits - 1 - bit) for bit in range(bits))
        pieces = jnp.concatenate([even, odd], axis=0)
        even = jnp.take(pieces, spots, axis=0).reshape(1, width, 3 * span)
        odd = even

    shard = [attn_out_weight] + [scaled_in[:, c * width : (c + 1) * width] for c in range(blocks)] + [mlp_out_weight]
    shard_rows = share * (1 + blocks) + hidden_share
    part = -(-shard_rows // (8 * slices)) * 8
    shard = jnp.concatenate(shard + [jnp.zeros((part * slices - shard_rows, width), BF16)], axis=0)
    packed = lax.all_gather(lax.dynamic_slice_in_dim(shard, here * part, part, 0), ("fsdp", "seq"), axis=0, tiled=True)
    packed = packed.reshape(owners, part * slices, width)
    packed_share = share
    if not aligned:
        cuts = [share * c for c in range(2 + blocks)] + [shard_rows]
        packed = jnp.concatenate([packed[:, a:b].reshape(-1, width) for a, b in zip(cuts, cuts[1:])], axis=0)[None]
        packed_share = width

    w_qkv, normed_all, query, key, value = project(places, xs, even, odd, table, heads)
    context_23, query_far = attend_forward(query, key, value, heads, rows, 2, True)
    from_2 = exchange(context_23, "seq", 2)
    context_0, context_1, query_near = attend_forward(query, key, value, heads, rows, 0, False)
    from_1 = exchange(context_1, "seq", 1)
    from_2 = relay(from_2, context_0, late=(packed,))
    from_3 = exchange(from_2, "seq", 1)

    cot = cotangent[0]
    grad_rows = up16(-(-shard_rows // 2))
    cut = up16(grad_rows // 2)
    packed_rows = packed_share * (1 + blocks) + hidden_size // packed.shape[0]
    cuts = (grad_rows, cut) if aligned else (packed_rows // 2, packed_rows // 4)
    result, attended_grad, grad0, grad1, grad23, *mlp_grads = feed(
        spot, x, cot, context_0, from_1, from_2, from_3, packed, packed_share, hidden_size, *cuts
    )
    grad23 = exchange(grad23, "seq", 2)
    grad1 = exchange(grad1, "seq", 1)

    kept_one, kept_two, sent_one, sent_two = mlp_grads
    if not aligned:
        core = here & 1
        kept, sent = jnp.concatenate(mlp_grads[:2], axis=1), jnp.concatenate(mlp_grads[2:], axis=1)
        both = jnp.where(core == 0, jnp.concatenate([kept, sent], axis=1), jnp.concatenate([sent, kept], axis=1))[0]
        edges = [width * c for c in range(2 + blocks)] + [packed_rows]
        both = jnp.concatenate([both[a:b].reshape(owners, -1, width) for a, b in zip(edges, edges[1:])], axis=1)
        both = jnp.pad(both, ((0, 0), (0, 2 * grad_rows - shard_rows), (0, 0)))
        kept = lax.dynamic_slice_in_dim(both, core * grad_rows, grad_rows, 1)
        sent = lax.dynamic_slice_in_dim(both, (1 - core) * grad_rows, grad_rows, 1)
        kept_one, kept_two, sent_one, sent_two = kept[:, :cut], kept[:, cut:], sent[:, :cut], sent[:, cut:]
    one = [kept_one, exchange(sent_one, "seq", 1)]
    two = [kept_two, exchange(sent_two, "seq", 1)]

    dq_0, dq_1, *back = attend_backward(
        key, value, [(query_near, 0, context_0, None, grad0, None), (query_near, 1, context_1, None, grad1, None)], heads
    )
    grad23 = relay(grad23, dq_1)
    grad3 = exchange(grad23, "seq", 1)
    one = step(places, one, "seq", 1, columns=True, tokens=(dq_1,))
    two = step(places, two, "fsdp", 0, tokens=(dq_1,))
    dq_2, dq_3, *back = attend_backward(
        key, value, [(query_far, 0, context_23, 0, grad23, 0), (query_far, 1, context_23, 1, grad3, 1)], heads, back
    )
    one = step(places, one, "fsdp", 0, tokens=(dq_3,))
    two = step(places, two, "fsdp", 1, tokens=(dq_3,))
    tokens = (one[1], two[1])
    qkv_back, qkv_kept, qkv_sent = qkv_grads(
        places, (dq_0, dq_1, dq_2, dq_3), *back, table, normed_all, heads, rows,
        owners if aligned else 2
    )
    one = step(places, one, "fsdp", 1, tokens=(qkv_kept,))
    two = step(places, two, "fsdp", 2, tokens=(qkv_kept,))
    back_kept, back_sent = input_back(qkv_back, w_qkv, rows, tokens=tokens)
    tokens = (back_kept, one[1], two[1])
    bits = owners.bit_length() - 1
    for bit in range(2, bits):
        one = step(places, one, "fsdp", bit)
    for bit in range(3, bits):
        two = step(places, two, "fsdp", bit)
    two = step(places, two, "seq", 1, columns=True)
    if aligned:
        qkv = [qkv_kept, exchange(qkv_sent, "fsdp", 1)]
        qkv = step(places, qkv, "fsdp", 1, tokens=tokens)
        for bit in range(2, bits):
            qkv = step(places, qkv, "fsdp", bit)
    else:
        side = owner & 1
        qkv = jnp.where(side == 0, jnp.concatenate([qkv_kept, qkv_sent]), jnp.concatenate([qkv_sent, qkv_kept]))
        qkv = scatter_rows(split_owners([qkv.reshape(owners, share, 3 * span)], "fsdp"), "fsdp")
    mlp_part = combine([[(a, 0) for a in one], [(a, 0) for a in two]], tokens=(qkv[1],))
    back_near = exchange(back_sent, "seq", 1)
    back_far = exchange(combine([[(back_kept, 1), (back_near, 1)]]), "seq", 2)
    input_gradient, input_done = input_grad(x, attended_grad, back_kept, back_near, back_far)
    mlp_blocks = from_slices(mlp_part)
    gain_one, gain_two = norm_one[:, None], norm_two[:, None]
    if aligned:
        attn_gradient, in_gradient, gain_grad2, out_gradient = finish(
            finish_feed_kernel, "finish_feed", spot, mlp_blocks, mlp_in_weight, gain_two,
            ((share, width), (share, 2 * hidden_size), (1, share), (hidden_share, width)),
        )
        qkv_blocks = from_slices(combine([[(a, 0) for a in qkv]], tokens=(input_done,)))
        qkv_gradient, gain_grad1 = finish(
            finish_qkv_kernel, "finish_qkv", spot, qkv_blocks, qkv_weight, gain_one, ((share, 3 * width), (1, share))
        )
    else:
        qkv_blocks = from_slices(total(qkv).astype(BF16))
        ordered = in_order(qkv_blocks, here)
        summed = jnp.concatenate(
            [b[:, c * span : (c + 1) * span] for c in range(3) for b in ordered], axis=1
        ).astype(F32)
        gain_grad1 = jnp.sum(qkv_weight.astype(F32) * summed, axis=1)
        qkv_gradient = summed * gain_one.astype(F32)
        ordered = in_order(mlp_blocks, here)
        summed = jnp.concatenate(
            [jnp.concatenate([ordered[core], ordered[2 + core]], axis=1) for core in range(2)], axis=0
        ).astype(F32)
        attn_gradient = summed[:share]
        first_out = share * (1 + blocks)
        out_gradient = summed[first_out : first_out + hidden_share]
        summed = jnp.concatenate([summed[share * (1 + c) : share * (2 + c)] for c in range(blocks)], axis=1)
        gain_grad2 = jnp.sum(mlp_in_weight.astype(F32) * summed, axis=1)
        in_gradient = summed * gain_two.astype(F32)
    return (
        result,
        input_gradient,
        gain_grad1.reshape(share),
        qkv_gradient,
        attn_gradient,
        gain_grad2.reshape(share),
        in_gradient,
        out_gradient,
    )


def solution(mesh):
    tokens = P("fsdp", "seq", None)
    vector = P("fsdp")
    matrix = P("fsdp", None)
    return jax.shard_map(
        body,
        mesh=mesh,
        in_specs=(tokens, vector, matrix, matrix, vector, matrix, matrix, tokens),
        out_specs=(tokens, tokens, vector, matrix, matrix, vector, matrix, matrix),
        check_vma=False,
    )
```
